32 devices in a mesh: dp: 8 (over y, x, core), mp: 4 (over z).
Axes of the slice: x: 2, y: 2, z: 4, core: 2. Of those that a mesh axis runs over, the one named last changes fastest.
Arguments:
- layer_in: bfloat16 [16384, 512], P('dp'), may hold values from -9 to 9
- cotangent: bfloat16 [16384, 512], P('dp'), may hold values from -6 to 6
- w_qkv: bfloat16 [3, 512, 512], P(None, None, 'mp'), may hold values from -0.25 to 0.25
- bias_qv: float32 [2, 512], P(None, 'mp'), may hold values from -3 to 3
- w_out: bfloat16 [512, 512], P('mp'), may hold values from -0.75 to 0.75
- bias_out: float32 [512], replicated, may hold values from -3 to 3
- gain_one: float32 [512], replicated, may hold values from 0.5 to 1.5
- shift_one: float32 [512], replicated, may hold values from -2 to 2
- w_up: bfloat16 [512, 2048], P(None, 'mp'), may hold values from -0.25 to 0.25
- bias_up: float32 [2048], P('mp'), may hold values from -3 to 3
- w_down: bfloat16 [2048, 512], P('mp'), may hold values from -0.125 to 0.125
- bias_down: float32 [512], replicated, may hold values from -3 to 3
- gain_two: float32 [512], replicated, may hold values from 0.5 to 1.5
- shift_two: float32 [512], replicated, may hold values from -2 to 2
- segment_ids: int32 [16, 1024], P('dp'), may hold values from 0 to 31, never falling along the last dimension, each value on 1 to 250 neighbouring positions
- key_mask: int32 [16, 1024], P('dp'), may hold values 0 or 1
Outputs:
- omega: float32 [2, 512], replicated
- layer_out: float32 [16384, 512], P(('dp', 'mp'))
- grad_layer_in: float32 [16384, 512], P(('dp', 'mp'))
- grad_w_qkv: float32 [3, 512, 512], P(None, None, 'mp')
- grad_bias_qv: float32 [2, 512], P(None, 'mp')
- grad_w_out: float32 [512, 512], P('mp')
- grad_bias_out: float32 [512], replicated
- grad_gain_one: float32 [512], replicated
- grad_shift_one: float32 [512], replicated
- grad_w_up: float32 [512, 2048], P(None, 'mp')
- grad_bias_up: float32 [2048], P('mp')
- grad_w_down: float32 [2048, 512], P('mp')
- grad_bias_down: float32 [512], replicated
- grad_gain_two: float32 [512], replicated
- grad_shift_two: float32 [512], replicated
The draws below stay inside these ranges and needn't reach their ends.
Inputs may be any that keep to these rules, and one draw needn't show every extreme that they name: `segment_ids`: segment numbers never fall along a packed row; each sentence takes 1 to 250 slots.
All inputs are finite; a program needn't handle non-finite values. No bound on the sum of `key_mask` on one device may be relied on, other than what follows from the above.
Results may differ from the reference program's by a relative error of at most 0.012.
The reference program's roundings to bfloat16 on the way count: a program that leaves them out, or rounds other values in their place, can miss the bound.
Values may be sent and summed in bfloat16 or wider, within the bound.
A program may use at most 128 MiB of HBM per device.

```python
import math
import jax
import jax.numpy as jnp
import numpy as np
from jax import lax

D = 512
HEADS = 8
HD = 64
FF = 2048
ROW = 1024
LONGEST = 250
SEGS = 32
ROWS = 16
TOKENS = 16384


def draw_layer_in(key, part):
    key = jax.random.fold_in(key, 11)
    key_one = jax.random.fold_in(key, 0)
    row_scale = 0.6 + 1.2 * jnp.arange(TOKENS, dtype=jnp.float32)[:, None] / (TOKENS - 1)
    row_noise = jnp.clip(jax.random.normal(key_one, (TOKENS, D), jnp.float32), -5.0, 5.0)
    return (row_noise * row_scale).astype(jnp.bfloat16)


def plant(drawn, rng, low, high):
    shape = drawn.shape
    index_at = [jax.random.randint(jax.random.fold_in(rng, axis), (), 0, shape[axis]) for axis in range(len(shape))]
    drawn = drawn.at[tuple(index_at)].set(low)
    longest = shape.index(max(shape))
    index_at[longest] = (index_at[longest] + 1) % shape[longest]
    return drawn.at[tuple(index_at)].set(high)


def block_scale(rng, dims, cuts, low, high):
    def one(axis_at, parts):
        steps = jax.random.uniform(jax.random.fold_in(jax.random.fold_in(rng, 6), axis_at), (parts,), jnp.float32, low / len(cuts), high / len(cuts))
        return jnp.repeat(jnp.exp(steps), dims[axis_at] // parts).reshape((-1,) + (1,) * (len(dims) - axis_at - 1))

    factor_of = one(*cuts[0])
    for cut in cuts[1:]:
        factor_of = factor_of * one(*cut)
    return factor_of


def split_up(count, total, most, skew):
    weights = [(1 << 20) // math.isqrt(rank ** skew) + 1 for rank in range(2, count + 1)]
    spare, counts = total - most - (count - 1), [1] * (count - 1)
    while spare > 0:
        movable = [i for i in range(count - 1) if counts[i] < most]
        pool, left = sum([weights[i] for i in movable]), spare
        for i in movable:
            extra = min(most - counts[i], max(1, left * weights[i] // pool), spare)
            counts[i] = counts[i] + extra
            spare = spare - extra
    return np.array([most] + counts)


def uneven_parts(key, count, total, limit, skew):
    if count == 2:
        one = jax.random.randint(key, (), max(1, total - limit), min(limit, total - 1) + 1)
        return jnp.stack([one, total - one])
    lengths = jnp.asarray(split_up(count, total, limit, skew), jnp.int32)
    twos = (count - 1) // 2
    donor, taker = lengths[1:1 + 2 * twos:2], lengths[2:2 + 2 * twos:2]
    slack = jnp.minimum(donor - 1, limit - taker)
    moved = jax.random.randint(jax.random.fold_in(key, 1), (twos,), 0, 1 << 20) % (slack + 1)
    lengths = lengths.at[1:1 + 2 * twos:2].set(donor - moved).at[2:2 + 2 * twos:2].set(taker + moved)
    return lengths[jax.random.permutation(jax.random.fold_in(key, 2), count)]


def gaussian(rng, dims, width, most, cuts=(), kind=jnp.bfloat16):
    loudness = block_scale(rng, dims, cuts, -0.22, 0.18) if cuts else 1.0
    entries = jax.random.normal(rng, dims, jnp.float32) * width * loudness
    return jnp.minimum(jnp.maximum(entries, -most), most).astype(kind)


def setup_inputs(seed: int = 0) -> dict:
    seeds = jax.random.split(jax.random.key(seed), 17)
    return {
        "layer_in": draw_layer_in(jax.random.fold_in(seeds[16], 71), 0),
        "cotangent": gaussian(seeds[1], (TOKENS, D), 1.0, 6.0, ((0, 8),)),
        "w_qkv": gaussian(seeds[2], (3, D, D), D ** -0.5, 0.25, ((2, 4),)),
        "bias_qv": gaussian(seeds[3], (2, D), 0.5, 3.0, ((1, 4),), jnp.float32),
        "w_out": gaussian(seeds[4], (D, D), (D // 8) ** -0.5, 0.75, ((0, 4),)),
        "bias_out": gaussian(seeds[5], (D,), 0.5, 3.0, (), jnp.float32),
        "gain_one": jnp.clip(1.0 + 0.1 * jax.random.normal(seeds[6], (D,), jnp.float32), 0.5, 1.5),
        "shift_one": gaussian(seeds[7], (D,), 0.3, 2.0, (), jnp.float32),
        "w_up": gaussian(seeds[8], (D, FF), D ** -0.5, 0.25, ((1, 4),)),
        "bias_up": gaussian(seeds[9], (FF,), 0.5, 3.0, ((0, 4),), jnp.float32),
        "w_down": gaussian(seeds[10], (FF, D), FF ** -0.5, 0.125, ((0, 4),)),
        "bias_down": gaussian(seeds[11], (D,), 0.5, 3.0, (), jnp.float32),
        "gain_two": jnp.clip(1.0 + 0.1 * jax.random.normal(seeds[12], (D,), jnp.float32), 0.5, 1.5),
        "shift_two": gaussian(seeds[13], (D,), 0.3, 2.0, (), jnp.float32),
        "segment_ids": jax.vmap(lambda own: jnp.searchsorted(jnp.cumsum(uneven_parts(own, SEGS, ROW, LONGEST, 2)), jnp.arange(ROW), side="right"))(jax.random.split(seeds[14], ROWS)).reshape((ROWS, ROW)).astype(jnp.int32),
        "key_mask": plant((jax.random.randint(seeds[15], (ROWS, ROW), 0, 8) < 7).astype(jnp.int32), jax.random.fold_in(seeds[15], 1), 0, 1),
    }


norm_eps = 1e-05
masked_fill = -1000000000.0
highest = lax.Precision.HIGHEST

@jax.custom_vjp
def low(v):
    return lax.optimization_barrier(v.astype(jnp.bfloat16)).astype(jnp.float32)

@jax.custom_vjp
def low_back(v):
    return v

def low_keep(v):
    return (low(v), None)

def low_pass(kept, grad):
    return (grad,)

def back_keep(v):
    return (v, None)

def back_low(kept, grad):
    return (low(grad),)
low.defvjp(low_keep, low_pass)
low_back.defvjp(back_keep, back_low)

def both_ways(values):
    return low_back(low(values))

def norm_rows(values, gain, shift):
    row_mean = lax.optimization_barrier(jnp.mean(values, axis=-1, keepdims=True))
    centred = values - row_mean
    row_var = lax.optimization_barrier(jnp.mean(centred * centred, axis=-1, keepdims=True))
    return centred * lax.rsqrt(row_var + norm_eps) * gain + shift

def column_variance(values, valid):
    valid_sum = jnp.sum(valid)
    col_mean = lax.optimization_barrier(jnp.sum(values * valid, axis=0)) / valid_sum
    return lax.optimization_barrier(jnp.sum(values * values * valid, axis=0)) / valid_sum - col_mean * col_mean

def attend_row(packed):
    queries, key_rows, value_rows, segment, present = packed
    places = jnp.arange(segment.shape[0], dtype=jnp.int32)
    allowed = (segment[:, None] == segment[None, :]) & (places[None, :] <= places[:, None]) & (present[None, :] > 0)
    allowed = allowed[None]
    scores = low_back(jnp.einsum('shd,thd->hst', queries, key_rows, precision=highest) * HD ** (-0.5))
    filled = jnp.where(allowed, scores, masked_fill)
    row_top = lax.optimization_barrier(jnp.max(filled, axis=-1, keepdims=True))
    expo = jnp.where(allowed, jnp.exp(filled - row_top), 0.0)
    empty = 1.0 - lax.optimization_barrier(jnp.max(allowed.astype(jnp.float32), axis=-1, keepdims=True))
    total = lax.optimization_barrier(jnp.sum(expo, axis=-1, keepdims=True)) + empty
    probs = low(expo / total)
    return jnp.einsum('hst,thd->shd', probs, value_rows, precision=highest)

def attention_part(inputs, qkv_full, bias_qv, out_full, bias_out, segment_ids, key_mask):
    projected = jnp.einsum('td,cde->cte', inputs, qkv_full, precision=highest)
    queries = both_ways(projected[0] + bias_qv[0])
    key_rows = both_ways(projected[1])
    value_rows = both_ways(projected[2] + bias_qv[1])
    four_d = (segment_ids.shape[0], segment_ids.shape[1], HEADS, HD)
    context = lax.map(jax.checkpoint(attend_row), (queries.reshape(four_d), key_rows.reshape(four_d), value_rows.reshape(four_d), segment_ids, key_mask))
    context = both_ways(context.reshape(inputs.shape))
    return low_back(jnp.dot(context, out_full, preferred_element_type=jnp.float32, precision=highest) + bias_out)

def ffn_part(hidden_one, up_full, bias_up, down_full, bias_down):
    hidden_low = low(hidden_one)
    inner = low_back(jnp.dot(hidden_low, up_full, preferred_element_type=jnp.float32, precision=highest) + bias_up)
    acted = low(jax.nn.gelu(inner))
    return low_back(jnp.dot(acted, down_full, preferred_element_type=jnp.float32, precision=highest) + bias_down)

def reference(layer_in, cotangent, w_qkv, bias_qv, w_out, bias_out, gain_one, shift_one, w_up, bias_up, w_down, bias_down, gain_two, shift_two, segment_ids, key_mask):
    inputs = layer_in.astype(jnp.float32)
    qkv_full = w_qkv.astype(jnp.float32)
    out_full = w_out.astype(jnp.float32)
    up_full = w_up.astype(jnp.float32)
    down_full = w_down.astype(jnp.float32)
    valid = key_mask.reshape(-1, 1).astype(jnp.float32)
    attn = attention_part(inputs, qkv_full, bias_qv, out_full, bias_out, segment_ids, key_mask)
    var_attn = column_variance(attn, valid)
    omega_attn = jnp.sqrt(1.0 + var_attn)
    hidden_one = norm_rows(inputs * omega_attn + attn, gain_one, shift_one)
    ffn = ffn_part(hidden_one, up_full, bias_up, down_full, bias_down)
    var_ffn = column_variance(ffn, valid)
    omega_ffn = jnp.sqrt(1.0 + var_attn + var_ffn)

    def forward(x_in, qkv_in, bqv_in, out_in, bout_in, gone_in, sone_in, up_in, bup_in, down_in, bdown_in, gtwo_in, stwo_in):
        attn_now = attention_part(x_in, qkv_in, bqv_in, out_in, bout_in, segment_ids, key_mask)
        hidden_now = norm_rows(x_in * omega_attn + attn_now, gone_in, sone_in)
        ffn_now = ffn_part(hidden_now, up_in, bup_in, down_in, bdown_in)
        return norm_rows(hidden_now * omega_ffn + ffn_now, gtwo_in, stwo_in)
    layer_out, pullback = jax.vjp(forward, inputs, qkv_full, bias_qv, out_full, bias_out, gain_one, shift_one, up_full, bias_up, down_full, bias_down, gain_two, shift_two)
    grads = pullback(cotangent.astype(jnp.float32))
    return (jnp.stack([omega_attn, omega_ffn]), layer_out, grads[0], grads[1], grads[2], grads[3], grads[4], grads[5], grads[6], grads[7], grads[8], grads[9], grads[10], grads[11], grads[12])
```

```python
import functools
import types

import jax
import jax.numpy as jnp
from jax import lax
from jax.experimental import pallas as pl
from jax.experimental.pallas import tpu as pltpu
from jax.sharding import PartitionSpec as P

HD = 64
LONGEST = 250
TILE = 128
HALO = -(-LONGEST // TILE) * TILE
CHUNK = 64
PACK = 16
CORES = 2

norm_eps = 1e-05
masked_fill = -1000000000.0
shut = -1e30
MESH = pl.DeviceIdType.MESH
f32 = jnp.float32
bf16 = jnp.bfloat16


def dot(a, b):
    return lax.dot_general(a, b, (((1,), (0,)), ((), ())), preferred_element_type=f32)


def dot_nt(a, b):
    return lax.dot_general(a, b, (((1,), (1,)), ((), ())), preferred_element_type=f32)


def layer_kernel(sz, names, *refs):
    r = types.SimpleNamespace(**dict(zip(names, refs)))
    M, NP, R, ROW, HC, F, D = sz.M, sz.NP, sz.R, sz.ROW, sz.HC, sz.F, sz.D
    NDP = NP * CORES
    NH, NQ, KR, WIN = HC // HD, R // TILE, R + HALO, HALO + TILE
    dp, z = lax.axis_index("dp"), lax.axis_index("mp")
    core, plane = lax.rem(dp, CORES), lax.div(dp, CORES)
    piece = core * NP + plane
    partner = (plane * CORES + 1 - core, z)

    def plane_to(off):
        return (lax.rem(plane + off, NP) * CORES + core, z)

    def plane_from(off):
        return lax.rem(plane + NP - off, NP)

    def z_to(dz):
        return (dp, lax.rem(z + dz, M))

    def z_from(dz):
        return lax.rem(z + M - dz, M)

    plane_offs, z_offs = range(1, NP), range(1, M)

    def rcopy(src, dst, send, recv, dev):
        return pltpu.make_async_remote_copy(
            src_ref=src, dst_ref=dst, send_sem=send, recv_sem=recv, device_id=dev, device_id_type=MESH
        )

    def rows(at, count, unit):
        return pl.ds(pl.multiple_of(at * unit, unit), count)

    bar = pltpu.get_barrier_semaphore()
    peers = [partner] + [plane_to(o) for o in plane_offs] + [z_to(d) for d in z_offs]
    for peer in peers:
        pl.semaphore_signal(bar, inc=1, device_id=peer, device_id_type=MESH)

    w_in = dict(qkv=r.w_qkv, out=r.w_out, up=r.w_up, down=r.w_down)
    w_all = dict(qkv=r.WQ, out=r.WO, up=r.WU, down=r.WD)
    group = ("qkv", "out", "up", "down")
    load = [
        pltpu.make_async_copy(r.layer_in.at[rows(z, R, R)], r.XB.at[pl.ds(HALO, R)], r.ls.at[0]),
        pltpu.make_async_copy(
            r.layer_in.at[rows(lax.rem(z * (R // TILE) + (M * R - HALO) // TILE, M * R // TILE), HALO, TILE)],
            r.XB.at[pl.ds(0, HALO)],
            r.ls.at[1],
        ),
        pltpu.make_async_copy(r.cotangent.at[rows(z, R, R)], r.CT, r.ls.at[2]),
    ]
    load_w = {
        g: pltpu.make_async_copy(w_in[g], w_all[g].at[z], r.ls.at[3 + n]) for n, g in enumerate(group)
    }
    load[0].start()
    load[1].start()
    for g in group:
        load_w[g].start()
    load[2].start()
    r.SB[...] = jnp.zeros((8, sz.W), f32)
    r.SB[0:1, 0:F] = r.bias_up[...]
    r.SB[1:3, 0:HC] = r.bias_qv[...]
    r.RBI[z] = r.SB[...]

    pl.semaphore_wait(bar, len(peers))

    def g_split(g):
        return w_in[g].shape[0] % (NDP * PACK) == 0

    def gz(g, dz, zs):
        n = group.index(g)
        if not g_split(g):
            src, dst = w_in[g], w_all[g].at[zs]
        else:
            pr = w_in[g].shape[0] // NDP
            src, dst = w_in[g].at[rows(piece, pr, pr)], w_all[g].at[zs, rows(piece, pr, pr)]
        return rcopy(src, dst, r.gzs.at[n, dz - 1], r.gzr.at[n, dz - 1], z_to(dz))

    def gp(g, off, dz, at_plane):
        n, pr = group.index(g), w_in[g].shape[0] // NDP
        part = w_all[g].at[z_from(dz), rows(core * NP + at_plane, pr, pr)]
        return rcopy(part, part, r.gps.at[n, off - 1, dz - 1], r.gpr.at[n, off - 1, dz - 1], plane_to(off))

    def gc(g, dz, at_core):
        n, half = group.index(g), w_in[g].shape[0] // CORES
        part = w_all[g].at[z_from(dz), rows(at_core, half, half)]
        return rcopy(part, part, r.gcs.at[n, dz - 1], r.gcr.at[n, dz - 1], partner)

    def gz_start(g):
        for dz in z_offs:
            gz(g, dz, z).start()

    def gp_start(g):
        for dz in z_offs:
            gz(g, dz, z_from(dz)).wait_recv()
            if g_split(g):
                for off in plane_offs:
                    gp(g, off, dz, plane).start()

    def gc_start(g):
        if g_split(g):
            for dz in z_offs:
                for off in plane_offs:
                    gp(g, off, dz, plane_from(off)).wait_recv()
                gc(g, dz, core).start()

    def gc_wait(g):
        if g_split(g):
            for dz in z_offs:
                gc(g, dz, 1 - core).wait_recv()
        load_w[g].wait()

    def g_sent(g):
        for dz in z_offs:
            gz(g, dz, z).wait_send()
            if g_split(g):
                for off in plane_offs:
                    gp(g, off, dz, plane).wait_send()
                gc(g, dz, core).wait_send()

    def bias_copy(dz, zs):
        return rcopy(r.SB, r.RBI.at[zs], r.bzs.at[dz - 1], r.bzr.at[dz - 1], z_to(dz))

    g_part = dict(qkv=r.GQ, out=r.GO, up=r.GU, down=r.GD)
    g_ra = dict(qkv=r.RAQ, out=r.RAO, up=r.RAU, down=r.RAD)
    g_rb = dict(qkv=r.RBQ, out=r.RBO, up=r.RBU, down=r.RBD)
    g_qb = dict(qkv=r.QBQ, out=r.QBO, up=r.QBU, down=r.QBD)
    g_rc = dict(qkv=r.RCQ, out=r.RCO, up=r.RCU, down=r.RCD)
    g_out = dict(qkv=r.OQ, out=r.OO, up=r.OU, down=r.OD)
    g_res = dict(qkv=r.grad_w_qkv, out=r.grad_w_out, up=r.grad_w_up, down=r.grad_w_down)

    def pr_of(g):
        return g_part[g].shape[1] // NDP

    def rc(g, j):
        n, half = group.index(g), pr_of(g) * NP
        return rcopy(
            g_part[g].at[j, rows(1 - core, half, half)], g_ra[g].at[j], r.rcs.at[n, j], r.rcr.at[n, j], partner
        )

    def rp(g, off, j):
        n, pr = group.index(g), pr_of(g)
        at = core * NP + lax.rem(plane + off, NP)
        return rcopy(
            g_part[g].at[j, rows(at, pr, pr)],
            g_rb[g].at[off - 1, j],
            r.rps.at[n, off - 1, j],
            r.rpr.at[n, off - 1, j],
            plane_to(off),
        )

    def rz(g, dz):
        n = group.index(g)
        return rcopy(
            g_qb[g].at[lax.rem(z + dz, M)],
            g_rc[g].at[dz - 1],
            r.rzs.at[n, dz - 1],
            r.rzr.at[n, dz - 1],
            z_to(dz),
        )

    def ap(g, off, at_plane):
        n, pr = group.index(g), pr_of(g)
        part = g_out[g].at[rows(core * NP + at_plane, pr, pr)]
        return rcopy(part, part, r.aps.at[n, off - 1], r.apr.at[n, off - 1], plane_to(off))

    def ac(g, at_core):
        n, half = group.index(g), pr_of(g) * NP
        part = g_out[g].at[rows(at_core, half, half)]
        return rcopy(part, part, r.acs.at[n], r.acr.at[n], partner)

    def rc_start(g, j):
        rc(g, j).start()

    def rp_start(g, j):
        rc(g, j).wait_recv()
        half = pr_of(g) * NP
        mine = rows(core, half, half)
        g_part[g][j, mine] = (g_part[g][j, mine].astype(f32) + g_ra[g][j].astype(f32)).astype(bf16)
        for off in plane_offs:
            rp(g, off, j).start()

    def rz_start(g):
        pr = pr_of(g)

        def one(j, c):
            total = g_part[g][j, rows(piece, pr, pr)].astype(f32)
            for off in plane_offs:
                rp(g, off, j).wait_recv()
                total = total + g_rb[g][off - 1, j].astype(f32)
            g_qb[g][j] = total.astype(bf16)
            return c

        lax.fori_loop(0, M, one, 0)
        for dz in z_offs:
            rz(g, dz).start()

    def ap_start(g):
        pr = pr_of(g)
        total = g_qb[g][z].astype(f32)
        for dz in z_offs:
            rz(g, dz).wait_recv()
            total = total + g_rc[g][dz - 1].astype(f32)
        g_out[g][rows(piece, pr, pr)] = total.astype(bf16)
        for off in plane_offs:
            ap(g, off, plane).start()

    def ac_start(g):
        for off in plane_offs:
            ap(g, off, plane_from(off)).wait_recv()
        ac(g, core).start()

    def result(g):
        n = group.index(g)
        got = g_out[g].at[pl.ds(0, g_res[g].shape[0])]
        return pltpu.make_async_copy(got, g_res[g], r.ls.at[7 + n])

    def ac_wait(g):
        ac(g, 1 - core).wait_recv()
        result(g).start()

    def r_sent(g):
        def one(j, c):
            rc(g, j).wait_send()
            for off in plane_offs:
                rp(g, off, j).wait_send()
            return c

        lax.fori_loop(0, M, one, 0)
        for dz in z_offs:
            rz(g, dz).wait_send()
        for off in plane_offs:
            ap(g, off, plane).wait_send()
        ac(g, core).wait_send()
        result(g).wait()

    sums = [(r.S0, r.S0c, r.S0p, r.S0z), (r.S1, r.S1c, r.S1p, r.S1z), (r.V, r.Vc, r.Vp, r.Vz)]

    def sc(k):
        return rcopy(sums[k][0], sums[k][1], r.scs.at[k], r.scr.at[k], partner)

    def sp(k, off, at):
        part = sums[k][2].at[at]
        return rcopy(part, part, r.sps.at[k, off - 1], r.spr.at[k, off - 1], plane_to(off))

    def sz_(k, dz, at):
        part = sums[k][3].at[at]
        return rcopy(part, part, r.szs.at[k, dz - 1], r.szr.at[k, dz - 1], z_to(dz))

    def sum_core(k):
        sc(k).start()

    def sum_plane(k):
        sc(k).wait_recv()
        sums[k][2][plane] = sums[k][0][...] + sums[k][1][...]
        for off in plane_offs:
            sp(k, off, plane).start()

    def sum_z(k):
        for off in plane_offs:
            sp(k, off, plane_from(off)).wait_recv()
        total = sums[k][2][0]
        for s in plane_offs:
            total = total + sums[k][2][s]
        sums[k][3][z] = total
        for dz in z_offs:
            sz_(k, dz, z).start()

    def sum_done(k):
        for dz in z_offs:
            sz_(k, dz, z_from(dz)).wait_recv()
        total = sums[k][3][0]
        for s in z_offs:
            total = total + sums[k][3][s]
        return total

    def sum_sent(k):
        sc(k).wait_send()
        for off in plane_offs:
            sp(k, off, plane).wait_send()
        for dz in z_offs:
            sz_(k, dz, z).wait_send()

    def halo(j):
        return rcopy(r.HS.at[j], r.HR.at[j], r.hss.at[j], r.hsr.at[j], z_to(M - 1))

    def chunks(body, init=0):
        return lax.fori_loop(0, R // CHUNK, lambda c, s: body(rows(c, CHUNK, CHUNK), s), init)

    def wide(cols):
        return jnp.concatenate([cols] * (D // TILE), axis=1)

    gz_start("qkv")
    for dz in z_offs:
        bias_copy(dz, z).start()

    unit = M * R // TILE
    marks = []
    for b in range(KR // TILE):
        at = lax.rem(z * NQ + (b - HALO // TILE) + unit, unit)
        packed, col = lax.div(at, ROW // TILE), lax.rem(at, ROW // TILE)
        spot = rows(col, TILE, TILE)
        sent, present = r.segment_ids[0:1, spot], r.key_mask[0:1, spot]
        for p in range(1, r.segment_ids.shape[0]):
            sent = jnp.where(packed == p, r.segment_ids[p : p + 1, spot] + p * ROW, sent)
            present = jnp.where(packed == p, r.key_mask[p : p + 1, spot], present)
        sent, present = sent.astype(f32), present.astype(f32)
        keyed = jnp.where(present > 0.5, sent, -1.0)
        if b < HALO // TILE:
            keyed = jnp.where(z > 0, keyed, -1.0)
        else:
            own = b - HALO // TILE
            r.VAL[own * TILE : (own + 1) * TILE, :] = jnp.broadcast_to(present, (TILE, TILE)).T
        marks.append((sent, jnp.broadcast_to(keyed, (TILE, TILE)).T))
    key_pos = lax.broadcasted_iota(jnp.int32, (TILE, TILE), 0)
    query_pos = lax.broadcasted_iota(jnp.int32, (TILE, TILE), 1)
    for i in range(NQ):
        asker = marks[i + HALO // TILE][0]
        for b in range(WIN // TILE):
            allowed = marks[i + b][1] == asker
            if b == WIN // TILE - 1:
                allowed = allowed & (key_pos <= query_pos)
            r.MB[i, b * TILE : (b + 1) * TILE, :] = jnp.where(allowed, 0.0, shut)

    head_of = lax.broadcasted_iota(jnp.int32, (1, HC), 1) // HD
    in_head = [(head_of == h).astype(f32) for h in range(NH)]
    scale = HD ** (-0.5)

    def diagonal(both):
        return jnp.concatenate(
            [both[h * HD : (h + 1) * HD, h * TILE : (h + 1) * TILE] for h in range(NH)], axis=0
        )

    def split_heads(dst, j, whole, factor):
        for h in range(NH):
            one = (whole * (in_head[h] * factor)).astype(bf16)
            for i in range(NQ):
                dst[j, i, h * TILE : (h + 1) * TILE, :] = one[i * TILE : (i + 1) * TILE, :]

    def project(j):
        bias = r.RBI[j]
        query = dot(r.XB[HALO:KR, :], r.WQ[j, 0:D, :]) + bias[1:2, 0:HC]
        split_heads(r.QM, j, query, scale)
        key = dot(r.XB[...], r.WQ[j, D : 2 * D, :])
        r.KN[j] = key.astype(bf16)
        r.KT[j] = (key * scale).astype(bf16).T
        value = (dot(r.XB[...], r.WQ[j, 2 * D : 3 * D, :]) + bias[2:3, 0:HC]).astype(bf16)
        r.VN[j] = value
        r.VT[j] = value.T

    def attend(j):
        for i in range(NQ):
            lo, hi = i * TILE, i * TILE + WIN
            scores = dot_nt(r.KN[j, lo:hi, :], r.QM[j, i])
            scores = scores + jnp.concatenate([r.MB[i]] * NH, axis=1)
            top = jnp.maximum(jnp.max(scores, axis=0, keepdims=True), masked_fill)
            expo = jnp.exp(scores - top)
            total = jnp.maximum(jnp.sum(expo, axis=0, keepdims=True), 1.0)
            probs = expo * (1.0 / total)
            r.PS[j, i] = probs
            context = diagonal(dot(r.VT[j, :, lo:hi], probs.astype(bf16))).astype(bf16)
            r.CXT[j, :, i * TILE : (i + 1) * TILE] = context
            r.CX[j, i * TILE : (i + 1) * TILE, :] = context.T

    load[0].wait()
    load[1].wait()
    load_w["qkv"].wait()
    project(z)
    gp_start("qkv")
    for g in ("out", "up", "down"):
        gz_start(g)
    attend(z)
    r.XT[...] = r.XB[HALO:KR, :].T
    gc_start("qkv")
    for dz in z_offs:
        bias_copy(dz, z_from(dz)).wait_recv()
    for dz in z_offs:
        gc("qkv", dz, 1 - core).wait_recv()

    def forward_step(t, c):
        j = lax.rem(z + t, M)
        project(j)
        attend(j)

        @pl.when(t == 1)
        def _():
            gp_start("out")
            gp_start("up")

        @pl.when(t == 2)
        def _():
            gc_start("out")
            gp_start("down")

        return c

    lax.fori_loop(1, M, forward_step, 0)
    gc_wait("out")

    attn = r.bias_out[...]
    for j in range(M):
        attn = attn + dot(r.CX[j], r.WO[j])
    r.ACC[...] = attn

    def moments(slot):
        def body(at, s):
            v, valid = r.ACC[at, :], wide(r.VAL[at, :])
            vv = v * valid
            return (
                s[0] + jnp.sum(vv, axis=0, keepdims=True),
                s[1] + jnp.sum(vv * v, axis=0, keepdims=True),
                s[2] + jnp.sum(valid, axis=0, keepdims=True),
            )

        zero = jnp.zeros((1, D), f32)
        s = chunks(body, (zero, zero, zero))
        slot[...] = jnp.concatenate([s[0], s[1], s[2], jnp.zeros((5, D), f32)], axis=0)

    def variance(total, count):
        col_mean = total[0:1] / count
        return total[1:2] / count - col_mean * col_mean

    moments(r.S0)
    sum_core(0)
    gc_start("up")
    sum_plane(0)
    gc_start("down")
    sum_z(0)
    total = sum_done(0)
    count = total[2:3]
    var_attn = variance(total, count)
    omega_attn = jnp.sqrt(1.0 + var_attn)
    gain_one, shift_one = r.gain_one[...], r.shift_one[...]
    gain_two, shift_two = r.gain_two[...], r.shift_two[...]

    def normed(pre):
        centred = pre - jnp.mean(pre, axis=-1, keepdims=True)
        var = jnp.mean(centred * centred, axis=-1, keepdims=True)
        rstd = lax.rsqrt(var + norm_eps)
        return centred * rstd, rstd

    def norm_back(dy, n, rstd, gain):
        dn = dy * gain
        return rstd * (
            dn - jnp.mean(dn, axis=-1, keepdims=True) - n * jnp.mean(dn * n, axis=-1, keepdims=True)
        )

    def norm_one(c, s):
        at, xat = rows(c, CHUNK, CHUNK), rows(c + HALO // CHUNK, CHUNK, CHUNK)
        n, rstd = normed(r.XB[xat, :].astype(f32) * omega_attn + r.ACC[at, :])
        r.N1[at, :] = n
        r.RS[at, :] = jnp.broadcast_to(rstd, (CHUNK, TILE))
        r.HL[at, :] = (n * gain_one + shift_one).astype(bf16)
        return s

    lax.fori_loop(0, R // CHUNK, norm_one, 0)
    gc_wait("up")
    gc_wait("down")

    r.ACC[...] = jnp.broadcast_to(r.bias_down[...], (R, D))
    c0 = (2.0 / jnp.pi) ** 0.5

    def ffn_step(t, c):
        j = lax.rem(z + t, M)
        r.INN[...] = dot(r.HL[...], r.WU[j]) + r.RBI[j, 0:1, 0:F]

        def body(at, s):
            u = r.INN[at, :]
            uu = u * u
            th = jnp.tanh(u * (c0 + (c0 * 0.044715) * uu))
            half = 0.5 + 0.5 * th
            r.AC[j, at, :] = (u * half).astype(bf16)
            r.GP[j, at, :] = half + (0.5 * u) * (1.0 - th * th) * (c0 + (3.0 * 0.044715 * c0) * uu)
            return s

        chunks(body)
        r.ACC[...] += dot(r.AC[j], r.WD[j])
        return c

    lax.fori_loop(0, M, ffn_step, 0)

    moments(r.S1)
    sum_core(1)
    r.HLT[...] = r.HL[...].T
    sum_plane(1)
    sum_z(1)
    total = sum_done(1)
    omega_ffn = jnp.sqrt(1.0 + var_attn + variance(total, count))
    r.omega[...] = jnp.concatenate([omega_attn, omega_ffn, jnp.zeros((6, D), f32)], axis=0)
    load[2].wait()

    def norm_two(at, s):
        hidden = r.N1[at, :] * gain_one + shift_one
        n, rstd = normed(hidden * omega_ffn + r.ACC[at, :])
        r.LO[at, :] = n * gain_two + shift_two
        dy = r.CT[at, :].astype(f32)
        d_pre = norm_back(dy, n, rstd, gain_two)
        low = d_pre.astype(bf16)
        r.DP[at, :] = d_pre
        r.DF[at, :] = low
        return (
            s[0] + jnp.sum(low.astype(f32), axis=0, keepdims=True),
            s[1] + jnp.sum(dy * n, axis=0, keepdims=True),
            s[2] + jnp.sum(dy, axis=0, keepdims=True),
        )

    zero = jnp.zeros((1, D), f32)
    s = chunks(norm_two, (zero, zero, zero))
    r.V[...] = jnp.zeros(r.V.shape, f32)
    r.VB[...] = jnp.zeros(r.VB.shape, f32)
    for n in range(3):
        r.V[3 + n : 4 + n, :] = s[n]
    put_out = pltpu.make_async_copy(r.LO, r.layer_out, r.ls.at[11])
    put_out.start()

    r.ACC[...] = jnp.zeros((R, D), f32)

    def ffn_back(t, c):
        j = lax.rem(z + t, M)
        r.GD[j, 0:F, :] = dot(r.AC[j].T, r.DF[...]).astype(bf16)
        rc_start("down", j)
        r.INN[...] = dot_nt(r.DF[...], r.WD[j])

        def body(at, s):
            low = (r.INN[at, :] * r.GP[j, at, :]).astype(bf16)
            r.DI[at, :] = low
            return s + jnp.sum(low.astype(f32), axis=0, keepdims=True)

        r.VB[j, 0:1, 0:F] = chunks(body, jnp.zeros((1, F), f32))
        r.GU[j, 0:D, :] = dot(r.HLT[...], r.DI[...]).astype(bf16)
        rc_start("up", j)
        r.ACC[...] += dot_nt(r.DI[...], r.WU[j])

        @pl.when(t > 0)
        def _():
            before = lax.rem(z + t + (M - 1), M)
            rp_start("down", before)
            rp_start("up", before)

        return c

    lax.fori_loop(0, M, ffn_back, 0)

    def back_one(at, s):
        dy = r.ACC[at, :] + omega_ffn * r.DP[at, :]
        n = r.N1[at, :]
        d_pre = norm_back(dy, n, r.RS[at, 0:1], gain_one)
        low = d_pre.astype(bf16)
        r.DA[at, :] = low
        r.GI[at, :] = omega_attn * d_pre
        return (
            s[0] + jnp.sum(low.astype(f32), axis=0, keepdims=True),
            s[1] + jnp.sum(dy * n, axis=0, keepdims=True),
            s[2] + jnp.sum(dy, axis=0, keepdims=True),
        )

    s = chunks(back_one, (zero, zero, zero))
    for n in range(3):
        r.V[n : n + 1, :] = s[n]
    last = lax.rem(z + M - 1, M)
    rp_start("down", last)
    rp_start("up", last)

    def out_back(j, c):
        r.GO[j, 0:HC, :] = dot(r.CXT[j], r.DA[...]).astype(bf16)
        rc_start("out", j)
        split_heads(r.DCM, j, dot_nt(r.DA[...], r.WO[j]), 1.0)
        return c

    lax.fori_loop(0, M, out_back, 0)

    def attend_back(j, slot):
        r.DK[slot] = jnp.zeros((KR, HC), f32)
        r.DV[slot] = jnp.zeros((KR, HC), f32)
        for i in range(NQ):
            lo, hi = i * TILE, i * TILE + WIN
            probs = r.PS[j, i]
            d_context = r.DCM[j, i]
            d_probs = dot_nt(r.VN[j, lo:hi, :], d_context)
            delta = jnp.sum(probs * d_probs, axis=0, keepdims=True)
            d_scores = (probs * (d_probs - delta)).astype(bf16)
            r.DV[slot, lo:hi, :] += dot(probs.astype(bf16), d_context)
            r.DK[slot, lo:hi, :] += dot(d_scores, r.QM[j, i])
            d_query = diagonal(dot(r.KT[j, :, lo:hi], d_scores)).astype(bf16)
            r.DQ[slot, i * TILE : (i + 1) * TILE, :] = d_query.T
        r.HS[j, 0:HALO, :] = r.DK[slot, 0:HALO, :].astype(bf16)
        r.HS[j, HALO : 2 * HALO, :] = r.DV[slot, 0:HALO, :].astype(bf16)
        halo(j).start()

    def qkv_back(j, slot):
        halo(j).wait_recv()
        r.DK[slot, R:KR, :] += r.HR[j, 0:HALO, :].astype(f32)
        r.DV[slot, R:KR, :] += r.HR[j, HALO : 2 * HALO, :].astype(f32)
        d_query = r.DQ[slot]
        d_key = r.DK[slot, HALO:KR, :].astype(bf16)
        d_value = r.DV[slot, HALO:KR, :].astype(bf16)
        r.VB[j, 1:2, 0:HC] = jnp.sum(d_query.astype(f32), axis=0, keepdims=True)
        r.VB[j, 2:3, 0:HC] = jnp.sum(d_value.astype(f32), axis=0, keepdims=True)
        for n, part in enumerate((d_query, d_key, d_value)):
            r.GQ[j, n * D : (n + 1) * D, :] = dot(r.XT[...], part).astype(bf16)
        rc_start("qkv", j)
        r.GI[...] += (
            dot_nt(d_query, r.WQ[j, 0:D, :])
            + dot_nt(d_key, r.WQ[j, D : 2 * D, :])
            + dot_nt(d_value, r.WQ[j, 2 * D : 3 * D, :])
        )

    def attn_step(t, c):
        attend_back(t, lax.rem(t, 2))

        @pl.when(t > 0)
        def _():
            qkv_back(t - 1, lax.rem(t + 1, 2))

        @pl.when(t > 1)
        def _():
            rp_start("qkv", t - 2)

        @pl.when(t == 0)
        def _():
            lax.fori_loop(0, M, lambda k, cc: (rp_start("out", k), cc)[1], 0)

        @pl.when(t == 1)
        def _():
            rz_start("down")
            rz_start("up")
            rz_start("out")

        @pl.when(t == 2)
        def _():
            ap_start("down")
            ap_start("up")
            ap_start("out")

        @pl.when(t == M - 1)
        def _():
            ac_start("down")
            ac_start("up")
            ac_start("out")

        return c

    lax.fori_loop(0, M, attn_step, 0)
    qkv_back(M - 1, (M - 1) % 2)
    for j in range(M):
        r.V[6 + 3 * j : 9 + 3 * j, :] = r.VB[j, 0:3, :]
    sum_core(2)
    if M > 1:
        rp_start("qkv", M - 2)
    rp_start("qkv", M - 1)
    sum_plane(2)
    put_in = pltpu.make_async_copy(r.GI, r.grad_layer_in, r.ls.at[12])
    put_in.start()
    for g in ("down", "up", "out"):
        ac_wait(g)
    rz_start("qkv")
    sum_z(2)
    ap_start("qkv")
    total = sum_done(2)
    for j in range(M):
        r.VB[j, 0:3, :] = total[6 + 3 * j : 9 + 3 * j]
    r.vectors[0:6, :] = total[0:6]
    r.vectors[6:9, :] = r.VB[z, 0:3, :]
    r.vectors[9:16, :] = jnp.zeros((7, D), f32)
    ac_start("qkv")
    ac_wait("qkv")

    for g in group:
        g_sent(g)
        r_sent(g)
    for dz in z_offs:
        bias_copy(dz, z).wait_send()
    for k in range(3):
        sum_sent(k)
    lax.fori_loop(0, M, lambda j, c: (halo(j).wait_send(), c)[1], 0)
    put_out.wait()
    put_in.wait()


def shards(
    layer_in,
    cotangent,
    w_qkv,
    bias_qv,
    w_out,
    bias_out,
    gain_one,
    shift_one,
    w_up,
    bias_up,
    w_down,
    bias_down,
    gain_two,
    shift_two,
    segment_ids,
    key_mask,
):
    M, NDP = lax.axis_size("mp"), lax.axis_size("dp")
    D = layer_in.shape[1]
    HC, F, ROW = w_qkv.shape[2], w_up.shape[1], segment_ids.shape[1]
    R = layer_in.shape[0] // M
    NP, NH, NQ, KR, WIN = NDP // CORES, HC // HD, R // TILE, R + HALO, HALO + TILE
    sz = types.SimpleNamespace(M=M, NP=NP, R=R, ROW=ROW, HC=HC, F=F, D=D, W=max(F, HC))

    hbm, vmem = pl.BlockSpec(memory_space=pl.ANY), pl.BlockSpec(memory_space=pltpu.VMEM)
    ins = dict(
        layer_in=(layer_in, hbm),
        cotangent=(cotangent, hbm),
        w_qkv=(w_qkv.reshape(3 * D, HC), hbm),
        w_out=(w_out, hbm),
        w_up=(w_up, hbm),
        w_down=(w_down, hbm),
        bias_qv=(bias_qv, vmem),
        bias_up=(bias_up[None], vmem),
        bias_out=(bias_out[None], vmem),
        gain_one=(gain_one[None], vmem),
        shift_one=(shift_one[None], vmem),
        bias_down=(bias_down[None], vmem),
        gain_two=(gain_two[None], vmem),
        shift_two=(shift_two[None], vmem),
        segment_ids=(segment_ids, vmem),
        key_mask=(key_mask, vmem),
    )
    outs = dict(
        omega=((8, D), f32, vmem),
        layer_out=((R, D), f32, hbm),
        grad_layer_in=((R, D), f32, hbm),
        grad_w_qkv=((3 * D, HC), bf16, hbm),
        grad_w_out=((HC, D), bf16, hbm),
        grad_w_up=((D, F), bf16, hbm),
        grad_w_down=((F, D), bf16, hbm),
        vectors=((16, D), f32, vmem),
    )
    scratch = dict(
        XB=((KR, D), bf16),
        XT=((D, R), bf16),
        CT=((R, D), bf16),
        WQ=((M, 3 * D, HC), bf16),
        WO=((M, HC, D), bf16),
        WU=((M, D, F), bf16),
        WD=((M, F, D), bf16),
        SB=((8, sz.W), f32),
        RBI=((M, 8, sz.W), f32),
        QM=((M, NQ, NH * TILE, HC), bf16),
        KN=((M, KR, HC), bf16),
        KT=((M, HC, KR), bf16),
        VN=((M, KR, HC), bf16),
        VT=((M, HC, KR), bf16),
        PS=((M, NQ, WIN, NH * TILE), f32),
        CX=((M, R, HC), bf16),
        CXT=((M, HC, R), bf16),
        DCM=((M, NQ, NH * TILE, HC), bf16),
        MB=((NQ, WIN, TILE), f32),
        VAL=((R, TILE), f32),
        ACC=((R, D), f32),
        N1=((R, D), f32),
        RS=((R, TILE), f32),
        HL=((R, D), bf16),
        HLT=((D, R), bf16),
        INN=((R, F), f32),
        AC=((M, R, F), bf16),
        GP=((M, R, F), f32),
        LO=((R, D), f32),
        DP=((R, D), f32),
        DF=((R, D), bf16),
        DI=((R, F), bf16),
        DA=((R, D), bf16),
        GI=((R, D), f32),
        DK=((2, KR, HC), f32),
        DV=((2, KR, HC), f32),
        DQ=((2, R, HC), bf16),
        HS=((M, 2 * HALO, HC), bf16),
        HR=((M, 2 * HALO, HC), bf16),
        VB=((M, 8, D), f32),
    )
    for tag, shape in (("Q", (3 * D, HC)), ("O", (HC, D)), ("U", (D, F)), ("D", (F, D))):
        pr = -(-shape[0] // (NDP * PACK)) * PACK
        scratch["G" + tag] = ((M, pr * NDP, shape[1]), bf16)
        scratch["RA" + tag] = ((M, pr * NP, shape[1]), bf16)
        scratch["RB" + tag] = ((NP - 1, M, pr, shape[1]), bf16)
        scratch["QB" + tag] = ((M, pr, shape[1]), bf16)
        scratch["RC" + tag] = ((M - 1, pr, shape[1]), bf16)
        scratch["O" + tag] = ((pr * NDP, shape[1]), bf16)
    vec_rows = -(-(6 + 3 * M) // 8) * 8
    for tag, count in (("S0", 8), ("S1", 8), ("V", vec_rows)):
        scratch[tag] = ((count, D), f32)
        scratch[tag + "c"] = ((count, D), f32)
        scratch[tag + "p"] = ((NP, count, D), f32)
        scratch[tag + "z"] = ((M, count, D), f32)
    sems = dict(
        ls=(13,),
        gzs=(4, M - 1),
        gzr=(4, M - 1),
        gps=(4, NP - 1, M - 1),
        gpr=(4, NP - 1, M - 1),
        gcs=(4, M - 1),
        gcr=(4, M - 1),
        bzs=(M - 1,),
        bzr=(M - 1,),
        rcs=(4, M),
        rcr=(4, M),
        rps=(4, NP - 1, M),
        rpr=(4, NP - 1, M),
        rzs=(4, M - 1),
        rzr=(4, M - 1),
        aps=(4, NP - 1),
        apr=(4, NP - 1),
        acs=(4,),
        acr=(4,),
        scs=(3,),
        scr=(3,),
        sps=(3, NP - 1),
        spr=(3, NP - 1),
        szs=(3, M - 1),
        szr=(3, M - 1),
        hss=(M,),
        hsr=(M,),
    )
    names = list(ins) + list(outs) + list(scratch) + list(sems)
    got = pl.pallas_call(
        functools.partial(layer_kernel, sz, names),
        out_shape=[jax.ShapeDtypeStruct(s, t) for s, t, _ in outs.values()],
        in_specs=[spec for _, spec in ins.values()],
        out_specs=[spec for _, _, spec in outs.values()],
        scratch_shapes=[pltpu.VMEM(s, t) for s, t in scratch.values()]
        + [pltpu.SemaphoreType.DMA(s) for s in sems.values()],
        compiler_params=pltpu.CompilerParams(
            collective_id=0, has_side_effects=True, vmem_limit_bytes=62 << 20
        ),
    )(*[value for value, _ in ins.values()])
    o = dict(zip(outs, got))
    vec = o["vectors"]
    return (
        o["omega"][0:2],
        o["layer_out"],
        o["grad_layer_in"],
        o["grad_w_qkv"].reshape(3, D, HC).astype(f32),
        vec[7:9, 0:HC],
        o["grad_w_out"].astype(f32),
        vec[0],
        vec[1],
        vec[2],
        o["grad_w_up"].astype(f32),
        vec[6, 0:F],
        o["grad_w_down"].astype(f32),
        vec[3],
        vec[4],
        vec[5],
    )


def solution(mesh):
    in_specs = (
        P("dp", None),
        P("dp", None),
        P(None, None, "mp"),
        P(None, "mp"),
        P("mp", None),
        P(),
        P(),
        P(),
        P(None, "mp"),
        P("mp"),
        P("mp", None),
        P(),
        P(),
        P(),
        P("dp", None),
        P("dp", None),
    )
    out_specs = (
        P(),
        P(("dp", "mp"), None),
        P(("dp", "mp"), None),
        P(None, None, "mp"),
        P(None, "mp"),
        P("mp", None),
        P(),
        P(),
        P(),
        P(None, "mp"),
        P("mp"),
        P("mp", None),
        P(),
        P(),
        P(),
    )
    return jax.shard_map(shards, mesh=mesh, in_specs=in_specs, out_specs=out_specs, check_vma=False)
```

```python
import functools
import types

import jax
import jax.numpy as jnp
from jax import lax
from jax.experimental import pallas as pl
from jax.experimental.pallas import tpu as pltpu
from jax.sharding import PartitionSpec as P

HD = 64
LONGEST = 250
TILE = 128
HALO = -(-LONGEST // TILE) * TILE
CHUNK = 64
PACK = 16
CORES = 2

norm_eps = 1e-05
masked_fill = -1000000000.0
shut = -1e30
MESH = pl.DeviceIdType.MESH
f32 = jnp.float32
bf16 = jnp.bfloat16


def dot(a, b):
    return lax.dot_general(a, b, (((1,), (0,)), ((), ())), preferred_element_type=f32)


def dot_nt(a, b):
    return lax.dot_general(a, b, (((1,), (1,)), ((), ())), preferred_element_type=f32)


def layer_kernel(sz, names, *refs):
    r = types.SimpleNamespace(**dict(zip(names, refs)))
    M, NP, R, ROW, HC, F, D = sz.M, sz.NP, sz.R, sz.ROW, sz.HC, sz.F, sz.D
    NDP = NP * CORES
    NH, NQ, KR, WIN = HC // HD, R // TILE, R + HALO, HALO + TILE
    dp, z = lax.axis_index("dp"), lax.axis_index("mp")
    core, plane = lax.rem(dp, CORES), lax.div(dp, CORES)
    piece = core * NP + plane
    partner = (plane * CORES + 1 - core, z)

    def plane_to(off):
        return (lax.rem(plane + off, NP) * CORES + core, z)

    def plane_from(off):
        return lax.rem(plane + NP - off, NP)

    def flipped(at, mask, count):
        for b in range(count.bit_length() - 1):
            if mask >> b & 1:
                at = at + (1 - 2 * lax.rem(lax.div(at, 1 << b), 2)) * (1 << b)
        return at

    def z_from(dz):
        if isinstance(dz, int):
            return flipped(z, dz, M)
        return sum(
            (lax.rem(lax.div(z, 1 << b) + lax.div(dz, 1 << b), 2)) * (1 << b) for b in range(M.bit_length() - 1)
        )

    def z_apart(j):
        return z_from(j)

    def z_to(dz):
        return (dp, z_from(dz))

    def chip_to(n):
        return (lax.rem(plane + n // M, NP) * CORES + core, lax.rem(z + n % M, M))

    plane_offs, z_offs = range(1, NP), range(1, M)
    bits = NP.bit_length() - 1

    def flip(mask):
        return flipped(plane, mask, NP)

    def flip_to(mask):
        return (flip(mask) * CORES + core, z)

    orders = (tuple(range(bits)), tuple(reversed(range(bits))))

    def subsets(some):
        masks = [0]
        for b in some:
            masks = masks + [m | 1 << b for m in masks]
        return masks

    def rcopy(src, dst, send, recv, dev):
        return pltpu.make_async_remote_copy(
            src_ref=src, dst_ref=dst, send_sem=send, recv_sem=recv, device_id=dev, device_id_type=MESH
        )

    def rows(at, count, unit):
        return pl.ds(pl.multiple_of(at * unit, unit), count)

    bar = pltpu.get_barrier_semaphore()
    peers = [partner] + [chip_to(n) for n in range(1, NP * M)]
    for peer in peers:
        pl.semaphore_signal(bar, inc=1, device_id=peer, device_id_type=MESH)

    w_in = dict(qkv=r.w_qkv, out=r.w_out, up=r.w_up, down=r.w_down)
    w_all = dict(qkv=r.WQ, out=r.WO, up=r.WU, down=r.WD)
    group = ("qkv", "out", "up", "down")
    load = [
        pltpu.make_async_copy(r.layer_in.at[rows(z, R, R)], r.XB.at[pl.ds(HALO, R)], r.ls.at[0]),
        pltpu.make_async_copy(
            r.layer_in.at[rows(lax.rem(z * (R // TILE) + (M * R - HALO) // TILE, M * R // TILE), HALO, TILE)],
            r.XB.at[pl.ds(0, HALO)],
            r.ls.at[1],
        ),
        pltpu.make_async_copy(r.cotangent.at[rows(z, R, R)], r.CT, r.ls.at[2]),
    ]
    load_w = {
        g: pltpu.make_async_copy(w_in[g], w_all[g].at[z], r.ls.at[3 + n]) for n, g in enumerate(group)
    }
    load[0].start()
    load[1].start()
    for g in group:
        load_w[g].start()
    load[2].start()
    r.SB[...] = jnp.zeros((8, sz.W), f32)
    r.SB[0:1, 0:F] = r.bias_up[...]
    r.SB[1:3, 0:HC] = r.bias_qv[...]
    r.RBI[z] = r.SB[...]

    pl.semaphore_wait(bar, len(peers))

    def g_split(g):
        return w_in[g].shape[0] % (NDP * PACK) == 0

    def gz(g, dz, zs):
        n = group.index(g)
        if not g_split(g):
            src, dst = w_in[g], w_all[g].at[zs]
        else:
            pr = w_in[g].shape[0] // NDP
            src, dst = w_in[g].at[rows(piece, pr, pr)], w_all[g].at[zs, rows(piece, pr, pr)]
        return rcopy(src, dst, r.gzs.at[n, dz - 1], r.gzr.at[n, dz - 1], z_to(dz))

    def g_halves(g):
        return 2 if w_in[g].shape[0] // NDP % (2 * PACK) == 0 else 1

    def gp(g, h, s, m, dz, there):
        n, hp = group.index(g), w_in[g].shape[0] // NDP // g_halves(g)
        order = orders[h]
        have = subsets(order[:s])[m] ^ (there << order[s])
        part = w_all[g].at[z_from(dz), rows((core * NP + flip(have)) * g_halves(g) + h, hp, hp)]
        at = (n, h, (1 << s) - 1 + m, dz - 1)
        return rcopy(part, part, r.gps.at[at], r.gpr.at[at], flip_to(1 << order[s]))

    def gc(g, dz, at_core):
        n, half = group.index(g), w_in[g].shape[0] // CORES
        part = w_all[g].at[z_from(dz), rows(at_core, half, half)]
        return rcopy(part, part, r.gcs.at[n, dz - 1], r.gcr.at[n, dz - 1], partner)

    def gz_start(g):
        for dz in z_offs:
            gz(g, dz, z).start()

    def gp_all(g, s):
        return [(h, m) for h in range(g_halves(g)) for m in range(1 << s)]

    def gp_start(g, s, dzs):
        for dz in dzs:
            if s == 0:
                gz(g, dz, z_from(dz)).wait_recv()
            if not g_split(g):
                continue
            if s > 0:
                for h, m in gp_all(g, s - 1):
                    gp(g, h, s - 1, m, dz, 1).wait_recv()
            if s < bits:
                for h, m in gp_all(g, s):
                    gp(g, h, s, m, dz, 0).start()
            else:
                gc(g, dz, core).start()

    near = [tuple(z_offs[0:1]), tuple(z_offs[1:2]), tuple(z_offs[2:])]

    def gather(phase, which, *groups):
        for dz in near[which - 1]:
            for s in ((0,), range(1, bits), (bits,))[phase]:
                for g in groups:
                    gp_start(g, s, (dz,))

    def gc_wait(g, dz):
        if g_split(g):
            gc(g, dz, 1 - core).wait_recv()

    def g_sent(g):
        for dz in z_offs:
            gz(g, dz, z).wait_send()
            if g_split(g):
                for s in range(bits):
                    for h, m in gp_all(g, s):
                        gp(g, h, s, m, dz, 0).wait_send()
                gc(g, dz, core).wait_send()

    def bias_copy(dz, zs):
        return rcopy(r.SB, r.RBI.at[zs], r.bzs.at[dz - 1], r.bzr.at[dz - 1], z_to(dz))

    g_part = dict(qkv=r.GQ, out=r.GO, up=r.GU, down=r.GD)
    g_ra = dict(qkv=r.RAQ, out=r.RAO, up=r.RAU, down=r.RAD)
    g_rb = dict(qkv=r.RBQ, out=r.RBO, up=r.RBU, down=r.RBD)
    g_qb = dict(qkv=r.QBQ, out=r.QBO, up=r.QBU, down=r.QBD)
    g_rc = dict(qkv=r.RCQ, out=r.RCO, up=r.RCU, down=r.RCD)
    g_out = dict(qkv=r.OQ, out=r.OO, up=r.OU, down=r.OD)
    g_res = dict(qkv=r.grad_w_qkv, out=r.grad_w_out, up=r.grad_w_up, down=r.grad_w_down)

    def pr_of(g):
        return g_part[g].shape[1] // NDP

    def rc(g, j):
        n, half = group.index(g), pr_of(g) * NP
        return rcopy(
            g_part[g].at[j, rows(1 - core, half, half)], g_ra[g].at[j], r.rcs.at[n, j], r.rcr.at[n, j], partner
        )

    def r_halves(g):
        return 2 if pr_of(g) % (2 * PACK) == 0 else 1

    def rp(g, off, j):
        n, pr = group.index(g), pr_of(g)
        at = core * NP + lax.rem(plane + off, NP)
        return rcopy(
            g_part[g].at[j, rows(at, pr, pr)],
            g_rb[g].at[off - 1, j],
            r.rps.at[n, 0, off - 1, j],
            r.rpr.at[n, 0, off - 1, j],
            plane_to(off),
        )

    def r_rows(g, h, mask):
        hp = pr_of(g) // r_halves(g)
        return rows((core * NP + flip(mask)) * r_halves(g) + h, hp, hp)

    def r_slot(g, h, s, m):
        hp = pr_of(g) // r_halves(g)
        return NP - (1 << (bits - s)) + m, pl.ds(h * hp, hp)

    def rh(g, h, s, m, j):
        n, order = group.index(g), orders[h]
        slot, half = r_slot(g, h, s, m)
        away = subsets(order[s + 1 :])[m] | 1 << order[s]
        return rcopy(
            g_part[g].at[j, r_rows(g, h, away)],
            g_rb[g].at[slot, j, half],
            r.rps.at[n, h, slot, j],
            r.rpr.at[n, h, slot, j],
            flip_to(1 << order[s]),
        )

    def rh_all(g, s):
        return [(h, m) for h in range(r_halves(g)) for m in range(1 << (bits - 1 - s))]

    def rz(g, j, dz):
        n = group.index(g)
        return rcopy(g_qb[g].at[j], g_rc[g].at[dz - 1], r.rzs.at[n, dz - 1], r.rzr.at[n, dz - 1], (dp, j))

    def ap(g, off, at_plane):
        n, pr = group.index(g), pr_of(g)
        part = g_out[g].at[rows(core * NP + at_plane, pr, pr)]
        return rcopy(part, part, r.aps.at[n, off - 1], r.apr.at[n, off - 1], plane_to(off))

    def ac(g, at_core):
        n, half = group.index(g), pr_of(g) * NP
        part = g_out[g].at[rows(at_core, half, half)]
        return rcopy(part, part, r.acs.at[n], r.acr.at[n], partner)

    def rc_start(g, j):
        rc(g, j).start()

    def rp_start(g, j, direct=False):
        rc(g, j).wait_recv()
        half = pr_of(g) * NP
        mine = rows(core, half, half)
        g_part[g][j, mine] = (g_part[g][j, mine].astype(f32) + g_ra[g][j].astype(f32)).astype(bf16)
        if direct:
            for off in plane_offs:
                rp(g, off, j).start()
        else:
            for h, m in rh_all(g, 0):
                rh(g, h, 0, m, j).start()

    def rp_step(g, j, s):
        for h, m in rh_all(g, s - 1):
            rh(g, h, s - 1, m, j).wait_recv()
            slot, half = r_slot(g, h, s - 1, m)
            at = r_rows(g, h, subsets(orders[h][s:])[m])
            g_part[g][j, at] = (g_part[g][j, at].astype(f32) + g_rb[g][slot, j, half].astype(f32)).astype(bf16)
        for h, m in rh_all(g, s):
            rh(g, h, s, m, j).start()

    def mids(g, j):
        for s in range(1, bits):
            rp_step(g, j, s)

    def rz_start(g, j, direct=False):
        pr = pr_of(g)
        total = g_part[g][j, rows(piece, pr, pr)].astype(f32)
        if direct:
            for off in plane_offs:
                rp(g, off, j).wait_recv()
                total = total + g_rb[g][off - 1, j].astype(f32)
        else:
            for h, m in rh_all(g, bits - 1):
                rh(g, h, bits - 1, m, j).wait_recv()
            total = total + g_rb[g][NP - 2, j].astype(f32)
        g_qb[g][j] = total.astype(bf16)

        @pl.when(j != z)
        def _():
            rz(g, j, z_apart(j)).start()

    def ap_start(g):
        pr = pr_of(g)
        total = g_qb[g][z].astype(f32)
        for dz in z_offs:
            rz(g, z, dz).wait_recv()
            total = total + g_rc[g][dz - 1].astype(f32)
        g_out[g][rows(piece, pr, pr)] = total.astype(bf16)
        for off in plane_offs:
            ap(g, off, plane).start()

    def ac_start(g):
        for off in plane_offs:
            ap(g, off, plane_from(off)).wait_recv()
        ac(g, core).start()

    def result(g):
        n = group.index(g)
        got = g_out[g].at[pl.ds(0, g_res[g].shape[0])]
        return pltpu.make_async_copy(got, g_res[g], r.ls.at[7 + n])

    def ac_wait(g):
        ac(g, 1 - core).wait_recv()
        result(g).start()

    def r_sent(g):
        def one(j, c):
            rc(g, j).wait_send()
            for s in range(bits):
                for h, m in rh_all(g, s):
                    rh(g, h, s, m, j).wait_send()
            return c

        def direct(j, c):
            rc(g, j).wait_send()
            for off in plane_offs:
                rp(g, off, j).wait_send()
            return c

        if g == "qkv":
            lax.fori_loop(0, M - 1, lambda t, c: one(step_of(t), c), 0)
            direct(step_of(M - 1), 0)
        else:
            lax.fori_loop(0, M, one, 0)
        for dz in z_offs:
            rz(g, z_from(dz), dz).wait_send()
        for off in plane_offs:
            ap(g, off, plane).wait_send()
        ac(g, core).wait_send()
        result(g).wait()

    def sc(k):
        return rcopy(r.S.at[k], r.Sc.at[k], r.scs.at[k], r.scr.at[k], partner)

    def sa(k, n, there):
        if there:
            at = lax.rem(plane + NP - n // M, NP) * M + lax.rem(z + M - n % M, M)
        else:
            at = plane * M + z
        return rcopy(r.Sa.at[k, at], r.Sa.at[k, at], r.sas.at[k, n - 1], r.sar.at[k, n - 1], chip_to(n))

    def sum_core(k):
        sc(k).start()

    def sum_chips(k):
        sc(k).wait_recv()
        r.Sa[k, plane * M + z] = r.S[k] + r.Sc[k]
        for n in range(1, NP * M):
            sa(k, n, False).start()

    def sum_done(k):
        for n in range(1, NP * M):
            sa(k, n, True).wait_recv()
        total = r.Sa[k, 0]
        for n in range(1, NP * M):
            total = total + r.Sa[k, n]
        return total

    def sum_sent(k):
        sc(k).wait_send()
        for n in range(1, NP * M):
            sa(k, n, False).wait_send()

    def vc():
        return rcopy(r.V, r.Vc, r.vs.at[0], r.vr.at[0], partner)

    def vp(off, at):
        return rcopy(r.Vp.at[at], r.Vp.at[at], r.vs.at[off], r.vr.at[off], plane_to(off))

    def vz(dz, at):
        return rcopy(r.Vz.at[at], r.Vz.at[at], r.vs.at[NP - 1 + dz], r.vr.at[NP - 1 + dz], z_to(dz))

    def vec_plane():
        vc().wait_recv()
        r.Vp[plane] = r.V[...] + r.Vc[...]
        for off in plane_offs:
            vp(off, plane).start()

    def vec_z():
        for off in plane_offs:
            vp(off, plane_from(off)).wait_recv()
        total = r.Vp[0]
        for s in plane_offs:
            total = total + r.Vp[s]
        r.Vz[z] = total
        for dz in z_offs:
            vz(dz, z).start()

    def vec_done():
        for dz in z_offs:
            vz(dz, z_from(dz)).wait_recv()
        total = r.Vz[0]
        for s in z_offs:
            total = total + r.Vz[s]
        return total

    def vec_sent():
        vc().wait_send()
        for off in plane_offs:
            vp(off, plane).wait_send()
        for dz in z_offs:
            vz(dz, z).wait_send()

    def halo(j):
        return rcopy(r.HS.at[j], r.HR.at[j], r.hss.at[j], r.hsr.at[j], (dp, lax.rem(z + M - 1, M)))

    sharing = max(ROW // R, 1)
    first_shard = lax.rem((lax.div(z, sharing) + 1) * sharing, M)

    def step_of(t):
        return lax.rem(first_shard + t, M)

    joined = lax.rem(z * R, ROW) > 0

    def chunks(body, init=0):
        return lax.fori_loop(0, R // CHUNK, lambda c, s: body(rows(c, CHUNK, CHUNK), s), init, unroll=4)

    def wide(cols):
        return jnp.concatenate([cols] * (D // TILE), axis=1)

    gz_start("qkv")
    for dz in z_offs:
        bias_copy(dz, z).start()
    gz_start("out")
    for dz in z_offs:
        gz("up", dz, z).start()
        gz("down", dz, z).start()

    unit = M * R // TILE
    marks = []
    for b in range(KR // TILE):
        at = lax.rem(z * NQ + (b - HALO // TILE) + unit, unit)
        packed, col = lax.div(at, ROW // TILE), lax.rem(at, ROW // TILE)
        spot = rows(col, TILE, TILE)
        sent, present = r.segment_ids[0:1, spot], r.key_mask[0:1, spot]
        for p in range(1, r.segment_ids.shape[0]):
            sent = jnp.where(packed == p, r.segment_ids[p : p + 1, spot] + p * ROW, sent)
            present = jnp.where(packed == p, r.key_mask[p : p + 1, spot], present)
        sent, present = sent.astype(f32), present.astype(f32)
        keyed = jnp.where(present > 0.5, sent, -1.0)
        if b < HALO // TILE:
            keyed = jnp.where(z > 0, keyed, -1.0)
        else:
            own = b - HALO // TILE
            r.VAL[own * TILE : (own + 1) * TILE, :] = jnp.broadcast_to(present, (TILE, TILE)).T
        marks.append((sent, jnp.broadcast_to(keyed, (TILE, TILE)).T))
    key_pos = lax.broadcasted_iota(jnp.int32, (TILE, TILE), 0)
    query_pos = lax.broadcasted_iota(jnp.int32, (TILE, TILE), 1)
    for i in range(NQ):
        asker = marks[i + HALO // TILE][0]
        for b in range(WIN // TILE):
            allowed = marks[i + b][1] == asker
            if b == WIN // TILE - 1:
                allowed = allowed & (key_pos <= query_pos)
            r.MB[i, b * TILE : (b + 1) * TILE, :] = jnp.where(allowed, 0.0, shut)

    head_of = lax.broadcasted_iota(jnp.int32, (1, HC), 1) // HD
    in_head = [(head_of == h).astype(f32) for h in range(NH)]
    scale = HD ** (-0.5)

    def diagonal(both):
        return jnp.concatenate(
            [both[h * HD : (h + 1) * HD, h * TILE : (h + 1) * TILE] for h in range(NH)], axis=0
        )

    def split_heads(dst, j, whole, factor):
        for h in range(NH):
            one = (whole * (in_head[h] * factor)).astype(bf16)
            for i in range(NQ):
                dst[j, i, h * TILE : (h + 1) * TILE, :] = one[i * TILE : (i + 1) * TILE, :]

    def project(j):
        bias = r.RBI[j]
        query = dot(r.XB[HALO:KR, :], r.WQ[j, 0:D, :]) + bias[1:2, 0:HC]
        split_heads(r.QM, j, query, scale)
        key = dot(r.XB[...], r.WQ[j, D : 2 * D, :])
        r.KN[j] = key.astype(bf16)
        r.KT[j] = (key * scale).astype(bf16).T
        value = (dot(r.XB[...], r.WQ[j, 2 * D : 3 * D, :]) + bias[2:3, 0:HC]).astype(bf16)
        r.VN[j] = value
        r.VT[j] = value.T

    def attend(j):
        for i in range(NQ):
            lo, hi = i * TILE, i * TILE + WIN
            scores = dot_nt(r.KN[j, lo:hi, :], r.QM[j, i])
            scores = scores + jnp.concatenate([r.MB[i]] * NH, axis=1)
            top = jnp.maximum(jnp.max(scores, axis=0, keepdims=True), masked_fill)
            expo = jnp.exp(scores - top)
            total = jnp.maximum(jnp.sum(expo, axis=0, keepdims=True), 1.0)
            probs = (expo * (1.0 / total)).astype(bf16)
            r.PS[j, i] = probs
            context = diagonal(dot(r.VT[j, :, lo:hi], probs)).astype(bf16)
            r.CXT[j, :, i * TILE : (i + 1) * TILE] = context
            r.CX[j, i * TILE : (i + 1) * TILE, :] = context.T


    load[0].wait()
    load[1].wait()
    load_w["qkv"].wait()
    project(z)
    attend(z)
    r.XT[...] = r.XB[HALO:KR, :].T
    r.S[0] = jnp.broadcast_to(
        jnp.sum(r.VAL[...].reshape(R // 8, 8, TILE), axis=0).sum(axis=0, keepdims=True), (8, TILE)
    )
    sum_core(0)
    gather(0, 1, "qkv")
    gather(0, 2, "qkv")
    gather(1, 1, "qkv")
    gather(0, 3, "qkv")
    gather(1, 2, "qkv")
    gather(0, 1, "up", "down")
    for which in (1, 2, 3):
        gather(0, which, "out")
    gather(1, 3, "qkv")
    gather(2, 1, "qkv")
    gather(2, 2, "qkv")
    for dz in z_offs:
        bias_copy(dz, z_from(dz)).wait_recv()
    sum_chips(0)

    def forward_step(t, c):
        j = z_from(t)
        gc_wait("qkv", t)
        project(j)
        attend(j)

        @pl.when(t == 1)
        def _():
            gather(2, 3, "qkv")
            for which in (1, 2, 3):
                gather(1, which, "out")
            gather(1, 1, "up", "down")

        @pl.when(t == 2)
        def _():
            gather(0, 2, "up", "down")

        @pl.when(t == 3)
        def _():
            for which in (1, 2, 3):
                gather(2, which, "out")

        return c

    lax.fori_loop(1, M, forward_step, 0)
    for g in ("out", "up", "down"):
        load_w[g].wait()
    for dz in z_offs:
        gc_wait("out", dz)

    attn = r.bias_out[...]
    for j in range(M):
        attn = attn + dot(r.CX[j], r.WO[j])
    r.ACC[...] = attn

    def moments(k):
        def body(at, s):
            v, valid = r.ACC[at, :], wide(r.VAL[at, :])
            vv = v * valid
            return s[0] + jnp.sum(vv, axis=0, keepdims=True), s[1] + jnp.sum(vv * v, axis=0, keepdims=True)

        zero = jnp.zeros((1, D), f32)
        s = chunks(body, (zero, zero))
        for n in range(2):
            for b in range(D // TILE):
                at = n * (D // TILE) + b
                r.S[k, at : at + 1, :] = s[n][:, b * TILE : (b + 1) * TILE]

    def unfold(total, n):
        return jnp.concatenate([total[n * (D // TILE) + b :][:1] for b in range(D // TILE)], axis=1)

    def variance(total, count):
        col_mean = unfold(total, 0) / count
        return unfold(total, 1) / count - col_mean * col_mean

    moments(1)
    sum_core(1)
    gather(2, 1, "up", "down")
    gather(1, 2, "up", "down")
    sum_chips(1)
    gather(0, 3, "up", "down")
    count = sum_done(0)[0:1, 0:1]
    var_attn = variance(sum_done(1), count)
    omega_attn = jnp.sqrt(1.0 + var_attn)
    gather(1, 3, "up", "down")
    gain_one, shift_one = r.gain_one[...], r.shift_one[...]
    gain_two, shift_two = r.gain_two[...], r.shift_two[...]

    def normed(pre):
        centred = pre - jnp.mean(pre, axis=-1, keepdims=True)
        var = jnp.mean(centred * centred, axis=-1, keepdims=True)
        rstd = lax.rsqrt(var + norm_eps)
        return centred * rstd, rstd

    def norm_back(dy, n, rstd, gain):
        dn = dy * gain
        return rstd * (
            dn - jnp.mean(dn, axis=-1, keepdims=True) - n * jnp.mean(dn * n, axis=-1, keepdims=True)
        )

    def norm_one(c, s):
        at, xat = rows(c, CHUNK, CHUNK), rows(c + HALO // CHUNK, CHUNK, CHUNK)
        n, rstd = normed(r.XB[xat, :].astype(f32) * omega_attn + r.ACC[at, :])
        r.N1[at, :] = n
        r.RS[at, :] = jnp.broadcast_to(rstd, (CHUNK, TILE))
        r.HL[at, :] = (n * gain_one + shift_one).astype(bf16)
        return s

    lax.fori_loop(0, R // CHUNK, norm_one, 0, unroll=4)
    gather(2, 2, "up", "down")

    r.ACC[...] = jnp.broadcast_to(r.bias_down[...], (R, D))
    c0 = (2.0 / jnp.pi) ** 0.5

    def ffn_step(t, c):
        j = z_from(t)

        @pl.when(t > 0)
        def _():
            gc_wait("up", t)
            gc_wait("down", t)

        r.INN[...] = dot(r.HL[...], r.WU[j]) + r.RBI[j, 0:1, 0:F]

        def body(at, s):
            u = r.INN[at, :]
            uu = u * u
            th = jnp.tanh(u * (c0 + (c0 * 0.044715) * uu))
            half = 0.5 + 0.5 * th
            r.AC[j, at, :] = (u * half).astype(bf16)
            r.GP[j, at, :] = half + (0.5 * u) * (1.0 - th * th) * (c0 + (3.0 * 0.044715 * c0) * uu)
            return s

        chunks(body)
        r.ACC[...] += dot(r.AC[j], r.WD[j])

        @pl.when(t == 2)
        def _():
            gather(2, 3, "up", "down")

        return c

    lax.fori_loop(0, M, ffn_step, 0)

    moments(2)
    sum_core(2)
    r.HLT[...] = r.HL[...].T
    sum_chips(2)
    omega_ffn = jnp.sqrt(1.0 + var_attn + variance(sum_done(2), count))
    r.omega[...] = jnp.concatenate([omega_attn, omega_ffn, jnp.zeros((6, D), f32)], axis=0)
    load[2].wait()

    def norm_two(at, s):
        hidden = r.N1[at, :] * gain_one + shift_one
        n, rstd = normed(hidden * omega_ffn + r.ACC[at, :])
        r.GI[at, :] = n * gain_two + shift_two
        dy = r.CT[at, :].astype(f32)
        d_pre = norm_back(dy, n, rstd, gain_two)
        low = d_pre.astype(bf16)
        r.DP[at, :] = d_pre
        r.DF[at, :] = low
        return (
            s[0] + jnp.sum(low.astype(f32), axis=0, keepdims=True),
            s[1] + jnp.sum(dy * n, axis=0, keepdims=True),
            s[2] + jnp.sum(dy, axis=0, keepdims=True),
        )

    zero = jnp.zeros((1, D), f32)
    s = chunks(norm_two, (zero, zero, zero))
    r.V[...] = jnp.zeros(r.V.shape, f32)
    r.VB[...] = jnp.zeros(r.VB.shape, f32)
    for n in range(3):
        r.V[3 + n : 4 + n, :] = s[n]
    put_out = pltpu.make_async_copy(r.GI, r.layer_out, r.ls.at[11])
    put_out.start()

    r.ACC[...] = jnp.zeros((R, D), f32)

    shard = [z_from(t) for t in range(M)]

    def ffn_back(t, c):
        j = z_from(t)
        r.GD[j, 0:F, :] = dot(r.AC[j].T, r.DF[...]).astype(bf16)
        rc_start("down", j)
        r.INN[...] = dot_nt(r.DF[...], r.WD[j])

        def body(at, s):
            low = (r.INN[at, :] * r.GP[j, at, :]).astype(bf16)
            r.DI[at, :] = low
            return s + jnp.sum(low.astype(f32), axis=0, keepdims=True)

        r.VB[j, 0:1, 0:F] = chunks(body, jnp.zeros((1, F), f32))
        r.GU[j, 0:D, :] = dot(r.HLT[...], r.DI[...]).astype(bf16)
        rc_start("up", j)
        r.ACC[...] += dot_nt(r.DI[...], r.WU[j])

        rp_start("down", j)

        @pl.when(t > 0)
        def _():
            rp_start("up", z_from(t - 1))

        @pl.when(t == 2)
        def _():
            mids("down", shard[0])

        return c

    lax.fori_loop(0, M, ffn_back, 0)

    put_out.wait()

    def back_one(at, s):
        dy = r.ACC[at, :] + omega_ffn * r.DP[at, :]
        n = r.N1[at, :]
        d_pre = norm_back(dy, n, r.RS[at, 0:1], gain_one)
        low = d_pre.astype(bf16)
        r.DA[at, :] = low
        r.GI[at, :] = omega_attn * d_pre
        return (
            s[0] + jnp.sum(low.astype(f32), axis=0, keepdims=True),
            s[1] + jnp.sum(dy * n, axis=0, keepdims=True),
            s[2] + jnp.sum(dy, axis=0, keepdims=True),
        )

    s = chunks(back_one, (zero, zero, zero))
    for n in range(3):
        r.V[n : n + 1, :] = s[n]
    for j in range(M):
        r.V[6 + j : 7 + j, :] = r.VB[j, 0:1, :]
    vc().start()
    rp_start("up", shard[M - 1])
    mids("down", shard[1])
    mids("up", shard[0])

    def both(step, *a):
        step("down", *a)
        step("up", *a)

    def out_back(j, c):
        r.GO[j, 0:HC, :] = dot(r.CXT[j], r.DA[...]).astype(bf16)
        rc_start("out", j)
        split_heads(r.DCM, j, dot_nt(r.DA[...], r.WO[j]), 1.0)
        return c

    lax.fori_loop(0, M, out_back, 0)
    rz_start("down", shard[0])

    def attend_back(j, which):
        for i in which:
            lo, hi = i * TILE, i * TILE + WIN
            probs_low = r.PS[j, i]
            probs = probs_low.astype(f32)
            d_context = r.DCM[j, i]
            d_probs = dot_nt(r.VN[j, lo:hi, :], d_context)
            delta = jnp.sum(probs * d_probs, axis=0, keepdims=True)
            d_scores = (probs * (d_probs - delta)).astype(bf16)
            r.DV[j, lo:hi, :] += dot(probs_low, d_context)
            r.DK[j, lo:hi, :] += dot(d_scores, r.QM[j, i])
            d_query = diagonal(dot(r.KT[j, :, lo:hi], d_scores)).astype(bf16)
            r.DL[j, 0, i * TILE : (i + 1) * TILE, :] = d_query.T

    early = range(min(HALO // TILE, NQ))

    def attend_early(t, c):
        j = step_of(t)
        r.DK[j] = jnp.zeros((KR, HC), f32)
        r.DV[j] = jnp.zeros((KR, HC), f32)
        attend_back(j, early)
        r.HS[j, 0:HALO, :] = r.DK[j, 0:HALO, :].astype(bf16)
        r.HS[j, HALO : 2 * HALO, :] = r.DV[j, 0:HALO, :].astype(bf16)

        @pl.when(joined)
        def _():
            halo(j).start()

        @pl.when(t == 0)
        def _():
            vec_plane()
            for_all("out", rp_start)

        @pl.when(t == 1)
        def _():
            mids("up", shard[1])
            mids("down", shard[2])
            rz_start("up", shard[0])

        @pl.when(t == 2)
        def _():
            rz_start("down", shard[1])

        @pl.when(t == 3)
        def _():
            vec_z()

        return c

    def qkv_back(j):
        @pl.when(lax.rem((z + 1) * R, ROW) > 0)
        def _():
            halo(j).wait_recv()
            r.DK[j, R:KR, :] += r.HR[j, 0:HALO, :].astype(f32)
            r.DV[j, R:KR, :] += r.HR[j, HALO : 2 * HALO, :].astype(f32)

        r.DL[j, 1] = r.DK[j, HALO:KR, :].astype(bf16)
        r.DL[j, 2] = r.DV[j, HALO:KR, :].astype(bf16)
        two = [jnp.sum(r.DL[j, n].astype(f32), axis=0, keepdims=True) for n in (0, 2)]
        two = jnp.concatenate(two, axis=1)
        for n in range(2 * HC // TILE):
            r.VB[j, 1 + n : 2 + n, 0:TILE] = two[:, n * TILE : (n + 1) * TILE]
        for n in range(3):
            r.GQ[j, n * D : (n + 1) * D, :] = dot(r.XT[...], r.DL[j, n]).astype(bf16)
        rc_start("qkv", j)

    def back_in(j, c):
        r.GI[...] += (
            dot_nt(r.DL[j, 0], r.WQ[j, 0:D, :])
            + dot_nt(r.DL[j, 1], r.WQ[j, D : 2 * D, :])
            + dot_nt(r.DL[j, 2], r.WQ[j, 2 * D : 3 * D, :])
        )
        return c

    def for_all(g, step):
        lax.fori_loop(0, M, lambda j, c: (step(g, j), c)[1], 0)

    lax.fori_loop(0, M, attend_early, 0)

    def attend_late(t, c):
        j = step_of(t)
        attend_back(j, range(len(early), NQ))
        qkv_back(j)

        @pl.when(t == 0)
        def _():
            mids("up", shard[2])
            for n in range(3, M):
                both(mids, shard[n])
            rz_start("up", shard[1])
            rz_start("down", shard[2])

        @pl.when(t > 0)
        def _():
            rp_start("qkv", step_of(t - 1))

        @pl.when(t == 1)
        def _():
            for_all("out", mids)

        @pl.when(t == 2)
        def _():
            rz_start("up", shard[2])
            for n in range(3, M):
                both(rz_start, shard[n])

        @pl.when(t > 1)
        def _():
            mids("qkv", step_of(t - 2))

        @pl.when(t == 3)
        def _():
            for_all("out", rz_start)

        @pl.when(t > 3)
        def _():
            rz_start("qkv", step_of(t - 4))

        return c

    lax.fori_loop(0, M, attend_late, 0)
    for j in range(M):
        for n in range(2 * HC // TILE):
            at = j * (2 * HC // TILE) + n
            r.S[3, at : at + 1, :] = r.VB[j, 1 + n : 2 + n, 0:TILE]
    sum_core(3)
    lax.fori_loop(0, 1, back_in, 0)
    rp_start("qkv", step_of(M - 1), True)
    rz_start("qkv", step_of(M - 4))
    sum_chips(3)
    mids("qkv", step_of(M - 2))
    lax.fori_loop(1, M, back_in, 0)
    put_in = pltpu.make_async_copy(r.GI, r.grad_layer_in, r.ls.at[12])
    put_in.start()
    rz_start("qkv", step_of(M - 3))
    ap_start("down")
    ap_start("up")
    rz_start("qkv", step_of(M - 2))
    rz_start("qkv", step_of(M - 1), True)
    ap_start("out")
    ac_start("down")
    ac_start("up")
    ac_start("out")
    total = vec_done()
    r.vectors[0:6, :] = total[0:6]
    for j in range(M):
        r.VB[j, 0:1, :] = total[6 + j : 7 + j]
    total = sum_done(3)
    for j in range(M):
        for n in range(2 * HC // TILE):
            at = j * (2 * HC // TILE) + n
            r.VB[j, 1 + n : 2 + n, 0:TILE] = total[at : at + 1]
    r.vectors[6:7, :] = r.VB[z, 0:1, :]
    r.vectors[7:8, :] = jnp.zeros((1, D), f32)
    for n in range(2 * HC // TILE):
        r.vectors[7:8, n * TILE : (n + 1) * TILE] = r.VB[z, 1 + n : 2 + n, 0:TILE]
    for g in ("down", "up", "out"):
        ac_wait(g)
    ap_start("qkv")
    ac_start("qkv")
    ac_wait("qkv")

    for g in group:
        g_sent(g)
        r_sent(g)
    for dz in z_offs:
        bias_copy(dz, z).wait_send()
    for k in range(4):
        sum_sent(k)
    vec_sent()

    @pl.when(joined)
    def _():
        lax.fori_loop(0, M, lambda j, c: (halo(j).wait_send(), c)[1], 0)

    put_in.wait()


def shards(
    layer_in,
    cotangent,
    w_qkv,
    bias_qv,
    w_out,
    bias_out,
    gain_one,
    shift_one,
    w_up,
    bias_up,
    w_down,
    bias_down,
    gain_two,
    shift_two,
    segment_ids,
    key_mask,
):
    M, NDP = lax.axis_size("mp"), lax.axis_size("dp")
    D = layer_in.shape[1]
    HC, F, ROW = w_qkv.shape[2], w_up.shape[1], segment_ids.shape[1]
    R = layer_in.shape[0] // M
    NP, NH, NQ, KR, WIN = NDP // CORES, HC // HD, R // TILE, R + HALO, HALO + TILE
    sz = types.SimpleNamespace(M=M, NP=NP, R=R, ROW=ROW, HC=HC, F=F, D=D, W=max(F, HC))

    hbm, vmem = pl.BlockSpec(memory_space=pl.ANY), pl.BlockSpec(memory_space=pltpu.VMEM)
    ins = dict(
        layer_in=(layer_in, hbm),
        cotangent=(cotangent, hbm),
        w_qkv=(w_qkv.reshape(3 * D, HC), hbm),
        w_out=(w_out, hbm),
        w_up=(w_up, hbm),
        w_down=(w_down, hbm),
        bias_qv=(bias_qv, vmem),
        bias_up=(bias_up[None], vmem),
        bias_out=(bias_out[None], vmem),
        gain_one=(gain_one[None], vmem),
        shift_one=(shift_one[None], vmem),
        bias_down=(bias_down[None], vmem),
        gain_two=(gain_two[None], vmem),
        shift_two=(shift_two[None], vmem),
        segment_ids=(segment_ids, vmem),
        key_mask=(key_mask, vmem),
    )
    outs = dict(
        omega=((8, D), f32, vmem),
        layer_out=((R, D), f32, hbm),
        grad_layer_in=((R, D), f32, hbm),
        grad_w_qkv=((3 * D, HC), bf16, hbm),
        grad_w_out=((HC, D), bf16, hbm),
        grad_w_up=((D, F), bf16, hbm),
        grad_w_down=((F, D), bf16, hbm),
        vectors=((8, D), f32, vmem),
    )
    scratch = dict(
        XB=((KR, D), bf16),
        XT=((D, R), bf16),
        CT=((R, D), bf16),
        WQ=((M, 3 * D, HC), bf16),
        WO=((M, HC, D), bf16),
        WU=((M, D, F), bf16),
        WD=((M, F, D), bf16),
        SB=((8, sz.W), f32),
        RBI=((M, 8, sz.W), f32),
        QM=((M, NQ, NH * TILE, HC), bf16),
        KN=((M, KR, HC), bf16),
        KT=((M, HC, KR), bf16),
        VN=((M, KR, HC), bf16),
        VT=((M, HC, KR), bf16),
        PS=((M, NQ, WIN, NH * TILE), bf16),
        CX=((M, R, HC), bf16),
        CXT=((M, HC, R), bf16),
        DCM=((M, NQ, NH * TILE, HC), bf16),
        MB=((NQ, WIN, TILE), f32),
        VAL=((R, TILE), f32),
        ACC=((R, D), f32),
        N1=((R, D), f32),
        RS=((R, TILE), f32),
        HL=((R, D), bf16),
        HLT=((D, R), bf16),
        INN=((R, F), f32),
        AC=((M, R, F), bf16),
        GP=((M, R, F), f32),
        DP=((R, D), f32),
        DF=((R, D), bf16),
        DI=((R, F), bf16),
        DA=((R, D), bf16),
        GI=((R, D), f32),
        DK=((M, KR, HC), f32),
        DV=((M, KR, HC), f32),
        DL=((M, 3, R, HC), bf16),
        HS=((M, 2 * HALO, HC), bf16),
        HR=((M, 2 * HALO, HC), bf16),
        VB=((M, 8, D), f32),
    )
    for tag, shape in (("Q", (3 * D, HC)), ("O", (HC, D)), ("U", (D, F)), ("D", (F, D))):
        pr = -(-shape[0] // (NDP * PACK)) * PACK
        scratch["G" + tag] = ((M, pr * NDP, shape[1]), bf16)
        scratch["RA" + tag] = ((M, pr * NP, shape[1]), bf16)
        scratch["RB" + tag] = ((NP - 1, M, pr, shape[1]), bf16)
        scratch["QB" + tag] = ((M, pr, shape[1]), bf16)
        scratch["RC" + tag] = ((M - 1, pr, shape[1]), bf16)
        scratch["O" + tag] = ((pr * NDP, shape[1]), bf16)
    vec_rows = -(-(6 + M) // 8) * 8
    scratch["V"] = scratch["Vc"] = ((vec_rows, D), f32)
    scratch["Vp"] = ((NP, vec_rows, D), f32)
    scratch["Vz"] = ((M, vec_rows, D), f32)
    scratch["S"] = scratch["Sc"] = ((4, 8, TILE), f32)
    scratch["Sa"] = ((4, NP * M, 8, TILE), f32)
    halves = 2 if any(-(-n // (NDP * PACK)) % 2 == 0 for n in (3 * D, D, F)) else 1
    sems = dict(
        ls=(13,),
        gzs=(4, M - 1),
        gzr=(4, M - 1),
        gps=(4, halves, NP - 1, M - 1),
        gpr=(4, halves, NP - 1, M - 1),
        gcs=(4, M - 1),
        gcr=(4, M - 1),
        bzs=(M - 1,),
        bzr=(M - 1,),
        rcs=(4, M),
        rcr=(4, M),
        rps=(4, halves, NP - 1, M),
        rpr=(4, halves, NP - 1, M),
        rzs=(4, M - 1),
        rzr=(4, M - 1),
        aps=(4, NP - 1),
        apr=(4, NP - 1),
        acs=(4,),
        acr=(4,),
        scs=(4,),
        scr=(4,),
        sas=(4, NP * M - 1),
        sar=(4, NP * M - 1),
        vs=(NP - 1 + M,),
        vr=(NP - 1 + M,),
        hss=(M,),
        hsr=(M,),
    )
    names = list(ins) + list(outs) + list(scratch) + list(sems)
    got = pl.pallas_call(
        functools.partial(layer_kernel, sz, names),
        out_shape=[jax.ShapeDtypeStruct(s, t) for s, t, _ in outs.values()],
        in_specs=[spec for _, spec in ins.values()],
        out_specs=[spec for _, _, spec in outs.values()],
        scratch_shapes=[pltpu.VMEM(s, t) for s, t in scratch.values()]
        + [pltpu.SemaphoreType.DMA(s) for s in sems.values()],
        compiler_params=pltpu.CompilerParams(
            collective_id=0, has_side_effects=True, vmem_limit_bytes=62 << 20
        ),
    )(*[value for value, _ in ins.values()])
    shapes = [(2, D), (R, D), (R, D), (3 * D, HC), (2, HC), (HC, D)] + [(1, D)] * 3
    shapes += [(D, F), (1, F), (F, D)] + [(1, D)] * 3
    big = (1, 2, 3, 5, 9, 11)
    done = list(pl.pallas_call(
        functools.partial(result_kernel, HC, F),
        out_shape=[jax.ShapeDtypeStruct(s, f32) for s in shapes],
        in_specs=[vmem if n in ("omega", "vectors") else hbm for n in outs],
        out_specs=[hbm if n in big else vmem for n in range(len(shapes))],
        scratch_shapes=[
            pltpu.VMEM(shape, t)
            for n in (1, 2, 3, 9, 11, 5)
            for shape, t in ((shapes[n], f32 if n < 3 else bf16), ((8, TILE) if n < 3 else shapes[n], f32))
        ]
        + [pltpu.SemaphoreType.DMA((12,))],
    )(*got))
    done[3] = done[3].reshape(3, D, HC)
    return tuple(v[0] if v.shape[0] == 1 else v for v in done)


def result_kernel(HC, F, *refs):
    omega, layer_out, grad_in, g_qkv, g_out, g_up, g_down, vectors = refs[:8]
    out, held, sem = refs[8:23], refs[23:-1], refs[-1]
    reads, writes = [], []
    pairs = ((layer_out, 1), (grad_in, 2), (g_qkv, 3), (g_up, 9), (g_down, 11), (g_out, 5))
    for n, (src, at) in enumerate(pairs):
        low, high = held[2 * n], held[2 * n + 1]
        reads.append(pltpu.make_async_copy(src, low, sem.at[n]))
        writes.append(pltpu.make_async_copy(low if n < 2 else high, out[at], sem.at[len(pairs) + n]))
        reads[n].start()
    out[0][...] = omega[0:2, :]
    out[4][0:1, :] = vectors[7:8, 0:HC]
    out[4][1:2, :] = vectors[7:8, HC : 2 * HC]
    out[10][...] = vectors[6:7, 0:F]
    for n, at in enumerate((6, 7, 8, 12, 13, 14)):
        out[at][...] = vectors[n : n + 1, :]
    for n in range(len(pairs)):
        reads[n].wait()
        if n >= 2:
            held[2 * n + 1][...] = held[2 * n][...].astype(f32)
        writes[n].start()
    for copy in writes:
        copy.wait()


def solution(mesh):
    in_specs = (
        P("dp", None),
        P("dp", None),
        P(None, None, "mp"),
        P(None, "mp"),
        P("mp", None),
        P(),
        P(),
        P(),
        P(None, "mp"),
        P("mp"),
        P("mp", None),
        P(),
        P(),
        P(),
        P("dp", None),
        P("dp", None),
    )
    out_specs = (
        P(),
        P(("dp", "mp"), None),
        P(("dp", "mp"), None),
        P(None, None, "mp"),
        P(None, "mp"),
        P("mp", None),
        P(),
        P(),
        P(),
        P(None, "mp"),
        P("mp"),
        P("mp", None),
        P(),
        P(),
        P(),
    )
    return jax.shard_map(shards, mesh=mesh, in_specs=in_specs, out_specs=out_specs, check_vma=False)
```

```python
import functools
import types

import jax
import jax.numpy as jnp
from jax import lax
from jax.experimental import pallas as pl
from jax.experimental.pallas import tpu as pltpu
from jax.sharding import PartitionSpec as P

HD = 64
LONGEST = 250
TILE = 128
HALO = -(-LONGEST // TILE) * TILE
CHUNK = 64
PARTS = 2
PACK = 16
CORES = 2

norm_eps = 1e-05
masked_fill = -1000000000.0
shut = -1e30
MESH = pl.DeviceIdType.MESH
f32 = jnp.float32
bf16 = jnp.bfloat16


def dot(a, b):
    return lax.dot_general(a, b, (((1,), (0,)), ((), ())), preferred_element_type=f32)


def dot_nt(a, b):
    return lax.dot_general(a, b, (((1,), (1,)), ((), ())), preferred_element_type=f32)


def layer_kernel(sz, names, *refs):
    r = types.SimpleNamespace(**dict(zip(names, refs)))
    M, NP, R, ROW, HC, F, D = sz.M, sz.NP, sz.R, sz.ROW, sz.HC, sz.F, sz.D
    NDP = NP * CORES
    NH, NQ, KR, WIN = HC // HD, R // TILE, R + HALO, HALO + TILE
    dp, z = lax.axis_index("dp"), lax.axis_index("mp")
    core, plane = lax.rem(dp, CORES), lax.div(dp, CORES)
    piece = core * NP + plane
    partner = (plane * CORES + 1 - core, z)

    def plane_to(off):
        return (lax.rem(plane + off, NP) * CORES + core, z)

    def plane_from(off):
        return lax.rem(plane + NP - off, NP)

    def flipped(at, mask, count):
        for b in range(count.bit_length() - 1):
            if mask >> b & 1:
                at = at + (1 - 2 * lax.rem(lax.div(at, 1 << b), 2)) * (1 << b)
        return at

    def z_from(dz):
        if isinstance(dz, int):
            return flipped(z, dz, M)
        return sum(
            (lax.rem(lax.div(z, 1 << b) + lax.div(dz, 1 << b), 2)) * (1 << b) for b in range(M.bit_length() - 1)
        )

    def z_apart(j):
        return z_from(j)

    def z_to(dz):
        return (dp, z_from(dz))

    def chip_to(n):
        return (lax.rem(plane + n // M, NP) * CORES + core, lax.rem(z + n % M, M))

    plane_offs, z_offs = range(1, NP), range(1, M)
    bits = NP.bit_length() - 1

    def flip(mask):
        return flipped(plane, mask, NP)

    def flip_to(mask):
        return (flip(mask) * CORES + core, z)

    orders = (tuple(range(bits)), tuple(reversed(range(bits))))

    def subsets(some):
        masks = [0]
        for b in some:
            masks = masks + [m | 1 << b for m in masks]
        return masks

    def rcopy(src, dst, send, recv, dev):
        return pltpu.make_async_remote_copy(
            src_ref=src, dst_ref=dst, send_sem=send, recv_sem=recv, device_id=dev, device_id_type=MESH
        )

    def rows(at, count, unit):
        return pl.ds(pl.multiple_of(at * unit, unit), count)

    bar = pltpu.get_barrier_semaphore()
    peers = [partner] + [chip_to(n) for n in range(1, NP * M)]
    for peer in peers:
        pl.semaphore_signal(bar, inc=1, device_id=peer, device_id_type=MESH)

    w_in = dict(qkv=r.w_qkv, out=r.w_out, up=r.w_up, down=r.w_down)
    w_all = dict(qkv=r.WQ, out=r.WO, up=r.WU, down=r.WD)
    group = ("qkv", "out", "up", "down")
    load = [
        pltpu.make_async_copy(r.layer_in.at[rows(z, R, R)], r.XB.at[pl.ds(HALO, R)], r.ls.at[0]),
        pltpu.make_async_copy(
            r.layer_in.at[rows(lax.rem(z * (R // TILE) + (M * R - HALO) // TILE, M * R // TILE), HALO, TILE)],
            r.XB.at[pl.ds(0, HALO)],
            r.ls.at[1],
        ),
        pltpu.make_async_copy(r.cotangent.at[rows(z, R, R)], r.CT, r.ls.at[2]),
    ]
    load_w = {
        g: pltpu.make_async_copy(w_in[g], w_all[g].at[z], r.ls.at[3 + n]) for n, g in enumerate(group)
    }
    little = {
        name: pltpu.make_async_copy(getattr(r, name + "_in"), getattr(r, name), r.bs.at[n])
        for n, name in enumerate(sz.little)
    }
    for name in sz.little:
        little[name].start()
    load[0].start()
    load[1].start()
    for g in group:
        load_w[g].start()
    load[2].start()

    pl.semaphore_wait(bar, len(peers))

    def g_split(g):
        return w_in[g].shape[0] % (NDP * PACK) == 0

    def gz(g, dz, zs):
        n = group.index(g)
        if not g_split(g):
            src, dst = w_in[g], w_all[g].at[zs]
        else:
            pr = w_in[g].shape[0] // NDP
            src, dst = w_in[g].at[rows(piece, pr, pr)], w_all[g].at[zs, rows(piece, pr, pr)]
        return rcopy(src, dst, r.gzs.at[n, dz - 1], r.gzr.at[n, dz - 1], z_to(dz))

    def g_halves(g):
        return 2 if w_in[g].shape[0] // NDP % (2 * PACK) == 0 else 1

    def gp(g, h, s, m, dz, there):
        n, hp = group.index(g), w_in[g].shape[0] // NDP // g_halves(g)
        order = orders[h]
        have = subsets(order[:s])[m] ^ (there << order[s])
        part = w_all[g].at[z_from(dz), rows((core * NP + flip(have)) * g_halves(g) + h, hp, hp)]
        at = (n, h, (1 << s) - 1 + m, dz - 1)
        return rcopy(part, part, r.gps.at[at], r.gpr.at[at], flip_to(1 << order[s]))

    def gc(g, dz, at_core):
        n, half = group.index(g), w_in[g].shape[0] // CORES
        part = w_all[g].at[z_from(dz), rows(at_core, half, half)]
        return rcopy(part, part, r.gcs.at[n, dz - 1], r.gcr.at[n, dz - 1], partner)

    def gz_start(g):
        for dz in z_offs:
            gz(g, dz, z).start()

    def gp_all(g, s):
        return [(h, m) for h in range(g_halves(g)) for m in range(1 << s)]

    def gp_start(g, s, dzs):
        for dz in dzs:
            if s == 0:
                gz(g, dz, z_from(dz)).wait_recv()
            if not g_split(g):
                continue
            if s > 0:
                for h, m in gp_all(g, s - 1):
                    gp(g, h, s - 1, m, dz, 1).wait_recv()
            if s < bits:
                for h, m in gp_all(g, s):
                    gp(g, h, s, m, dz, 0).start()
            else:
                gc(g, dz, core).start()

    near = [tuple(z_offs[0:1]), tuple(z_offs[1:2]), tuple(z_offs[2:])]

    def gather(phase, which, *groups):
        for dz in near[which - 1]:
            for s in ((0,), range(1, bits), (bits,))[phase]:
                for g in groups:
                    gp_start(g, s, (dz,))

    def gc_wait(g, dz):
        if g_split(g):
            gc(g, dz, 1 - core).wait_recv()

    def g_sent(g):
        for dz in z_offs:
            gz(g, dz, z).wait_send()
            if g_split(g):
                for s in range(bits):
                    for h, m in gp_all(g, s):
                        gp(g, h, s, m, dz, 0).wait_send()
                gc(g, dz, core).wait_send()

    def bias_copy(dz, zs):
        return rcopy(r.SB, r.RBI.at[zs], r.bzs.at[dz - 1], r.bzr.at[dz - 1], z_to(dz))

    g_part = dict(qkv=r.GQ, out=r.GO, up=r.GU, down=r.GD)
    g_ra = dict(qkv=r.RAQ, out=r.RAO, up=r.RAU, down=r.RAD)
    g_rb = dict(qkv=r.RBQ, out=r.RBO, up=r.RBU, down=r.RBD)
    g_qb = dict(qkv=r.QBQ, out=r.QBO, up=r.QBU, down=r.QBD)
    g_rc = dict(qkv=r.RCQ, out=r.RCO, up=r.RCU, down=r.RCD)
    g_out = dict(qkv=r.OQ, out=r.OO, up=r.OU, down=r.OD)
    g_res = dict(qkv=r.grad_w_qkv, out=r.grad_w_out, up=r.grad_w_up, down=r.grad_w_down)

    def pr_of(g):
        return g_part[g].shape[1] // NDP

    def rc(g, j):
        n, half = group.index(g), pr_of(g) * NP
        return rcopy(
            g_part[g].at[j, rows(1 - core, half, half)], g_ra[g].at[j], r.rcs.at[n, j], r.rcr.at[n, j], partner
        )

    def r_halves(g):
        return 2 if pr_of(g) % (2 * PACK) == 0 else 1

    def rp(g, off, j):
        n, pr = group.index(g), pr_of(g)
        at = core * NP + lax.rem(plane + off, NP)
        return rcopy(
            g_part[g].at[j, rows(at, pr, pr)],
            g_rb[g].at[off - 1, j],
            r.rps.at[n, 0, off - 1, j],
            r.rpr.at[n, 0, off - 1, j],
            plane_to(off),
        )

    def r_rows(g, h, mask):
        hp = pr_of(g) // r_halves(g)
        return rows((core * NP + flip(mask)) * r_halves(g) + h, hp, hp)

    def r_slot(g, h, s, m):
        hp = pr_of(g) // r_halves(g)
        return NP - (1 << (bits - s)) + m, pl.ds(h * hp, hp)

    def rh(g, h, s, m, j):
        n, order = group.index(g), orders[h]
        slot, half = r_slot(g, h, s, m)
        away = subsets(order[s + 1 :])[m] | 1 << order[s]
        return rcopy(
            g_part[g].at[j, r_rows(g, h, away)],
            g_rb[g].at[slot, j, half],
            r.rps.at[n, h, slot, j],
            r.rpr.at[n, h, slot, j],
            flip_to(1 << order[s]),
        )

    def rh_all(g, s):
        return [(h, m) for h in range(r_halves(g)) for m in range(1 << (bits - 1 - s))]

    def rz(g, j, dz):
        n = group.index(g)
        return rcopy(g_qb[g].at[j], g_rc[g].at[dz - 1], r.rzs.at[n, dz - 1], r.rzr.at[n, dz - 1], (dp, j))

    def ap(g, off, at_plane):
        n, pr = group.index(g), pr_of(g)
        part = g_out[g].at[rows(core * NP + at_plane, pr, pr)]
        return rcopy(part, part, r.aps.at[n, off - 1], r.apr.at[n, off - 1], plane_to(off))

    def ac(g, at_core):
        n, half = group.index(g), pr_of(g) * NP
        part = g_out[g].at[rows(at_core, half, half)]
        return rcopy(part, part, r.acs.at[n], r.acr.at[n], partner)

    def rc_start(g, j):
        rc(g, j).start()

    def rp_start(g, j, direct=False):
        rc(g, j).wait_recv()
        half = pr_of(g) * NP
        mine = rows(core, half, half)
        g_part[g][j, mine] = (g_part[g][j, mine].astype(f32) + g_ra[g][j].astype(f32)).astype(bf16)
        if direct:
            for off in plane_offs:
                rp(g, off, j).start()
        else:
            for h, m in rh_all(g, 0):
                rh(g, h, 0, m, j).start()

    def rp_step(g, j, s):
        for h, m in rh_all(g, s - 1):
            rh(g, h, s - 1, m, j).wait_recv()
            slot, half = r_slot(g, h, s - 1, m)
            at = r_rows(g, h, subsets(orders[h][s:])[m])
            g_part[g][j, at] = (g_part[g][j, at].astype(f32) + g_rb[g][slot, j, half].astype(f32)).astype(bf16)
        for h, m in rh_all(g, s):
            rh(g, h, s, m, j).start()

    def mids(g, j):
        for s in range(1, bits):
            rp_step(g, j, s)

    def rz_start(g, j, direct=False):
        pr = pr_of(g)
        total = g_part[g][j, rows(piece, pr, pr)].astype(f32)
        if direct:
            for off in plane_offs:
                rp(g, off, j).wait_recv()
                total = total + g_rb[g][off - 1, j].astype(f32)
        else:
            for h, m in rh_all(g, bits - 1):
                rh(g, h, bits - 1, m, j).wait_recv()
            total = total + g_rb[g][NP - 2, j].astype(f32)
        g_qb[g][j] = total.astype(bf16)

        @pl.when(j != z)
        def _():
            rz(g, j, z_apart(j)).start()

    def ap_start(g):
        pr = pr_of(g)
        total = g_qb[g][z].astype(f32)
        for dz in z_offs:
            rz(g, z, dz).wait_recv()
            total = total + g_rc[g][dz - 1].astype(f32)
        g_out[g][rows(piece, pr, pr)] = total.astype(bf16)
        for off in plane_offs:
            ap(g, off, plane).start()

    def ac_start(g):
        for off in plane_offs:
            ap(g, off, plane_from(off)).wait_recv()
        ac(g, core).start()

    def result(g):
        n = group.index(g)
        got = g_out[g].at[pl.ds(0, g_res[g].shape[0])]
        return pltpu.make_async_copy(got, g_res[g], r.ls.at[7 + n])

    def ac_wait(g):
        ac(g, 1 - core).wait_recv()
        result(g).start()

    def r_sent(g):
        def one(j, c):
            rc(g, j).wait_send()
            for s in range(bits):
                for h, m in rh_all(g, s):
                    rh(g, h, s, m, j).wait_send()
            return c

        def direct(j, c):
            rc(g, j).wait_send()
            for off in plane_offs:
                rp(g, off, j).wait_send()
            return c

        if g == "qkv":
            lax.fori_loop(0, M - 1, lambda t, c: one(step_of(t), c), 0)
            direct(step_of(M - 1), 0)
        else:
            lax.fori_loop(0, M, one, 0)
        for dz in z_offs:
            rz(g, z_from(dz), dz).wait_send()
        for off in plane_offs:
            ap(g, off, plane).wait_send()
        ac(g, core).wait_send()
        result(g).wait()

    def sc(k):
        return rcopy(r.S.at[k], r.Sc.at[k], r.scs.at[k], r.scr.at[k], partner)

    def sa(k, n, there):
        if there:
            at = lax.rem(plane + NP - n // M, NP) * M + lax.rem(z + M - n % M, M)
        else:
            at = plane * M + z
        return rcopy(r.Sa.at[k, at], r.Sa.at[k, at], r.sas.at[k, n - 1], r.sar.at[k, n - 1], chip_to(n))

    def sum_core(k):
        sc(k).start()

    def sum_chips(k):
        sc(k).wait_recv()
        r.Sa[k, plane * M + z] = r.S[k] + r.Sc[k]
        for n in reversed(range(1, NP * M)):
            sa(k, n, False).start()

    def sum_done(k):
        for n in range(1, NP * M):
            sa(k, n, True).wait_recv()
        total = r.Sa[k, 0]
        for n in range(1, NP * M):
            total = total + r.Sa[k, n]
        return total

    def sum_sent(k):
        sc(k).wait_send()
        for n in range(1, NP * M):
            sa(k, n, False).wait_send()

    def vc():
        return rcopy(r.V, r.Vc, r.vs.at[0], r.vr.at[0], partner)

    def vp(off, at):
        return rcopy(r.Vp.at[at], r.Vp.at[at], r.vs.at[off], r.vr.at[off], plane_to(off))

    def vz(dz, at):
        return rcopy(r.Vz.at[at], r.Vz.at[at], r.vs.at[NP - 1 + dz], r.vr.at[NP - 1 + dz], z_to(dz))

    def vec_plane():
        vc().wait_recv()
        r.Vp[plane] = r.V[...] + r.Vc[...]
        for off in plane_offs:
            vp(off, plane).start()

    def vec_z():
        for off in plane_offs:
            vp(off, plane_from(off)).wait_recv()
        total = r.Vp[0]
        for s in plane_offs:
            total = total + r.Vp[s]
        r.Vz[z] = total
        for dz in z_offs:
            vz(dz, z).start()

    def vec_done():
        for dz in z_offs:
            vz(dz, z_from(dz)).wait_recv()
        total = r.Vz[0]
        for s in z_offs:
            total = total + r.Vz[s]
        return total

    def vec_sent():
        vc().wait_send()
        for off in plane_offs:
            vp(off, plane).wait_send()
        for dz in z_offs:
            vz(dz, z).wait_send()

    def halo(j):
        return rcopy(r.HS.at[j], r.HR.at[j], r.hss.at[j], r.hsr.at[j], (dp, lax.rem(z + M - 1, M)))

    sharing = max(ROW // R, 1)
    first_shard = lax.rem((lax.div(z, sharing) + 1) * sharing, M)

    def step_of(t):
        return lax.rem(first_shard + t, M)

    joined = lax.rem(z * R, ROW) > 0

    def chunks(body, init=0):
        return lax.fori_loop(0, R // CHUNK, lambda c, s: body(rows(c, CHUNK, CHUNK), s), init, unroll=4)

    def wide(cols):
        return jnp.concatenate([cols] * (D // TILE), axis=1)

    gz_start("qkv")
    little["bias_up"].wait()
    little["bias_qv"].wait()
    r.SB[...] = jnp.zeros((8, sz.W), f32)
    r.SB[0:1, 0:F] = r.bias_up[...]
    r.SB[1:3, 0:HC] = r.bias_qv[...]
    r.RBI[z] = r.SB[...]
    for dz in z_offs:
        bias_copy(dz, z).start()
    gz_start("out")
    for dz in z_offs:
        gz("up", dz, z).start()
        gz("down", dz, z).start()

    for name in sz.little[2:]:
        little[name].wait()
    unit = M * R // TILE
    marks = []
    for b in range(KR // TILE):
        at = lax.rem(z * NQ + (b - HALO // TILE) + unit, unit)
        packed, col = lax.div(at, ROW // TILE), lax.rem(at, ROW // TILE)
        spot = rows(col, TILE, TILE)
        sent, present = r.segment_ids[0:1, spot], r.key_mask[0:1, spot]
        for p in range(1, r.segment_ids.shape[0]):
            sent = jnp.where(packed == p, r.segment_ids[p : p + 1, spot] + p * ROW, sent)
            present = jnp.where(packed == p, r.key_mask[p : p + 1, spot], present)
        sent, present = sent.astype(f32), present.astype(f32)
        keyed = jnp.where(present > 0.5, sent, -1.0)
        if b < HALO // TILE:
            keyed = jnp.where(z > 0, keyed, -1.0)
        else:
            own = b - HALO // TILE
            r.VAL[own * TILE : (own + 1) * TILE, :] = jnp.broadcast_to(present, (TILE, TILE)).T
        marks.append((sent, jnp.broadcast_to(keyed, (TILE, TILE)).T))
    key_pos = lax.broadcasted_iota(jnp.int32, (TILE, TILE), 0)
    query_pos = lax.broadcasted_iota(jnp.int32, (TILE, TILE), 1)
    for i in range(NQ):
        asker = marks[i + HALO // TILE][0]
        for b in range(WIN // TILE):
            allowed = marks[i + b][1] == asker
            if b == WIN // TILE - 1:
                allowed = allowed & (key_pos <= query_pos)
            r.MB[i, b * TILE : (b + 1) * TILE, :] = jnp.where(allowed, 0.0, shut)

    head_of = lax.broadcasted_iota(jnp.int32, (1, HC), 1) // HD
    in_head = [(head_of == h).astype(f32) for h in range(NH)]
    scale = HD ** (-0.5)

    def diagonal(both):
        return jnp.concatenate(
            [both[h * HD : (h + 1) * HD, h * TILE : (h + 1) * TILE] for h in range(NH)], axis=0
        )

    def split_heads(dst, j, whole, factor):
        for h in range(NH):
            one = (whole * (in_head[h] * factor)).astype(bf16)
            for i in range(NQ):
                dst[j, i, h * TILE : (h + 1) * TILE, :] = one[i * TILE : (i + 1) * TILE, :]

    def side_by_side(j):
        return jnp.concatenate([r.WQ[j, n * D : (n + 1) * D, :] for n in range(3)], axis=1)

    def project(j):
        bias = r.RBI[j]
        whole = dot(r.XB[...], side_by_side(j))
        split_heads(r.QM, j, whole[HALO:KR, 0:HC] + bias[1:2, 0:HC], scale)
        key = whole[:, HC : 2 * HC]
        r.KN[j] = key.astype(bf16)
        r.KT[j] = (key * scale).astype(bf16).T
        value = (whole[:, 2 * HC : 3 * HC] + bias[2:3, 0:HC]).astype(bf16)
        r.VN[j] = value
        r.VT[j] = value.T

    def attend(j):
        span = [slice(i * TILE, i * TILE + WIN) for i in range(NQ)]
        for some in (range(NQ),):
            scores = {i: dot_nt(r.KN[j, span[i], :], r.QM[j, i]) for i in some}
            for i in some:
                masked = scores[i] + jnp.concatenate([r.MB[i]] * NH, axis=1)
                top = jnp.maximum(jnp.max(masked, axis=0, keepdims=True), masked_fill)
                expo = jnp.exp(masked - top)
                total = jnp.maximum(jnp.sum(expo, axis=0, keepdims=True), 1.0)
                r.PS[j, i] = (expo * (1.0 / total)).astype(bf16)
            for i in some:
                context = diagonal(dot(r.VT[j, :, span[i]], r.PS[j, i])).astype(bf16)
                r.CXT[j, :, i * TILE : (i + 1) * TILE] = context
                r.CX[j, i * TILE : (i + 1) * TILE, :] = context.T

    load[0].wait()
    load[1].wait()
    load_w["qkv"].wait()
    project(z)
    attend(z)
    r.XT[...] = r.XB[HALO:KR, :].T
    r.S[0] = jnp.broadcast_to(
        jnp.sum(r.VAL[...].reshape(R // 8, 8, TILE), axis=0).sum(axis=0, keepdims=True), (8, TILE)
    )
    sum_core(0)
    gather(0, 1, "qkv")
    gather(0, 2, "qkv")
    gather(1, 1, "qkv")
    gather(0, 3, "qkv")
    gather(1, 2, "qkv")
    gather(0, 1, "up", "down")
    for which in (1, 2, 3):
        gather(0, which, "out")
    gather(1, 3, "qkv")
    gather(2, 1, "qkv")
    gather(2, 2, "qkv")
    for which in (1, 2, 3):
        gather(1, which, "out")
    for dz in z_offs:
        bias_copy(dz, z_from(dz)).wait_recv()
    sum_chips(0)

    def forward_step(t, c):
        j = z_from(t)
        gc_wait("qkv", t)
        project(j)
        attend(j)

        @pl.when(t == 1)
        def _():
            gather(2, 3, "qkv")
            gather(1, 1, "up", "down")

        @pl.when(t == 2)
        def _():
            gather(0, 2, "up", "down")
            for which in (1, 2, 3):
                gather(2, which, "out")

        return c

    lax.fori_loop(1, M, forward_step, 0)
    for g in ("out", "up", "down"):
        load_w[g].wait()
    for dz in z_offs:
        gc_wait("out", dz)

    attn = r.bias_out[...]
    for j in range(M):
        attn = attn + dot(r.CX[j], r.WO[j])
    r.ACC[...] = attn

    def moments(k):
        def body(at, s):
            v, valid = r.ACC[at, :], wide(r.VAL[at, :])
            vv = v * valid
            return s[0] + jnp.sum(vv, axis=0, keepdims=True), s[1] + jnp.sum(vv * v, axis=0, keepdims=True)

        zero = jnp.zeros((1, D), f32)
        s = chunks(body, (zero, zero))
        for n in range(2):
            for b in range(D // TILE):
                at = n * (D // TILE) + b
                r.S[k, at : at + 1, :] = s[n][:, b * TILE : (b + 1) * TILE]

    def unfold(total, n):
        return jnp.concatenate([total[n * (D // TILE) + b :][:1] for b in range(D // TILE)], axis=1)

    def variance(total, count):
        col_mean = unfold(total, 0) / count
        return unfold(total, 1) / count - col_mean * col_mean

    moments(1)
    sum_core(1)
    gather(2, 1, "up", "down")
    gather(1, 2, "up", "down")
    sum_chips(1)
    gather(0, 3, "up", "down")
    count = sum_done(0)[0:1, 0:1]
    var_attn = variance(sum_done(1), count)
    omega_attn = jnp.sqrt(1.0 + var_attn)
    gather(1, 3, "up", "down")
    gain_one, shift_one = r.gain_one[...], r.shift_one[...]
    gain_two, shift_two = r.gain_two[...], r.shift_two[...]

    def normed(pre):
        centred = pre - jnp.mean(pre, axis=-1, keepdims=True)
        var = jnp.mean(centred * centred, axis=-1, keepdims=True)
        rstd = lax.rsqrt(var + norm_eps)
        return centred * rstd, rstd

    def norm_back(dy, n, rstd, gain):
        dn = dy * gain
        return rstd * (
            dn - jnp.mean(dn, axis=-1, keepdims=True) - n * jnp.mean(dn * n, axis=-1, keepdims=True)
        )

    def norm_one(c, s):
        at, xat = rows(c, CHUNK, CHUNK), rows(c + HALO // CHUNK, CHUNK, CHUNK)
        n, rstd = normed(r.XB[xat, :].astype(f32) * omega_attn + r.ACC[at, :])
        r.N1[at, :] = n
        r.RS[at, :] = jnp.broadcast_to(rstd, (CHUNK, TILE))
        r.HL[at, :] = (n * gain_one + shift_one).astype(bf16)
        return s

    lax.fori_loop(0, R // CHUNK, norm_one, 0, unroll=4)
    gather(2, 2, "up", "down")

    r.ACC[...] = jnp.broadcast_to(r.bias_down[...], (R, D))
    c0 = (2.0 / jnp.pi) ** 0.5

    parts = [slice(n * R // PARTS, (n + 1) * R // PARTS) for n in range(PARTS)]

    def ffn_step(t, c):
        j = z_from(t)

        @pl.when(t > 0)
        def _():
            gc_wait("up", t)
            gc_wait("down", t)

        for at in parts:
            u = dot(r.HL[at, :], r.WU[j]) + r.RBI[j, 0:1, 0:F]
            uu = u * u
            th = jnp.tanh(u * (c0 + (c0 * 0.044715) * uu))
            half = 0.5 + 0.5 * th
            r.AC[j, at, :] = (u * half).astype(bf16)
            r.GP[j, at, :] = half + (0.5 * u) * (1.0 - th * th) * (c0 + (3.0 * 0.044715 * c0) * uu)
        r.ACC[...] += dot(r.AC[j], r.WD[j])

        @pl.when(t == 2)
        def _():
            gather(2, 3, "up", "down")

        return c

    lax.fori_loop(0, M, ffn_step, 0)

    moments(2)
    sum_core(2)
    r.HLT[...] = r.HL[...].T
    sum_chips(2)
    omega_ffn = jnp.sqrt(1.0 + var_attn + variance(sum_done(2), count))
    r.omega[...] = jnp.concatenate([omega_attn, omega_ffn, jnp.zeros((6, D), f32)], axis=0)
    load[2].wait()

    def norm_two(at, s):
        hidden = r.N1[at, :] * gain_one + shift_one
        n, rstd = normed(hidden * omega_ffn + r.ACC[at, :])
        r.GI[at, :] = n * gain_two + shift_two
        dy = r.CT[at, :].astype(f32)
        d_pre = norm_back(dy, n, rstd, gain_two)
        low = d_pre.astype(bf16)
        r.ACC[at, :] = omega_ffn * d_pre
        r.DF[at, :] = low
        return (
            s[0] + jnp.sum(low.astype(f32), axis=0, keepdims=True),
            s[1] + jnp.sum(dy * n, axis=0, keepdims=True),
            s[2] + jnp.sum(dy, axis=0, keepdims=True),
        )

    zero = jnp.zeros((1, D), f32)
    s = chunks(norm_two, (zero, zero, zero))
    r.V[...] = jnp.zeros(r.V.shape, f32)
    r.VB[...] = jnp.zeros(r.VB.shape, f32)
    for n in range(3):
        r.V[3 + n : 4 + n, :] = s[n]
    put_out = pltpu.make_async_copy(r.GI, r.layer_out, r.ls.at[11])
    put_out.start()


    shard = [z_from(t) for t in range(M)]

    def ffn_back(t, c):
        j = z_from(t)
        r.GD[j, 0:F, :] = dot(r.AC[j].T, r.DF[...]).astype(bf16)
        rc_start("down", j)
        total = jnp.zeros((1, F), f32)
        for at in parts:
            low = (dot_nt(r.DF[at, :], r.WD[j]) * r.GP[j, at, :]).astype(bf16)
            r.DI[at, :] = low
            total = total + jnp.sum(low.astype(f32), axis=0, keepdims=True)
        r.VB[j, 0:1, 0:F] = total
        r.GU[j, 0:D, :] = dot(r.HLT[...], r.DI[...]).astype(bf16)
        rc_start("up", j)
        r.ACC[...] += dot_nt(r.DI[...], r.WU[j])

        rp_start("down", j)

        @pl.when(t > 0)
        def _():
            rp_start("up", z_from(t - 1))

        @pl.when(t == 2)
        def _():
            mids("down", shard[0])

        return c

    lax.fori_loop(0, M, ffn_back, 0)

    put_out.wait()

    def back_one(at, s):
        dy = r.ACC[at, :]
        n = r.N1[at, :]
        d_pre = norm_back(dy, n, r.RS[at, 0:1], gain_one)
        low = d_pre.astype(bf16)
        r.DA[at, :] = low
        r.GI[at, :] = omega_attn * d_pre
        return (
            s[0] + jnp.sum(low.astype(f32), axis=0, keepdims=True),
            s[1] + jnp.sum(dy * n, axis=0, keepdims=True),
            s[2] + jnp.sum(dy, axis=0, keepdims=True),
        )

    s = chunks(back_one, (zero, zero, zero))
    for n in range(3):
        r.V[n : n + 1, :] = s[n]
    for j in range(M):
        r.V[6 + j : 7 + j, :] = r.VB[j, 0:1, :]
    vc().start()
    rp_start("up", shard[M - 1])
    mids("down", shard[1])
    mids("up", shard[0])

    def both(step, *a):
        step("down", *a)
        step("up", *a)

    def out_back(j, c):
        r.GO[j, 0:HC, :] = dot(r.CXT[j], r.DA[...]).astype(bf16)
        rc_start("out", j)
        split_heads(r.DCM, j, dot_nt(r.DA[...], r.WO[j]), 1.0)
        return c

    lax.fori_loop(0, M, out_back, 0)
    rz_start("down", shard[0])

    def attend_back(j, which):
        span = {i: slice(i * TILE, i * TILE + WIN) for i in which}
        d_probs = {i: dot_nt(r.VN[j, span[i], :], r.DCM[j, i]) for i in which}
        d_scores = {}
        for i in which:
            probs = r.PS[j, i].astype(f32)
            delta = jnp.sum(probs * d_probs[i], axis=0, keepdims=True)
            d_scores[i] = (probs * (d_probs[i] - delta)).astype(bf16)
        for i in which:
            d_query = diagonal(dot(r.KT[j, :, span[i]], d_scores[i])).astype(bf16)
            r.DL[j, 0, i * TILE : (i + 1) * TILE, :] = d_query.T
            r.DV[j, span[i], :] += dot(r.PS[j, i], r.DCM[j, i])
            r.DK[j, span[i], :] += dot(d_scores[i], r.QM[j, i])

    early = range(min(HALO // TILE, NQ))

    def attend_early(t, c):
        j = step_of(t)
        r.DK[j] = jnp.zeros((KR, HC), f32)
        r.DV[j] = jnp.zeros((KR, HC), f32)
        attend_back(j, early)
        r.HS[j, 0:HALO, :] = r.DK[j, 0:HALO, :].astype(bf16)
        r.HS[j, HALO : 2 * HALO, :] = r.DV[j, 0:HALO, :].astype(bf16)

        @pl.when(joined)
        def _():
            halo(j).start()

        @pl.when(t == 0)
        def _():
            vec_plane()

        @pl.when(t == 1)
        def _():
            mids("up", shard[1])
            mids("down", shard[2])

        @pl.when(t == 2)
        def _():
            rz_start("up", shard[0])

        @pl.when(t == 3)
        def _():
            vec_z()
            rz_start("down", shard[1])
            for_all("out", rp_start)

        return c

    def qkv_back(j):
        @pl.when(lax.rem((z + 1) * R, ROW) > 0)
        def _():
            halo(j).wait_recv()
            r.DK[j, R:KR, :] += r.HR[j, 0:HALO, :].astype(f32)
            r.DV[j, R:KR, :] += r.HR[j, HALO : 2 * HALO, :].astype(f32)

        r.DL[j, 1] = r.DK[j, HALO:KR, :].astype(bf16)
        r.DL[j, 2] = r.DV[j, HALO:KR, :].astype(bf16)
        two = [jnp.sum(r.DL[j, n].astype(f32), axis=0, keepdims=True) for n in (0, 2)]
        two = jnp.concatenate(two, axis=1)
        for n in range(2 * HC // TILE):
            r.VB[j, 1 + n : 2 + n, 0:TILE] = two[:, n * TILE : (n + 1) * TILE]
        whole = dot(r.XT[...], jnp.concatenate([r.DL[j, n] for n in range(3)], axis=1)).astype(bf16)
        for n in range(3):
            r.GQ[j, n * D : (n + 1) * D, :] = whole[:, n * HC : (n + 1) * HC]
        rc_start("qkv", j)

    def back_in(j, c):
        r.GI[...] += dot_nt(jnp.concatenate([r.DL[j, n] for n in range(3)], axis=1), side_by_side(j))
        return c

    def for_all(g, step):
        lax.fori_loop(0, M, lambda j, c: (step(g, j), c)[1], 0)

    lax.fori_loop(0, M, attend_early, 0)

    def attend_late(t, c):
        j = step_of(t)
        attend_back(j, range(len(early), NQ))
        qkv_back(j)

        @pl.when(t == 0)
        def _():
            mids("up", shard[2])
            for n in range(3, M):
                mids("down", shard[n])
            rz_start("up", shard[1])

        @pl.when(t == 1)
        def _():
            for n in range(3, M):
                mids("up", shard[n])
            rz_start("down", shard[2])
            for_all("out", mids)

        @pl.when(t == 2)
        def _():
            rz_start("up", shard[2])
            for n in range(3, M):
                rz_start("down", shard[n])

        @pl.when(t == 3)
        def _():
            for n in range(3, M):
                rz_start("up", shard[n])
            for_all("out", rz_start)

        @pl.when(t > 0)
        def _():
            rp_start("qkv", step_of(t - 1))

        @pl.when(t > 1)
        def _():
            mids("qkv", step_of(t - 2))

        @pl.when(t > 3)
        def _():
            rz_start("qkv", step_of(t - 4))

        return c

    lax.fori_loop(0, M, attend_late, 0)
    for j in range(M):
        for n in range(2 * HC // TILE):
            at = j * (2 * HC // TILE) + n
            r.S[3, at : at + 1, :] = r.VB[j, 1 + n : 2 + n, 0:TILE]
    sum_core(3)
    lax.fori_loop(0, 1, back_in, 0)
    rp_start("qkv", step_of(M - 1), True)
    rz_start("qkv", step_of(M - 4))
    sum_chips(3)
    mids("qkv", step_of(M - 2))
    lax.fori_loop(1, M, back_in, 0)
    put_in = pltpu.make_async_copy(r.GI, r.grad_layer_in, r.ls.at[12])
    put_in.start()
    rz_start("qkv", step_of(M - 3))
    ap_start("down")
    ap_start("up")
    rz_start("qkv", step_of(M - 2))
    rz_start("qkv", step_of(M - 1), True)
    ap_start("out")
    ac_start("down")
    ac_start("up")
    ac_start("out")
    total = vec_done()
    r.vectors[0:6, :] = total[0:6]
    for j in range(M):
        r.VB[j, 0:1, :] = total[6 + j : 7 + j]
    total = sum_done(3)
    for j in range(M):
        for n in range(2 * HC // TILE):
            at = j * (2 * HC // TILE) + n
            r.VB[j, 1 + n : 2 + n, 0:TILE] = total[at : at + 1]
    r.vectors[6:7, :] = r.VB[z, 0:1, :]
    r.vectors[7:8, :] = jnp.zeros((1, D), f32)
    for n in range(2 * HC // TILE):
        r.vectors[7:8, n * TILE : (n + 1) * TILE] = r.VB[z, 1 + n : 2 + n, 0:TILE]
    for g in ("down", "up", "out"):
        ac_wait(g)
    ap_start("qkv")
    ac_start("qkv")
    ac_wait("qkv")

    for g in group:
        g_sent(g)
        r_sent(g)
    for dz in z_offs:
        bias_copy(dz, z).wait_send()
    for k in range(4):
        sum_sent(k)
    vec_sent()

    @pl.when(joined)
    def _():
        lax.fori_loop(0, M, lambda j, c: (halo(j).wait_send(), c)[1], 0)

    put_in.wait()


def shards(
    layer_in,
    cotangent,
    w_qkv,
    bias_qv,
    w_out,
    bias_out,
    gain_one,
    shift_one,
    w_up,
    bias_up,
    w_down,
    bias_down,
    gain_two,
    shift_two,
    segment_ids,
    key_mask,
):
    M, NDP = lax.axis_size("mp"), lax.axis_size("dp")
    D = layer_in.shape[1]
    HC, F, ROW = w_qkv.shape[2], w_up.shape[1], segment_ids.shape[1]
    R = layer_in.shape[0] // M
    NP, NH, NQ, KR, WIN = NDP // CORES, HC // HD, R // TILE, R + HALO, HALO + TILE
    little = ("bias_qv", "bias_up", "segment_ids", "key_mask", "bias_out")
    little += ("gain_one", "shift_one", "bias_down", "gain_two", "shift_two")
    sz = types.SimpleNamespace(little=little, M=M, NP=NP, R=R, ROW=ROW, HC=HC, F=F, D=D, W=max(F, HC))

    hbm, vmem = pl.BlockSpec(memory_space=pl.ANY), pl.BlockSpec(memory_space=pltpu.VMEM)
    ins = dict(
        layer_in=(layer_in, hbm),
        cotangent=(cotangent, hbm),
        w_qkv=(w_qkv.reshape(3 * D, HC), hbm),
        w_out=(w_out, hbm),
        w_up=(w_up, hbm),
        w_down=(w_down, hbm),
        bias_qv_in=(bias_qv, hbm),
        bias_up_in=(bias_up[None], hbm),
        bias_out_in=(bias_out[None], hbm),
        gain_one_in=(gain_one[None], hbm),
        shift_one_in=(shift_one[None], hbm),
        bias_down_in=(bias_down[None], hbm),
        gain_two_in=(gain_two[None], hbm),
        shift_two_in=(shift_two[None], hbm),
        segment_ids_in=(segment_ids, hbm),
        key_mask_in=(key_mask, hbm),
    )
    outs = dict(
        omega=((8, D), f32, vmem),
        layer_out=((R, D), f32, hbm),
        grad_layer_in=((R, D), f32, hbm),
        grad_w_qkv=((3 * D, HC), bf16, hbm),
        grad_w_out=((HC, D), bf16, hbm),
        grad_w_up=((D, F), bf16, hbm),
        grad_w_down=((F, D), bf16, hbm),
        vectors=((8, D), f32, vmem),
    )
    scratch = {
        name[:-3]: (value.shape, value.dtype) for name, (value, _) in ins.items() if name.endswith("_in")
    }
    scratch |= dict(
        XB=((KR, D), bf16),
        XT=((D, R), bf16),
        CT=((R, D), bf16),
        WQ=((M, 3 * D, HC), bf16),
        WO=((M, HC, D), bf16),
        WU=((M, D, F), bf16),
        WD=((M, F, D), bf16),
        SB=((8, sz.W), f32),
        RBI=((M, 8, sz.W), f32),
        QM=((M, NQ, NH * TILE, HC), bf16),
        KN=((M, KR, HC), bf16),
        KT=((M, HC, KR), bf16),
        VN=((M, KR, HC), bf16),
        VT=((M, HC, KR), bf16),
        PS=((M, NQ, WIN, NH * TILE), bf16),
        CX=((M, R, HC), bf16),
        CXT=((M, HC, R), bf16),
        DCM=((M, NQ, NH * TILE, HC), bf16),
        MB=((NQ, WIN, TILE), f32),
        VAL=((R, TILE), f32),
        ACC=((R, D), f32),
        N1=((R, D), f32),
        RS=((R, TILE), f32),
        HL=((R, D), bf16),
        HLT=((D, R), bf16),
        AC=((M, R, F), bf16),
        GP=((M, R, F), f32),
        DF=((R, D), bf16),
        DI=((R, F), bf16),
        DA=((R, D), bf16),
        GI=((R, D), f32),
        DK=((M, KR, HC), f32),
        DV=((M, KR, HC), f32),
        DL=((M, 3, R, HC), bf16),
        HS=((M, 2 * HALO, HC), bf16),
        HR=((M, 2 * HALO, HC), bf16),
        VB=((M, 8, D), f32),
    )
    for tag, shape in (("Q", (3 * D, HC)), ("O", (HC, D)), ("U", (D, F)), ("D", (F, D))):
        pr = -(-shape[0] // (NDP * PACK)) * PACK
        scratch["G" + tag] = ((M, pr * NDP, shape[1]), bf16)
        scratch["RA" + tag] = ((M, pr * NP, shape[1]), bf16)
        scratch["RB" + tag] = ((NP - 1, M, pr, shape[1]), bf16)
        scratch["QB" + tag] = ((M, pr, shape[1]), bf16)
        scratch["RC" + tag] = ((M - 1, pr, shape[1]), bf16)
        scratch["O" + tag] = ((pr * NDP, shape[1]), bf16)
    vec_rows = -(-(6 + M) // 8) * 8
    scratch["V"] = scratch["Vc"] = ((vec_rows, D), f32)
    scratch["Vp"] = ((NP, vec_rows, D), f32)
    scratch["Vz"] = ((M, vec_rows, D), f32)
    scratch["S"] = scratch["Sc"] = ((4, 8, TILE), f32)
    scratch["Sa"] = ((4, NP * M, 8, TILE), f32)
    halves = 2 if any(-(-n // (NDP * PACK)) % 2 == 0 for n in (3 * D, D, F)) else 1
    sems = dict(
        ls=(13,),
        bs=(10,),
        gzs=(4, M - 1),
        gzr=(4, M - 1),
        gps=(4, halves, NP - 1, M - 1),
        gpr=(4, halves, NP - 1, M - 1),
        gcs=(4, M - 1),
        gcr=(4, M - 1),
        bzs=(M - 1,),
        bzr=(M - 1,),
        rcs=(4, M),
        rcr=(4, M),
        rps=(4, halves, NP - 1, M),
        rpr=(4, halves, NP - 1, M),
        rzs=(4, M - 1),
        rzr=(4, M - 1),
        aps=(4, NP - 1),
        apr=(4, NP - 1),
        acs=(4,),
        acr=(4,),
        scs=(4,),
        scr=(4,),
        sas=(4, NP * M - 1),
        sar=(4, NP * M - 1),
        vs=(NP - 1 + M,),
        vr=(NP - 1 + M,),
        hss=(M,),
        hsr=(M,),
    )
    names = list(ins) + list(outs) + list(scratch) + list(sems)
    got = pl.pallas_call(
        functools.partial(layer_kernel, sz, names),
        out_shape=[jax.ShapeDtypeStruct(s, t) for s, t, _ in outs.values()],
        in_specs=[spec for _, spec in ins.values()],
        out_specs=[spec for _, _, spec in outs.values()],
        scratch_shapes=[pltpu.VMEM(s, t) for s, t in scratch.values()]
        + [pltpu.SemaphoreType.DMA(s) for s in sems.values()],
        compiler_params=pltpu.CompilerParams(
            collective_id=0, has_side_effects=True, vmem_limit_bytes=62 << 20
        ),
    )(*[value for value, _ in ins.values()])
    shapes = [(2, D), (R, D), (R, D), (3 * D, HC), (2, HC), (HC, D)] + [(1, D)] * 3
    shapes += [(D, F), (1, F), (F, D)] + [(1, D)] * 3
    big = (1, 2, 3, 5, 9, 11)
    done = list(pl.pallas_call(
        functools.partial(result_kernel, HC, F),
        out_shape=[jax.ShapeDtypeStruct(s, f32) for s in shapes],
        in_specs=[vmem if n in ("omega", "vectors") else hbm for n in outs],
        out_specs=[hbm if n in big else vmem for n in range(len(shapes))],
        scratch_shapes=[
            pltpu.VMEM(shape, t)
            for n in (1, 2, 3, 9, 11, 5)
            for shape, t in ((shapes[n], f32 if n < 3 else bf16), ((8, TILE) if n < 3 else shapes[n], f32))
        ]
        + [pltpu.SemaphoreType.DMA((12,))],
    )(*got))
    done[3] = done[3].reshape(3, D, HC)
    return tuple(v[0] if v.shape[0] == 1 else v for v in done)


def result_kernel(HC, F, *refs):
    omega, layer_out, grad_in, g_qkv, g_out, g_up, g_down, vectors = refs[:8]
    out, held, sem = refs[8:23], refs[23:-1], refs[-1]
    reads, writes = [], []
    pairs = ((layer_out, 1), (grad_in, 2), (g_qkv, 3), (g_up, 9), (g_down, 11), (g_out, 5))
    for n, (src, at) in enumerate(pairs):
        low, high = held[2 * n], held[2 * n + 1]
        reads.append(pltpu.make_async_copy(src, low, sem.at[n]))
        writes.append(pltpu.make_async_copy(low if n < 2 else high, out[at], sem.at[len(pairs) + n]))
        reads[n].start()
    out[0][...] = omega[0:2, :]
    out[4][0:1, :] = vectors[7:8, 0:HC]
    out[4][1:2, :] = vectors[7:8, HC : 2 * HC]
    out[10][...] = vectors[6:7, 0:F]
    for n, at in enumerate((6, 7, 8, 12, 13, 14)):
        out[at][...] = vectors[n : n + 1, :]
    for n in range(len(pairs)):
        reads[n].wait()
        if n >= 2:
            held[2 * n + 1][...] = held[2 * n][...].astype(f32)
        writes[n].start()
    for copy in writes:
        copy.wait()


def solution(mesh):
    in_specs = (
        P("dp", None),
        P("dp", None),
        P(None, None, "mp"),
        P(None, "mp"),
        P("mp", None),
        P(),
        P(),
        P(),
        P(None, "mp"),
        P("mp"),
        P("mp", None),
        P(),
        P(),
        P(),
        P("dp", None),
        P("dp", None),
    )
    out_specs = (
        P(),
        P(("dp", "mp"), None),
        P(("dp", "mp"), None),
        P(None, None, "mp"),
        P(None, "mp"),
        P("mp", None),
        P(),
        P(),
        P(),
        P(None, "mp"),
        P("mp"),
        P("mp", None),
        P(),
        P(),
        P(),
    )
    return jax.shard_map(shards, mesh=mesh, in_specs=in_specs, out_specs=out_specs, check_vma=False)
```

```python
import functools
import types

import jax
import jax.numpy as jnp
from jax import lax
from jax.experimental import pallas as pl
from jax.experimental.pallas import tpu as pltpu
from jax.sharding import PartitionSpec as P

HD = 64
LONGEST = 250
TILE = 128
HALO = -(-LONGEST // TILE) * TILE
CHUNK = 64
PARTS = 2
PACK = 16
CORES = 2

norm_eps = 1e-05
masked_fill = -1000000000.0
shut = -1e30
MESH = pl.DeviceIdType.MESH
f32 = jnp.float32
bf16 = jnp.bfloat16


def dot(a, b):
    return lax.dot_general(a, b, (((1,), (0,)), ((), ())), preferred_element_type=f32)


def dot_nt(a, b):
    return lax.dot_general(a, b, (((1,), (1,)), ((), ())), preferred_element_type=f32)


def layer_kernel(sz, names, *refs):
    r = types.SimpleNamespace(**dict(zip(names, refs)))
    M, NP, R, ROW, HC, F, D = sz.M, sz.NP, sz.R, sz.ROW, sz.HC, sz.F, sz.D
    NDP = NP * CORES
    NH, NQ, KR, WIN = HC // HD, R // TILE, R + HALO, HALO + TILE
    dp, z = lax.axis_index("dp"), lax.axis_index("mp")
    core, plane = lax.rem(dp, CORES), lax.div(dp, CORES)
    piece = core * NP + plane
    partner = (plane * CORES + 1 - core, z)

    def plane_to(off):
        return (lax.rem(plane + off, NP) * CORES + core, z)

    def plane_from(off):
        return lax.rem(plane + NP - off, NP)

    def flipped(at, mask, count):
        for b in range(count.bit_length() - 1):
            if mask >> b & 1:
                at = at + (1 - 2 * lax.rem(lax.div(at, 1 << b), 2)) * (1 << b)
        return at

    def z_from(dz):
        if isinstance(dz, int):
            return flipped(z, dz, M)
        return sum(
            (lax.rem(lax.div(z, 1 << b) + lax.div(dz, 1 << b), 2)) * (1 << b) for b in range(M.bit_length() - 1)
        )

    def z_apart(j):
        return z_from(j)

    def z_to(dz):
        return (dp, z_from(dz))

    def chip_to(n):
        return (lax.rem(plane + n // M, NP) * CORES + core, lax.rem(z + n % M, M))

    plane_offs, z_offs = range(1, NP), range(1, M)
    bits = NP.bit_length() - 1

    def flip(mask):
        return flipped(plane, mask, NP)

    def flip_to(mask):
        return (flip(mask) * CORES + core, z)

    orders = (tuple(range(bits)), tuple(reversed(range(bits))))

    def subsets(some):
        masks = [0]
        for b in some:
            masks = masks + [m | 1 << b for m in masks]
        return masks

    def rcopy(src, dst, send, recv, dev):
        return pltpu.make_async_remote_copy(
            src_ref=src, dst_ref=dst, send_sem=send, recv_sem=recv, device_id=dev, device_id_type=MESH
        )

    def rows(at, count, unit):
        return pl.ds(pl.multiple_of(at * unit, unit), count)

    bar = pltpu.get_barrier_semaphore()
    peers = [partner] + [chip_to(n) for n in range(1, NP * M)]
    for peer in peers:
        pl.semaphore_signal(bar, inc=1, device_id=peer, device_id_type=MESH)

    w_in = dict(qkv=r.w_qkv, out=r.w_out, up=r.w_up, down=r.w_down)
    w_all = dict(qkv=r.WQ, out=r.WO, up=r.WU, down=r.WD)
    group = ("qkv", "out", "up", "down")
    load = [
        pltpu.make_async_copy(r.layer_in.at[rows(z, R, R)], r.XB.at[pl.ds(HALO, R)], r.ls.at[0]),
        pltpu.make_async_copy(
            r.layer_in.at[rows(lax.rem(z * (R // TILE) + (M * R - HALO) // TILE, M * R // TILE), HALO, TILE)],
            r.XB.at[pl.ds(0, HALO)],
            r.ls.at[1],
        ),
        pltpu.make_async_copy(r.cotangent.at[rows(z, R, R)], r.CT, r.ls.at[2]),
    ]
    load_w = {
        g: pltpu.make_async_copy(w_in[g], w_all[g].at[z], r.ls.at[3 + n]) for n, g in enumerate(group)
    }
    little = {
        name: pltpu.make_async_copy(getattr(r, name + "_in"), getattr(r, name), r.bs.at[n])
        for n, name in enumerate(sz.little)
    }
    for name in sz.little:
        little[name].start()
    load[0].start()
    load[1].start()
    for g in group:
        load_w[g].start()
    load[2].start()

    pl.semaphore_wait(bar, len(peers))

    def g_split(g):
        return w_in[g].shape[0] % (NDP * PACK) == 0

    def gz(g, dz, zs):
        n = group.index(g)
        if not g_split(g):
            src, dst = w_in[g], w_all[g].at[zs]
        else:
            pr = w_in[g].shape[0] // NDP
            src, dst = w_in[g].at[rows(piece, pr, pr)], w_all[g].at[zs, rows(piece, pr, pr)]
        return rcopy(src, dst, r.gzs.at[n, dz - 1], r.gzr.at[n, dz - 1], z_to(dz))

    def g_halves(g):
        return 2 if w_in[g].shape[0] // NDP % (2 * PACK) == 0 else 1

    def gp(g, h, s, m, dz, there):
        n, hp = group.index(g), w_in[g].shape[0] // NDP // g_halves(g)
        order = orders[h]
        have = subsets(order[:s])[m] ^ (there << order[s])
        part = w_all[g].at[z_from(dz), rows((core * NP + flip(have)) * g_halves(g) + h, hp, hp)]
        at = (n, h, (1 << s) - 1 + m, dz - 1)
        return rcopy(part, part, r.gps.at[at], r.gpr.at[at], flip_to(1 << order[s]))

    straight = ("qkv", "out")

    def gd(g, off, dz, at_plane):
        n, pr = group.index(g), w_in[g].shape[0] // NDP
        part = w_all[g].at[z_from(dz), rows(core * NP + at_plane, pr, pr)]
        at = (n, 0, off - 1, dz - 1)
        return rcopy(part, part, r.gps.at[at], r.gpr.at[at], plane_to(off))

    def gc(g, dz, at_core):
        n, half = group.index(g), w_in[g].shape[0] // CORES
        part = w_all[g].at[z_from(dz), rows(at_core, half, half)]
        return rcopy(part, part, r.gcs.at[n, dz - 1], r.gcr.at[n, dz - 1], partner)

    def gz_start(g):
        for dz in z_offs:
            gz(g, dz, z).start()

    def gp_all(g, s):
        return [(h, m) for h in range(g_halves(g)) for m in range(1 << s)]

    def gp_start(g, s, dzs):
        for dz in dzs:
            if s == 0:
                gz(g, dz, z_from(dz)).wait_recv()
            if not g_split(g):
                continue
            if g in straight:
                if s == 0:
                    for off in plane_offs:
                        gd(g, off, dz, plane).start()
                if s == bits:
                    for off in plane_offs:
                        gd(g, off, dz, plane_from(off)).wait_recv()
                    gc(g, dz, core).start()
                continue
            if s > 0:
                for h, m in gp_all(g, s - 1):
                    gp(g, h, s - 1, m, dz, 1).wait_recv()
            if s < bits:
                for h, m in gp_all(g, s):
                    gp(g, h, s, m, dz, 0).start()
            else:
                gc(g, dz, core).start()

    near = [tuple(z_offs[0:1]), tuple(z_offs[1:2]), tuple(z_offs[2:])]

    def gather(phase, which, *groups):
        for dz in near[which - 1]:
            for s in ((0,), range(1, bits), (bits,))[phase]:
                for g in groups:
                    gp_start(g, s, (dz,))

    def gc_wait(g, dz):
        if g_split(g):
            gc(g, dz, 1 - core).wait_recv()

    def g_sent(g):
        for dz in z_offs:
            gz(g, dz, z).wait_send()
            if g_split(g):
                if g in straight:
                    for off in plane_offs:
                        gd(g, off, dz, plane).wait_send()
                else:
                    for s in range(bits):
                        for h, m in gp_all(g, s):
                            gp(g, h, s, m, dz, 0).wait_send()
                gc(g, dz, core).wait_send()

    def bias_copy(dz, zs):
        return rcopy(r.SB, r.RBI.at[zs], r.bzs.at[dz - 1], r.bzr.at[dz - 1], z_to(dz))

    g_part = dict(qkv=r.GQ, out=r.GO, up=r.GU, down=r.GD)
    g_ra = dict(qkv=r.RAQ, out=r.RAO, up=r.RAU, down=r.RAD)
    g_rb = dict(qkv=r.RBQ, out=r.RBO, up=r.RBU, down=r.RBD)
    g_qb = dict(qkv=r.QBQ, out=r.QBO, up=r.QBU, down=r.QBD)
    g_rc = dict(qkv=r.RCQ, out=r.RCO, up=r.RCU, down=r.RCD)
    g_out = dict(qkv=r.OQ, out=r.OO, up=r.OU, down=r.OD)
    g_res = dict(qkv=r.grad_w_qkv, out=r.grad_w_out, up=r.grad_w_up, down=r.grad_w_down)

    def pr_of(g):
        return g_part[g].shape[1] // NDP

    def rc(g, j):
        n, half = group.index(g), pr_of(g) * NP
        return rcopy(
            g_part[g].at[j, rows(1 - core, half, half)], g_ra[g].at[j], r.rcs.at[n, j], r.rcr.at[n, j], partner
        )

    def r_halves(g):
        return 2 if pr_of(g) % (2 * PACK) == 0 else 1

    def rp(g, off, j):
        n, pr = group.index(g), pr_of(g)
        at = core * NP + lax.rem(plane + off, NP)
        return rcopy(
            g_part[g].at[j, rows(at, pr, pr)],
            g_rb[g].at[off - 1, j],
            r.rps.at[n, 0, off - 1, j],
            r.rpr.at[n, 0, off - 1, j],
            plane_to(off),
        )

    def r_rows(g, h, mask):
        hp = pr_of(g) // r_halves(g)
        return rows((core * NP + flip(mask)) * r_halves(g) + h, hp, hp)

    def r_slot(g, h, s, m):
        hp = pr_of(g) // r_halves(g)
        return NP - (1 << (bits - s)) + m, pl.ds(h * hp, hp)

    def rh(g, h, s, m, j):
        n, order = group.index(g), orders[h]
        slot, half = r_slot(g, h, s, m)
        away = subsets(order[s + 1 :])[m] | 1 << order[s]
        return rcopy(
            g_part[g].at[j, r_rows(g, h, away)],
            g_rb[g].at[slot, j, half],
            r.rps.at[n, h, slot, j],
            r.rpr.at[n, h, slot, j],
            flip_to(1 << order[s]),
        )

    def rh_all(g, s):
        return [(h, m) for h in range(r_halves(g)) for m in range(1 << (bits - 1 - s))]

    def rz(g, j, dz):
        n = group.index(g)
        return rcopy(g_qb[g].at[j], g_rc[g].at[dz - 1], r.rzs.at[n, dz - 1], r.rzr.at[n, dz - 1], (dp, j))

    def ap(g, off, at_plane):
        n, pr = group.index(g), pr_of(g)
        part = g_out[g].at[rows(core * NP + at_plane, pr, pr)]
        return rcopy(part, part, r.aps.at[n, off - 1], r.apr.at[n, off - 1], plane_to(off))

    def ac(g, at_core):
        n, half = group.index(g), pr_of(g) * NP
        part = g_out[g].at[rows(at_core, half, half)]
        into = g_res[g].at[rows(at_core, half, half)] if unpadded(g) else part
        return rcopy(part, into, r.acs.at[n], r.acr.at[n], partner)

    def rc_start(g, j):
        rc(g, j).start()

    def rp_start(g, j, direct=False):
        rc(g, j).wait_recv()
        half = pr_of(g) * NP
        mine = rows(core, half, half)
        g_part[g][j, mine] = (g_part[g][j, mine].astype(f32) + g_ra[g][j].astype(f32)).astype(bf16)
        if direct:
            for off in plane_offs:
                rp(g, off, j).start()
        else:
            for h, m in rh_all(g, 0):
                rh(g, h, 0, m, j).start()

    def rp_step(g, j, s):
        for h, m in rh_all(g, s - 1):
            rh(g, h, s - 1, m, j).wait_recv()
            slot, half = r_slot(g, h, s - 1, m)
            at = r_rows(g, h, subsets(orders[h][s:])[m])
            g_part[g][j, at] = (g_part[g][j, at].astype(f32) + g_rb[g][slot, j, half].astype(f32)).astype(bf16)
        for h, m in rh_all(g, s):
            rh(g, h, s, m, j).start()

    def mids(g, j):
        for s in range(1, bits):
            rp_step(g, j, s)

    def rz_start(g, j, direct=False):
        pr = pr_of(g)
        total = g_part[g][j, rows(piece, pr, pr)].astype(f32)
        if direct:
            for off in plane_offs:
                rp(g, off, j).wait_recv()
                total = total + g_rb[g][off - 1, j].astype(f32)
        else:
            for h, m in rh_all(g, bits - 1):
                rh(g, h, bits - 1, m, j).wait_recv()
            total = total + g_rb[g][NP - 2, j].astype(f32)
        g_qb[g][j] = total.astype(bf16)

        @pl.when(j != z)
        def _():
            rz(g, j, z_apart(j)).start()

    def ap_start(g):
        pr = pr_of(g)
        total = g_qb[g][z].astype(f32)
        for dz in z_offs:
            rz(g, z, dz).wait_recv()
            total = total + g_rc[g][dz - 1].astype(f32)
        g_out[g][rows(piece, pr, pr)] = total.astype(bf16)
        for off in plane_offs:
            ap(g, off, plane).start()

    def ac_start(g):
        for off in plane_offs:
            ap(g, off, plane_from(off)).wait_recv()
        ac(g, core).start()
        if unpadded(g):
            result(g).start()

    def unpadded(g):
        return g_res[g].shape[0] == g_out[g].shape[0]

    def result(g):
        n, half = group.index(g), pr_of(g) * NP
        if unpadded(g):
            mine = rows(core, half, half)
            return pltpu.make_async_copy(g_out[g].at[mine], g_res[g].at[mine], r.ls.at[7 + n])
        got = g_out[g].at[pl.ds(0, g_res[g].shape[0])]
        return pltpu.make_async_copy(got, g_res[g], r.ls.at[7 + n])

    def ac_wait(g):
        ac(g, 1 - core).wait_recv()
        if not unpadded(g):
            result(g).start()

    def r_sent(g):
        def one(j, c):
            rc(g, j).wait_send()
            for s in range(bits):
                for h, m in rh_all(g, s):
                    rh(g, h, s, m, j).wait_send()
            return c

        def direct(j, c):
            rc(g, j).wait_send()
            for off in plane_offs:
                rp(g, off, j).wait_send()
            return c

        if g == "qkv":
            lax.fori_loop(0, M - 1, lambda t, c: one(step_of(t), c), 0)
            direct(step_of(M - 1), 0)
        else:
            lax.fori_loop(0, M, one, 0)
        for dz in z_offs:
            rz(g, z_from(dz), dz).wait_send()
        for off in plane_offs:
            ap(g, off, plane).wait_send()
        ac(g, core).wait_send()
        result(g).wait()

    def sc(k):
        return rcopy(r.S.at[k], r.Sc.at[k], r.scs.at[k], r.scr.at[k], partner)

    def sa(k, n, there):
        if there:
            at = lax.rem(plane + NP - n // M, NP) * M + lax.rem(z + M - n % M, M)
        else:
            at = plane * M + z
        return rcopy(r.Sa.at[k, at], r.Sa.at[k, at], r.sas.at[k, n - 1], r.sar.at[k, n - 1], chip_to(n))

    def sum_core(k):
        sc(k).start()

    def sum_chips(k):
        sc(k).wait_recv()
        r.Sa[k, plane * M + z] = r.S[k] + r.Sc[k]
        for n in reversed(range(1, NP * M)):
            sa(k, n, False).start()

    def sum_done(k):
        for n in range(1, NP * M):
            sa(k, n, True).wait_recv()
        total = r.Sa[k, 0]
        for n in range(1, NP * M):
            total = total + r.Sa[k, n]
        return total

    def sum_sent(k):
        sc(k).wait_send()
        for n in range(1, NP * M):
            sa(k, n, False).wait_send()

    def vc():
        return rcopy(r.V, r.Vc, r.vs.at[0], r.vr.at[0], partner)

    def vp(off, at):
        return rcopy(r.Vp.at[at], r.Vp.at[at], r.vs.at[off], r.vr.at[off], plane_to(off))

    def vz(dz, at):
        return rcopy(r.Vz.at[at], r.Vz.at[at], r.vs.at[NP - 1 + dz], r.vr.at[NP - 1 + dz], z_to(dz))

    def vec_plane():
        vc().wait_recv()
        r.Vp[plane] = r.V[...] + r.Vc[...]
        for off in plane_offs:
            vp(off, plane).start()

    def vec_z():
        for off in plane_offs:
            vp(off, plane_from(off)).wait_recv()
        total = r.Vp[0]
        for s in plane_offs:
            total = total + r.Vp[s]
        r.Vz[z] = total
        for dz in z_offs:
            vz(dz, z).start()

    def vec_done():
        for dz in z_offs:
            vz(dz, z_from(dz)).wait_recv()
        total = r.Vz[0]
        for s in z_offs:
            total = total + r.Vz[s]
        return total

    def vec_sent():
        vc().wait_send()
        for off in plane_offs:
            vp(off, plane).wait_send()
        for dz in z_offs:
            vz(dz, z).wait_send()

    def halo(j):
        return rcopy(r.HS.at[j], r.HR.at[j], r.hss.at[j], r.hsr.at[j], (dp, lax.rem(z + M - 1, M)))

    sharing = max(ROW // R, 1)
    first_shard = lax.rem((lax.div(z, sharing) + 1) * sharing, M)

    def step_of(t):
        return lax.rem(first_shard + t, M)

    joined = lax.rem(z * R, ROW) > 0

    def chunks(body, init=0):
        return lax.fori_loop(0, R // CHUNK, lambda c, s: body(rows(c, CHUNK, CHUNK), s), init, unroll=4)

    def wide(cols):
        return jnp.concatenate([cols] * (D // TILE), axis=1)

    gz_start("qkv")
    little["bias_up"].wait()
    little["bias_qv"].wait()
    r.SB[...] = jnp.zeros((8, sz.W), f32)
    r.SB[0:1, 0:F] = r.bias_up[...]
    r.SB[1:3, 0:HC] = r.bias_qv[...]
    r.RBI[z] = r.SB[...]
    for dz in z_offs:
        bias_copy(dz, z).start()
    gz_start("out")
    for dz in z_offs:
        gz("up", dz, z).start()
        gz("down", dz, z).start()

    for name in sz.little[2:]:
        little[name].wait()
    unit = M * R // TILE
    marks = []
    for b in range(KR // TILE):
        at = lax.rem(z * NQ + (b - HALO // TILE) + unit, unit)
        packed, col = lax.div(at, ROW // TILE), lax.rem(at, ROW // TILE)
        spot = rows(col, TILE, TILE)
        sent, present = r.segment_ids[0:1, spot], r.key_mask[0:1, spot]
        for p in range(1, r.segment_ids.shape[0]):
            sent = jnp.where(packed == p, r.segment_ids[p : p + 1, spot] + p * ROW, sent)
            present = jnp.where(packed == p, r.key_mask[p : p + 1, spot], present)
        sent, present = sent.astype(f32), present.astype(f32)
        keyed = jnp.where(present > 0.5, sent, -1.0)
        if b < HALO // TILE:
            keyed = jnp.where(z > 0, keyed, -1.0)
        else:
            own = b - HALO // TILE
            r.VAL[own * TILE : (own + 1) * TILE, :] = jnp.broadcast_to(present, (TILE, TILE)).T
        marks.append((sent, jnp.broadcast_to(keyed, (TILE, TILE)).T))
    key_pos = lax.broadcasted_iota(jnp.int32, (TILE, TILE), 0)
    query_pos = lax.broadcasted_iota(jnp.int32, (TILE, TILE), 1)
    for i in range(NQ):
        asker = marks[i + HALO // TILE][0]
        for b in range(WIN // TILE):
            allowed = marks[i + b][1] == asker
            if b == WIN // TILE - 1:
                allowed = allowed & (key_pos <= query_pos)
            r.MB[i, b * TILE : (b + 1) * TILE, :] = jnp.where(allowed, 0.0, shut)

    head_of = lax.broadcasted_iota(jnp.int32, (1, HC), 1) // HD
    in_head = [(head_of == h).astype(f32) for h in range(NH)]
    scale = HD ** (-0.5)

    def diagonal(both):
        return jnp.concatenate(
            [both[h * HD : (h + 1) * HD, h * TILE : (h + 1) * TILE] for h in range(NH)], axis=0
        )

    def split_heads(dst, j, whole, factor):
        for h in range(NH):
            one = (whole * (in_head[h] * factor)).astype(bf16)
            for i in range(NQ):
                dst[j, i, h * TILE : (h + 1) * TILE, :] = one[i * TILE : (i + 1) * TILE, :]

    def side_by_side(j):
        return jnp.concatenate([r.WQ[j, n * D : (n + 1) * D, :] for n in range(3)], axis=1)

    def project(j):
        bias = r.RBI[j]
        whole = dot(r.XB[...], side_by_side(j))
        split_heads(r.QM, j, whole[HALO:KR, 0:HC] + bias[1:2, 0:HC], scale)
        key = whole[:, HC : 2 * HC]
        r.KN[j] = key.astype(bf16)
        r.KT[j] = (key * scale).astype(bf16).T
        value = (whole[:, 2 * HC : 3 * HC] + bias[2:3, 0:HC]).astype(bf16)
        r.VN[j] = value
        r.VT[j] = value.T

    def attend(j):
        span = [slice(i * TILE, i * TILE + WIN) for i in range(NQ)]
        for some in (range(NQ),):
            scores = {i: dot_nt(r.KN[j, span[i], :], r.QM[j, i]) for i in some}
            for i in some:
                masked = scores[i] + jnp.concatenate([r.MB[i]] * NH, axis=1)
                top = jnp.maximum(jnp.max(masked, axis=0, keepdims=True), masked_fill)
                expo = jnp.exp(masked - top)
                total = jnp.maximum(jnp.sum(expo, axis=0, keepdims=True), 1.0)
                r.PS[j, i] = (expo * (1.0 / total)).astype(bf16)
            for i in some:
                context = diagonal(dot(r.VT[j, :, span[i]], r.PS[j, i])).astype(bf16)
                r.CXT[j, :, i * TILE : (i + 1) * TILE] = context
                r.CX[j, i * TILE : (i + 1) * TILE, :] = context.T

    load[0].wait()
    load[1].wait()
    load_w["qkv"].wait()
    project(z)
    attend(z)
    r.XT[...] = r.XB[HALO:KR, :].T
    r.S[0] = jnp.broadcast_to(
        jnp.sum(r.VAL[...].reshape(R // 8, 8, TILE), axis=0).sum(axis=0, keepdims=True), (8, TILE)
    )
    sum_core(0)
    gather(0, 1, "qkv")
    gather(0, 2, "qkv")
    gather(0, 3, "qkv")
    gather(2, 1, "qkv")
    gather(2, 2, "qkv")
    for which in (1, 2, 3):
        gather(0, which, "out")
    gather(0, 1, "up", "down")
    for dz in z_offs:
        bias_copy(dz, z_from(dz)).wait_recv()
    sum_chips(0)

    def forward_step(t, c):
        j = z_from(t)
        gc_wait("qkv", t)
        project(j)
        attend(j)

        @pl.when(t == 1)
        def _():
            gather(2, 3, "qkv")

        @pl.when(t == 2)
        def _():
            for which in (1, 2, 3):
                gather(2, which, "out")
            gather(1, 1, "up", "down")

        @pl.when(t == 3)
        def _():
            gather(0, 2, "up", "down")

        return c

    lax.fori_loop(1, M, forward_step, 0)
    for g in ("out", "up", "down"):
        load_w[g].wait()
    for dz in z_offs:
        gc_wait("out", dz)

    attn = r.bias_out[...]
    for j in range(M):
        attn = attn + dot(r.CX[j], r.WO[j])
    r.ACC[...] = attn

    def moments(k):
        def body(at, s):
            v, valid = r.ACC[at, :], wide(r.VAL[at, :])
            vv = v * valid
            return s[0] + jnp.sum(vv, axis=0, keepdims=True), s[1] + jnp.sum(vv * v, axis=0, keepdims=True)

        zero = jnp.zeros((1, D), f32)
        s = chunks(body, (zero, zero))
        for n in range(2):
            for b in range(D // TILE):
                at = n * (D // TILE) + b
                r.S[k, at : at + 1, :] = s[n][:, b * TILE : (b + 1) * TILE]

    def unfold(total, n):
        return jnp.concatenate([total[n * (D // TILE) + b :][:1] for b in range(D // TILE)], axis=1)

    def variance(total, count):
        col_mean = unfold(total, 0) / count
        return unfold(total, 1) / count - col_mean * col_mean

    moments(1)
    sum_core(1)
    gather(2, 1, "up", "down")
    gather(1, 2, "up", "down")
    sum_chips(1)
    gather(0, 3, "up", "down")
    count = sum_done(0)[0:1, 0:1]
    var_attn = variance(sum_done(1), count)
    omega_attn = jnp.sqrt(1.0 + var_attn)
    gather(1, 3, "up", "down")
    gain_one, shift_one = r.gain_one[...], r.shift_one[...]
    gain_two, shift_two = r.gain_two[...], r.shift_two[...]

    def normed(pre):
        centred = pre - jnp.mean(pre, axis=-1, keepdims=True)
        var = jnp.mean(centred * centred, axis=-1, keepdims=True)
        rstd = lax.rsqrt(var + norm_eps)
        return centred * rstd, rstd

    def norm_back(dy, n, rstd, gain):
        dn = dy * gain
        return rstd * (
            dn - jnp.mean(dn, axis=-1, keepdims=True) - n * jnp.mean(dn * n, axis=-1, keepdims=True)
        )

    def norm_one(c, s):
        at, xat = rows(c, CHUNK, CHUNK), rows(c + HALO // CHUNK, CHUNK, CHUNK)
        n, rstd = normed(r.XB[xat, :].astype(f32) * omega_attn + r.ACC[at, :])
        r.N1[at, :] = n
        r.RS[at, :] = jnp.broadcast_to(rstd, (CHUNK, TILE))
        r.HL[at, :] = (n * gain_one + shift_one).astype(bf16)
        return s

    lax.fori_loop(0, R // CHUNK, norm_one, 0, unroll=4)
    gather(2, 2, "up", "down")

    r.ACC[...] = jnp.broadcast_to(r.bias_down[...], (R, D))
    c0 = (2.0 / jnp.pi) ** 0.5

    parts = [slice(n * R // PARTS, (n + 1) * R // PARTS) for n in range(PARTS)]

    def ffn_step(t, c):
        j = z_from(t)

        @pl.when(t > 0)
        def _():
            gc_wait("up", t)
            gc_wait("down", t)

        for at in parts:
            u = dot(r.HL[at, :], r.WU[j]) + r.RBI[j, 0:1, 0:F]
            uu = u * u
            th = jnp.tanh(u * (c0 + (c0 * 0.044715) * uu))
            half = 0.5 + 0.5 * th
            r.AC[j, at, :] = (u * half).astype(bf16)
            r.GP[j, at, :] = half + (0.5 * u) * (1.0 - th * th) * (c0 + (3.0 * 0.044715 * c0) * uu)
        r.ACC[...] += dot(r.AC[j], r.WD[j])

        @pl.when(t == 2)
        def _():
            gather(2, 3, "up", "down")

        return c

    lax.fori_loop(0, M, ffn_step, 0)

    moments(2)
    sum_core(2)
    r.HLT[...] = r.HL[...].T
    sum_chips(2)
    omega_ffn = jnp.sqrt(1.0 + var_attn + variance(sum_done(2), count))
    r.OM[...] = jnp.concatenate([omega_attn, omega_ffn, jnp.zeros((6, D), f32)], axis=0)
    put_omega = pltpu.make_async_copy(r.OM, r.omega, r.ls.at[13])
    put_omega.start()
    load[2].wait()

    def norm_two(at, s):
        hidden = r.N1[at, :] * gain_one + shift_one
        n, rstd = normed(hidden * omega_ffn + r.ACC[at, :])
        r.GI[at, :] = n * gain_two + shift_two
        dy = r.CT[at, :].astype(f32)
        d_pre = norm_back(dy, n, rstd, gain_two)
        low = d_pre.astype(bf16)
        r.ACC[at, :] = omega_ffn * d_pre
        r.DF[at, :] = low
        return (
            s[0] + jnp.sum(low.astype(f32), axis=0, keepdims=True),
            s[1] + jnp.sum(dy * n, axis=0, keepdims=True),
            s[2] + jnp.sum(dy, axis=0, keepdims=True),
        )

    zero = jnp.zeros((1, D), f32)
    s = chunks(norm_two, (zero, zero, zero))
    r.V[...] = jnp.zeros(r.V.shape, f32)
    r.VB[...] = jnp.zeros(r.VB.shape, f32)
    for n in range(3):
        r.V[3 + n : 4 + n, :] = s[n]
    put_out = pltpu.make_async_copy(r.GI, r.layer_out, r.ls.at[11])
    put_out.start()


    shard = [z_from(t) for t in range(M)]

    def ffn_back(t, c):
        j = z_from(t)
        r.GD[j, 0:F, :] = dot(r.AC[j].T, r.DF[...]).astype(bf16)
        rc_start("down", j)
        total = jnp.zeros((1, F), f32)
        for at in parts:
            low = (dot_nt(r.DF[at, :], r.WD[j]) * r.GP[j, at, :]).astype(bf16)
            r.DI[at, :] = low
            total = total + jnp.sum(low.astype(f32), axis=0, keepdims=True)
        r.VB[j, 0:1, 0:F] = total
        r.GU[j, 0:D, :] = dot(r.HLT[...], r.DI[...]).astype(bf16)
        rc_start("up", j)
        r.ACC[...] += dot_nt(r.DI[...], r.WU[j])

        rp_start("down", j)

        @pl.when(t > 0)
        def _():
            rp_start("up", z_from(t - 1))

        @pl.when(t == 2)
        def _():
            mids("down", shard[0])

        return c

    lax.fori_loop(0, M, ffn_back, 0)

    put_out.wait()

    def back_one(at, s):
        dy = r.ACC[at, :]
        n = r.N1[at, :]
        d_pre = norm_back(dy, n, r.RS[at, 0:1], gain_one)
        low = d_pre.astype(bf16)
        r.DA[at, :] = low
        r.GI[at, :] = omega_attn * d_pre
        return (
            s[0] + jnp.sum(low.astype(f32), axis=0, keepdims=True),
            s[1] + jnp.sum(dy * n, axis=0, keepdims=True),
            s[2] + jnp.sum(dy, axis=0, keepdims=True),
        )

    s = chunks(back_one, (zero, zero, zero))
    for n in range(3):
        r.V[n : n + 1, :] = s[n]
    for j in range(M):
        r.V[6 + j : 7 + j, :] = r.VB[j, 0:1, :]
    vc().start()
    rp_start("up", shard[M - 1])
    mids("down", shard[1])
    mids("up", shard[0])

    def both(step, *a):
        step("down", *a)
        step("up", *a)

    def out_back(j, c):
        r.GO[j, 0:HC, :] = dot(r.CXT[j], r.DA[...]).astype(bf16)
        rc_start("out", j)
        split_heads(r.DCM, j, dot_nt(r.DA[...], r.WO[j]), 1.0)
        return c

    lax.fori_loop(0, M, out_back, 0)
    rz_start("down", shard[0])

    def attend_back(j, which):
        span = {i: slice(i * TILE, i * TILE + WIN) for i in which}
        d_probs = {i: dot_nt(r.VN[j, span[i], :], r.DCM[j, i]) for i in which}
        d_scores = {}
        for i in which:
            probs = r.PS[j, i].astype(f32)
            delta = jnp.sum(probs * d_probs[i], axis=0, keepdims=True)
            d_scores[i] = (probs * (d_probs[i] - delta)).astype(bf16)
        for i in which:
            d_query = diagonal(dot(r.KT[j, :, span[i]], d_scores[i])).astype(bf16)
            r.DL[j, 0, i * TILE : (i + 1) * TILE, :] = d_query.T
            r.DV[j, span[i], :] += dot(r.PS[j, i], r.DCM[j, i])
            r.DK[j, span[i], :] += dot(d_scores[i], r.QM[j, i])

    early = range(min(HALO // TILE, NQ))

    def attend_early(t, c):
        j = step_of(t)
        r.DK[j] = jnp.zeros((KR, HC), f32)
        r.DV[j] = jnp.zeros((KR, HC), f32)
        attend_back(j, early)
        r.HS[j, 0:HALO, :] = r.DK[j, 0:HALO, :].astype(bf16)
        r.HS[j, HALO : 2 * HALO, :] = r.DV[j, 0:HALO, :].astype(bf16)

        @pl.when(joined)
        def _():
            halo(j).start()

        @pl.when(t == 0)
        def _():
            vec_plane()

        @pl.when(t == 1)
        def _():
            mids("up", shard[1])
            mids("down", shard[2])

        @pl.when(t == 2)
        def _():
            rz_start("up", shard[0])

        @pl.when(t == 3)
        def _():
            vec_z()
            rz_start("down", shard[1])
            for_all("out", rp_start)

        return c

    def qkv_back(j):
        @pl.when(lax.rem((z + 1) * R, ROW) > 0)
        def _():
            halo(j).wait_recv()
            r.DK[j, R:KR, :] += r.HR[j, 0:HALO, :].astype(f32)
            r.DV[j, R:KR, :] += r.HR[j, HALO : 2 * HALO, :].astype(f32)

        r.DL[j, 1] = r.DK[j, HALO:KR, :].astype(bf16)
        r.DL[j, 2] = r.DV[j, HALO:KR, :].astype(bf16)
        two = [jnp.sum(r.DL[j, n].astype(f32), axis=0, keepdims=True) for n in (0, 2)]
        two = jnp.concatenate(two, axis=1)
        for n in range(2 * HC // TILE):
            r.VB[j, 1 + n : 2 + n, 0:TILE] = two[:, n * TILE : (n + 1) * TILE]
        whole = dot(r.XT[...], jnp.concatenate([r.DL[j, n] for n in range(3)], axis=1)).astype(bf16)
        for n in range(3):
            r.GQ[j, n * D : (n + 1) * D, :] = whole[:, n * HC : (n + 1) * HC]
        rc_start("qkv", j)

    def back_in(j, c):
        r.GI[...] += dot_nt(jnp.concatenate([r.DL[j, n] for n in range(3)], axis=1), side_by_side(j))
        return c

    def for_all(g, step):
        lax.fori_loop(0, M, lambda j, c: (step(g, j), c)[1], 0)

    lax.fori_loop(0, M, attend_early, 0)

    def attend_late(t, c):
        j = step_of(t)
        attend_back(j, range(len(early), NQ))
        qkv_back(j)

        @pl.when(t == 0)
        def _():
            mids("up", shard[2])
            for n in range(3, M):
                mids("down", shard[n])
            rz_start("up", shard[1])

        @pl.when(t == 1)
        def _():
            for n in range(3, M):
                mids("up", shard[n])
            rz_start("down", shard[2])
            for_all("out", mids)

        @pl.when(t == 2)
        def _():
            rz_start("up", shard[2])
            for n in range(3, M):
                rz_start("down", shard[n])

        @pl.when(t == 3)
        def _():
            for n in range(3, M):
                rz_start("up", shard[n])
            for_all("out", rz_start)

        @pl.when(t > 0)
        def _():
            rp_start("qkv", step_of(t - 1))

        @pl.when(t > 1)
        def _():
            mids("qkv", step_of(t - 2))

        @pl.when(t > 3)
        def _():
            rz_start("qkv", step_of(t - 4))

        return c

    lax.fori_loop(0, M, attend_late, 0)
    for j in range(M):
        for n in range(2 * HC // TILE):
            at = j * (2 * HC // TILE) + n
            r.S[3, at : at + 1, :] = r.VB[j, 1 + n : 2 + n, 0:TILE]
    sum_core(3)
    lax.fori_loop(0, 1, back_in, 0)
    rp_start("qkv", step_of(M - 1), True)
    rz_start("qkv", step_of(M - 4))
    sum_chips(3)
    mids("qkv", step_of(M - 2))
    lax.fori_loop(1, M, back_in, 0)
    put_in = pltpu.make_async_copy(r.GI, r.grad_layer_in, r.ls.at[12])
    put_in.start()
    rz_start("qkv", step_of(M - 3))
    ap_start("down")
    ap_start("up")
    rz_start("qkv", step_of(M - 2))
    rz_start("qkv", step_of(M - 1), True)
    ap_start("out")
    ac_start("down")
    ac_start("up")
    ac_start("out")
    total = vec_done()
    r.VEC[0:6, :] = total[0:6]
    for j in range(M):
        r.VB[j, 0:1, :] = total[6 + j : 7 + j]
    total = sum_done(3)
    for j in range(M):
        for n in range(2 * HC // TILE):
            at = j * (2 * HC // TILE) + n
            r.VB[j, 1 + n : 2 + n, 0:TILE] = total[at : at + 1]
    r.VEC[6:7, :] = r.VB[z, 0:1, :]
    r.VEC[7:8, :] = jnp.zeros((1, D), f32)
    for n in range(2 * HC // TILE):
        r.VEC[7:8, n * TILE : (n + 1) * TILE] = r.VB[z, 1 + n : 2 + n, 0:TILE]
    put_vectors = pltpu.make_async_copy(r.VEC, r.vectors, r.ls.at[14])
    put_vectors.start()
    for g in ("down", "up", "out"):
        ac_wait(g)
    ap_start("qkv")
    ac_start("qkv")
    ac_wait("qkv")

    for g in group:
        g_sent(g)
        r_sent(g)
    for dz in z_offs:
        bias_copy(dz, z).wait_send()
    for k in range(4):
        sum_sent(k)
    vec_sent()

    @pl.when(joined)
    def _():
        lax.fori_loop(0, M, lambda j, c: (halo(j).wait_send(), c)[1], 0)

    put_in.wait()
    put_omega.wait()
    put_vectors.wait()


def shards(
    layer_in,
    cotangent,
    w_qkv,
    bias_qv,
    w_out,
    bias_out,
    gain_one,
    shift_one,
    w_up,
    bias_up,
    w_down,
    bias_down,
    gain_two,
    shift_two,
    segment_ids,
    key_mask,
):
    M, NDP = lax.axis_size("mp"), lax.axis_size("dp")
    D = layer_in.shape[1]
    HC, F, ROW = w_qkv.shape[2], w_up.shape[1], segment_ids.shape[1]
    R = layer_in.shape[0] // M
    NP, NH, NQ, KR, WIN = NDP // CORES, HC // HD, R // TILE, R + HALO, HALO + TILE
    little = ("bias_qv", "bias_up", "segment_ids", "key_mask", "bias_out")
    little += ("gain_one", "shift_one", "bias_down", "gain_two", "shift_two")
    sz = types.SimpleNamespace(little=little, M=M, NP=NP, R=R, ROW=ROW, HC=HC, F=F, D=D, W=max(F, HC))

    hbm, vmem = pl.BlockSpec(memory_space=pl.ANY), pl.BlockSpec(memory_space=pltpu.VMEM)
    ins = dict(
        layer_in=(layer_in, hbm),
        cotangent=(cotangent, hbm),
        w_qkv=(w_qkv.reshape(3 * D, HC), hbm),
        w_out=(w_out, hbm),
        w_up=(w_up, hbm),
        w_down=(w_down, hbm),
        bias_qv_in=(bias_qv, hbm),
        bias_up_in=(bias_up[None], hbm),
        bias_out_in=(bias_out[None], hbm),
        gain_one_in=(gain_one[None], hbm),
        shift_one_in=(shift_one[None], hbm),
        bias_down_in=(bias_down[None], hbm),
        gain_two_in=(gain_two[None], hbm),
        shift_two_in=(shift_two[None], hbm),
        segment_ids_in=(segment_ids, hbm),
        key_mask_in=(key_mask, hbm),
    )
    outs = dict(
        omega=((8, D), f32, hbm),
        layer_out=((R, D), f32, hbm),
        grad_layer_in=((R, D), f32, hbm),
        grad_w_qkv=((3 * D, HC), bf16, hbm),
        grad_w_out=((HC, D), bf16, hbm),
        grad_w_up=((D, F), bf16, hbm),
        grad_w_down=((F, D), bf16, hbm),
        vectors=((8, D), f32, hbm),
    )
    scratch = {
        name[:-3]: (value.shape, value.dtype) for name, (value, _) in ins.items() if name.endswith("_in")
    }
    scratch |= dict(
        XB=((KR, D), bf16),
        XT=((D, R), bf16),
        CT=((R, D), bf16),
        WQ=((M, 3 * D, HC), bf16),
        WO=((M, HC, D), bf16),
        WU=((M, D, F), bf16),
        WD=((M, F, D), bf16),
        SB=((8, sz.W), f32),
        RBI=((M, 8, sz.W), f32),
        QM=((M, NQ, NH * TILE, HC), bf16),
        KN=((M, KR, HC), bf16),
        KT=((M, HC, KR), bf16),
        VN=((M, KR, HC), bf16),
        VT=((M, HC, KR), bf16),
        PS=((M, NQ, WIN, NH * TILE), bf16),
        CX=((M, R, HC), bf16),
        CXT=((M, HC, R), bf16),
        DCM=((M, NQ, NH * TILE, HC), bf16),
        MB=((NQ, WIN, TILE), f32),
        VAL=((R, TILE), f32),
        ACC=((R, D), f32),
        N1=((R, D), f32),
        RS=((R, TILE), f32),
        HL=((R, D), bf16),
        HLT=((D, R), bf16),
        AC=((M, R, F), bf16),
        GP=((M, R, F), f32),
        DF=((R, D), bf16),
        DI=((R, F), bf16),
        DA=((R, D), bf16),
        GI=((R, D), f32),
        DK=((M, KR, HC), f32),
        DV=((M, KR, HC), f32),
        DL=((M, 3, R, HC), bf16),
        HS=((M, 2 * HALO, HC), bf16),
        HR=((M, 2 * HALO, HC), bf16),
        VB=((M, 8, D), f32),
        OM=((8, D), f32),
        VEC=((8, D), f32),
    )
    for tag, shape in (("Q", (3 * D, HC)), ("O", (HC, D)), ("U", (D, F)), ("D", (F, D))):
        pr = -(-shape[0] // (NDP * PACK)) * PACK
        scratch["G" + tag] = ((M, pr * NDP, shape[1]), bf16)
        scratch["RA" + tag] = ((M, pr * NP, shape[1]), bf16)
        scratch["RB" + tag] = ((NP - 1, M, pr, shape[1]), bf16)
        scratch["QB" + tag] = ((M, pr, shape[1]), bf16)
        scratch["RC" + tag] = ((M - 1, pr, shape[1]), bf16)
        scratch["O" + tag] = ((pr * NDP, shape[1]), bf16)
    vec_rows = -(-(6 + M) // 8) * 8
    scratch["V"] = scratch["Vc"] = ((vec_rows, D), f32)
    scratch["Vp"] = ((NP, vec_rows, D), f32)
    scratch["Vz"] = ((M, vec_rows, D), f32)
    scratch["S"] = scratch["Sc"] = ((4, 8, TILE), f32)
    scratch["Sa"] = ((4, NP * M, 8, TILE), f32)
    halves = 2 if any(-(-n // (NDP * PACK)) % 2 == 0 for n in (3 * D, D, F)) else 1
    sems = dict(
        ls=(15,),
        bs=(10,),
        gzs=(4, M - 1),
        gzr=(4, M - 1),
        gps=(4, halves, NP - 1, M - 1),
        gpr=(4, halves, NP - 1, M - 1),
        gcs=(4, M - 1),
        gcr=(4, M - 1),
        bzs=(M - 1,),
        bzr=(M - 1,),
        rcs=(4, M),
        rcr=(4, M),
        rps=(4, halves, NP - 1, M),
        rpr=(4, halves, NP - 1, M),
        rzs=(4, M - 1),
        rzr=(4, M - 1),
        aps=(4, NP - 1),
        apr=(4, NP - 1),
        acs=(4,),
        acr=(4,),
        scs=(4,),
        scr=(4,),
        sas=(4, NP * M - 1),
        sar=(4, NP * M - 1),
        vs=(NP - 1 + M,),
        vr=(NP - 1 + M,),
        hss=(M,),
        hsr=(M,),
    )
    names = list(ins) + list(outs) + list(scratch) + list(sems)
    got = pl.pallas_call(
        functools.partial(layer_kernel, sz, names),
        out_shape=[jax.ShapeDtypeStruct(s, t) for s, t, _ in outs.values()],
        in_specs=[spec for _, spec in ins.values()],
        out_specs=[spec for _, _, spec in outs.values()],
        scratch_shapes=[pltpu.VMEM(s, t) for s, t in scratch.values()]
        + [pltpu.SemaphoreType.DMA(s) for s in sems.values()],
        compiler_params=pltpu.CompilerParams(
            collective_id=0, has_side_effects=True, vmem_limit_bytes=62 << 20
        ),
    )(*[value for value, _ in ins.values()])
    shapes = [(2, D), (R, D), (R, D), (3 * D, HC), (2, HC), (HC, D)] + [(1, D)] * 3
    shapes += [(D, F), (1, F), (F, D)] + [(1, D)] * 3
    big = (1, 2, 3, 5, 9, 11)
    done = list(pl.pallas_call(
        functools.partial(result_kernel, HC, F),
        out_shape=[jax.ShapeDtypeStruct(s, f32) for s in shapes],
        in_specs=[hbm] * len(outs),
        out_specs=[hbm] * len(shapes),
        scratch_shapes=[
            pltpu.VMEM(shape, t)
            for n in (1, 2, 3, 9, 11, 5)
            for shape, t in ((shapes[n], f32 if n < 3 else bf16), ((8, TILE) if n < 3 else shapes[n], f32))
        ]
        + [pltpu.VMEM((8, D), f32)] * 2
        + [pltpu.VMEM(shape, f32) for n, shape in enumerate(shapes) if n not in big]
        + [pltpu.SemaphoreType.DMA((23,))],
    )(*got))
    done[3] = done[3].reshape(3, D, HC)
    return tuple(v[0] if v.shape[0] == 1 else v for v in done)


def result_kernel(HC, F, *refs):
    omega_in, layer_out, grad_in, g_qkv, g_out, g_up, g_down, vectors_in = refs[:8]
    out, held, (omega, vectors), little, sem = refs[8:23], refs[23:35], refs[35:37], refs[37:46], refs[46]
    pairs = ((layer_out, 1), (grad_in, 2), (g_qkv, 3), (g_up, 9), (g_down, 11), (g_out, 5))
    few = [pltpu.make_async_copy(omega_in, omega, sem.at[12]), pltpu.make_async_copy(vectors_in, vectors, sem.at[13])]
    reads, writes = [], []
    for n, (src, at) in enumerate(pairs):
        low, high = held[2 * n], held[2 * n + 1]
        reads.append(pltpu.make_async_copy(src, low, sem.at[n]))
        writes.append(pltpu.make_async_copy(low if n < 2 else high, out[at], sem.at[len(pairs) + n]))
        reads[n].start()
    for copy in few:
        copy.start()
    for copy in few:
        copy.wait()
    values = [omega[0:2, :], jnp.concatenate([vectors[7:8, 0:HC], vectors[7:8, HC : 2 * HC]], axis=0)]
    values += [vectors[n : n + 1, :] for n in range(3)] + [vectors[6:7, 0:F]]
    values += [vectors[n : n + 1, :] for n in range(3, 6)]
    for n, at in enumerate((0, 4, 6, 7, 8, 10, 12, 13, 14)):
        little[n][...] = values[n]
        writes.append(pltpu.make_async_copy(little[n], out[at], sem.at[14 + n]))
        writes[-1].start()
    for n in range(len(pairs)):
        reads[n].wait()
        if n >= 2:
            held[2 * n + 1][...] = held[2 * n][...].astype(f32)
        writes[n].start()
    for copy in writes:
        copy.wait()


def solution(mesh):
    in_specs = (
        P("dp", None),
        P("dp", None),
        P(None, None, "mp"),
        P(None, "mp"),
        P("mp", None),
        P(),
        P(),
        P(),
        P(None, "mp"),
        P("mp"),
        P("mp", None),
        P(),
        P(),
        P(),
        P("dp", None),
        P("dp", None),
    )
    out_specs = (
        P(),
        P(("dp", "mp"), None),
        P(("dp", "mp"), None),
        P(None, None, "mp"),
        P(None, "mp"),
        P("mp", None),
        P(),
        P(),
        P(),
        P(None, "mp"),
        P("mp"),
        P("mp", None),
        P(),
        P(),
        P(),
    )
    return jax.shard_map(shards, mesh=mesh, in_specs=in_specs, out_specs=out_specs, check_vma=False)
```

```python
import functools
import types

import jax
import jax.numpy as jnp
from jax import lax
from jax.experimental import pallas as pl
from jax.experimental.pallas import tpu as pltpu
from jax.sharding import PartitionSpec as P

HD = 64
LONGEST = 250
TILE = 128
HALO = -(-LONGEST // TILE) * TILE
CHUNK = 64
PARTS = 2
PACK = 16
CORES = 2

norm_eps = 1e-05
masked_fill = -1000000000.0
shut = -1e30
MESH = pl.DeviceIdType.MESH
f32 = jnp.float32
bf16 = jnp.bfloat16


def dot(a, b):
    return lax.dot_general(a, b, (((1,), (0,)), ((), ())), preferred_element_type=f32)


def dot_nt(a, b):
    return lax.dot_general(a, b, (((1,), (1,)), ((), ())), preferred_element_type=f32)


def layer_kernel(sz, names, *refs):
    r = types.SimpleNamespace(**dict(zip(names, refs)))
    M, NP, R, ROW, HC, F, D = sz.M, sz.NP, sz.R, sz.ROW, sz.HC, sz.F, sz.D
    NDP = NP * CORES
    NH, NQ, KR, WIN = HC // HD, R // TILE, R + HALO, HALO + TILE
    dp, z = lax.axis_index("dp"), lax.axis_index("mp")
    core, plane = lax.rem(dp, CORES), lax.div(dp, CORES)
    piece = core * NP + plane
    partner = (plane * CORES + 1 - core, z)

    def plane_to(off):
        return (lax.rem(plane + off, NP) * CORES + core, z)

    def plane_from(off):
        return lax.rem(plane + NP - off, NP)

    def flipped(at, mask, count):
        for b in range(count.bit_length() - 1):
            if mask >> b & 1:
                at = at + (1 - 2 * lax.rem(lax.div(at, 1 << b), 2)) * (1 << b)
        return at

    def z_from(dz):
        if isinstance(dz, int):
            return flipped(z, dz, M)
        return sum(
            (lax.rem(lax.div(z, 1 << b) + lax.div(dz, 1 << b), 2)) * (1 << b) for b in range(M.bit_length() - 1)
        )

    def z_apart(j):
        return z_from(j)

    def z_to(dz):
        return (dp, z_from(dz))

    def chip_to(n):
        return (lax.rem(plane + n // M, NP) * CORES + core, lax.rem(z + n % M, M))

    plane_offs, z_offs = range(1, NP), range(1, M)
    bits = NP.bit_length() - 1

    def flip(mask):
        return flipped(plane, mask, NP)

    def flip_to(mask):
        return (flip(mask) * CORES + core, z)

    orders = (tuple(range(bits)), tuple(reversed(range(bits))))

    def subsets(some):
        masks = [0]
        for b in some:
            masks = masks + [m | 1 << b for m in masks]
        return masks

    def rcopy(src, dst, send, recv, dev):
        return pltpu.make_async_remote_copy(
            src_ref=src, dst_ref=dst, send_sem=send, recv_sem=recv, device_id=dev, device_id_type=MESH
        )

    def rows(at, count, unit):
        return pl.ds(pl.multiple_of(at * unit, unit), count)

    bar = pltpu.get_barrier_semaphore()
    peers = [partner] + [chip_to(n) for n in range(1, NP * M)]
    for peer in peers:
        pl.semaphore_signal(bar, inc=1, device_id=peer, device_id_type=MESH)

    w_in = dict(qkv=r.w_qkv, out=r.w_out, up=r.w_up, down=r.w_down)
    w_all = dict(qkv=r.WQ, out=r.WO, up=r.WU, down=r.WD)
    group = ("qkv", "out", "up", "down")
    load = [
        pltpu.make_async_copy(r.layer_in.at[rows(z, R, R)], r.XB.at[pl.ds(HALO, R)], r.ls.at[0]),
        pltpu.make_async_copy(
            r.layer_in.at[rows(lax.rem(z * (R // TILE) + (M * R - HALO) // TILE, M * R // TILE), HALO, TILE)],
            r.XB.at[pl.ds(0, HALO)],
            r.ls.at[1],
        ),
        pltpu.make_async_copy(r.cotangent.at[rows(z, R, R)], r.CT, r.ls.at[2]),
    ]
    load_w = {
        g: pltpu.make_async_copy(w_in[g], w_all[g].at[z], r.ls.at[3 + n]) for n, g in enumerate(group)
    }
    little = {
        name: pltpu.make_async_copy(getattr(r, name + "_in"), getattr(r, name), r.bs.at[n])
        for n, name in enumerate(sz.little)
    }
    for name in sz.little:
        little[name].start()
    load[0].start()
    load[1].start()
    for g in group:
        load_w[g].start()
    load[2].start()

    pl.semaphore_wait(bar, len(peers))

    def g_split(g):
        return w_in[g].shape[0] % (NDP * PACK) == 0

    def gz(g, dz, zs):
        n = group.index(g)
        if not g_split(g):
            src, dst = w_in[g], w_all[g].at[zs]
        else:
            pr = w_in[g].shape[0] // NDP
            src, dst = w_in[g].at[rows(piece, pr, pr)], w_all[g].at[zs, rows(piece, pr, pr)]
        return rcopy(src, dst, r.gzs.at[n, dz - 1], r.gzr.at[n, dz - 1], z_to(dz))

    def g_halves(g):
        return 2 if w_in[g].shape[0] // NDP % (2 * PACK) == 0 else 1

    def gp(g, h, s, m, dz, there):
        n, hp = group.index(g), w_in[g].shape[0] // NDP // g_halves(g)
        order = orders[h]
        have = subsets(order[:s])[m] ^ (there << order[s])
        part = w_all[g].at[z_from(dz), rows((core * NP + flip(have)) * g_halves(g) + h, hp, hp)]
        at = (n, h, (1 << s) - 1 + m, dz - 1)
        return rcopy(part, part, r.gps.at[at], r.gpr.at[at], flip_to(1 << order[s]))

    straight = ("qkv", "out")

    def gd(g, off, dz, at_plane):
        n, pr = group.index(g), w_in[g].shape[0] // NDP
        part = w_all[g].at[z_from(dz), rows(core * NP + at_plane, pr, pr)]
        at = (n, 0, off - 1, dz - 1)
        return rcopy(part, part, r.gps.at[at], r.gpr.at[at], plane_to(off))

    def gc(g, dz, at_core):
        n, half = group.index(g), w_in[g].shape[0] // CORES
        part = w_all[g].at[z_from(dz), rows(at_core, half, half)]
        return rcopy(part, part, r.gcs.at[n, dz - 1], r.gcr.at[n, dz - 1], partner)

    def gz_start(g):
        for dz in z_offs:
            gz(g, dz, z).start()

    def gp_all(g, s):
        return [(h, m) for h in range(g_halves(g)) for m in range(1 << s)]

    def gp_start(g, s, dzs):
        for dz in dzs:
            if s == 0:
                gz(g, dz, z_from(dz)).wait_recv()
            if not g_split(g):
                continue
            if g in straight:
                if s == 0:
                    for off in plane_offs:
                        gd(g, off, dz, plane).start()
                if s == bits:
                    for off in plane_offs:
                        gd(g, off, dz, plane_from(off)).wait_recv()
                    gc(g, dz, core).start()
                continue
            if s > 0:
                for h, m in gp_all(g, s - 1):
                    gp(g, h, s - 1, m, dz, 1).wait_recv()
            if s < bits:
                for h, m in gp_all(g, s):
                    gp(g, h, s, m, dz, 0).start()
            else:
                gc(g, dz, core).start()

    near = [tuple(z_offs[0:1]), tuple(z_offs[1:2]), tuple(z_offs[2:])]

    def gather(phase, which, *groups):
        for dz in near[which - 1]:
            for s in ((0,), range(1, bits), (bits,))[phase]:
                for g in groups:
                    gp_start(g, s, (dz,))

    def gc_wait(g, dz):
        if g_split(g):
            gc(g, dz, 1 - core).wait_recv()

    def g_sent(g):
        for dz in z_offs:
            gz(g, dz, z).wait_send()
            if g_split(g):
                if g in straight:
                    for off in plane_offs:
                        gd(g, off, dz, plane).wait_send()
                else:
                    for s in range(bits):
                        for h, m in gp_all(g, s):
                            gp(g, h, s, m, dz, 0).wait_send()
                gc(g, dz, core).wait_send()

    def bias_copy(dz, zs):
        return rcopy(r.SB, r.RBI.at[zs], r.bzs.at[dz - 1], r.bzr.at[dz - 1], z_to(dz))

    g_part = dict(qkv=r.GQ, out=r.GO, up=r.GU, down=r.GD)
    g_ra = dict(qkv=r.RAQ, out=r.RAO, up=r.RAU, down=r.RAD)
    g_rb = dict(qkv=r.RBQ, out=r.RBO, up=r.RBU, down=r.RBD)
    g_qb = dict(qkv=r.QBQ, out=r.QBO, up=r.QBU, down=r.QBD)
    g_rc = dict(qkv=r.RCQ, out=r.RCO, up=r.RCU, down=r.RCD)
    g_out = dict(qkv=r.OQ, out=r.OO, up=r.OU, down=r.OD)
    g_res = dict(qkv=r.grad_w_qkv, out=r.grad_w_out, up=r.grad_w_up, down=r.grad_w_down)

    def pr_of(g):
        return g_part[g].shape[1] // NDP

    def rc(g, j):
        n, half = group.index(g), pr_of(g) * NP
        return rcopy(
            g_part[g].at[j, rows(1 - core, half, half)], g_ra[g].at[j], r.rcs.at[n, j], r.rcr.at[n, j], partner
        )

    def r_halves(g):
        return 2 if pr_of(g) % (2 * PACK) == 0 else 1

    def rp(g, off, j):
        n, pr = group.index(g), pr_of(g)
        at = core * NP + lax.rem(plane + off, NP)
        return rcopy(
            g_part[g].at[j, rows(at, pr, pr)],
            g_rb[g].at[off - 1, j],
            r.rps.at[n, 0, off - 1, j],
            r.rpr.at[n, 0, off - 1, j],
            plane_to(off),
        )

    def r_rows(g, h, mask):
        hp = pr_of(g) // r_halves(g)
        return rows((core * NP + flip(mask)) * r_halves(g) + h, hp, hp)

    def r_slot(g, h, s, m):
        hp = pr_of(g) // r_halves(g)
        return NP - (1 << (bits - s)) + m, pl.ds(h * hp, hp)

    def rh(g, h, s, m, j):
        n, order = group.index(g), orders[h]
        slot, half = r_slot(g, h, s, m)
        away = subsets(order[s + 1 :])[m] | 1 << order[s]
        return rcopy(
            g_part[g].at[j, r_rows(g, h, away)],
            g_rb[g].at[slot, j, half],
            r.rps.at[n, h, slot, j],
            r.rpr.at[n, h, slot, j],
            flip_to(1 << order[s]),
        )

    def rh_all(g, s):
        return [(h, m) for h in range(r_halves(g)) for m in range(1 << (bits - 1 - s))]

    def rz(g, j, dz):
        n = group.index(g)
        return rcopy(g_qb[g].at[j], g_rc[g].at[dz - 1], r.rzs.at[n, dz - 1], r.rzr.at[n, dz - 1], (dp, j))

    def ap(g, off, at_plane):
        n, pr = group.index(g), pr_of(g)
        part = g_out[g].at[rows(core * NP + at_plane, pr, pr)]
        return rcopy(part, part, r.aps.at[n, off - 1], r.apr.at[n, off - 1], plane_to(off))

    def ac(g, at_core):
        n, half = group.index(g), pr_of(g) * NP
        part = g_out[g].at[rows(at_core, half, half)]
        into = g_res[g].at[rows(at_core, half, half)] if unpadded(g) else part
        return rcopy(part, into, r.acs.at[n], r.acr.at[n], partner)

    def rc_start(g, j):
        rc(g, j).start()

    def rp_start(g, j, direct=False):
        rc(g, j).wait_recv()
        half = pr_of(g) * NP
        mine = rows(core, half, half)
        g_part[g][j, mine] = (g_part[g][j, mine].astype(f32) + g_ra[g][j].astype(f32)).astype(bf16)
        if direct:
            for off in plane_offs:
                rp(g, off, j).start()
        else:
            for h, m in rh_all(g, 0):
                rh(g, h, 0, m, j).start()

    def rp_step(g, j, s):
        for h, m in rh_all(g, s - 1):
            rh(g, h, s - 1, m, j).wait_recv()
            slot, half = r_slot(g, h, s - 1, m)
            at = r_rows(g, h, subsets(orders[h][s:])[m])
            g_part[g][j, at] = (g_part[g][j, at].astype(f32) + g_rb[g][slot, j, half].astype(f32)).astype(bf16)
        for h, m in rh_all(g, s):
            rh(g, h, s, m, j).start()

    def mids(g, j):
        for s in range(1, bits):
            rp_step(g, j, s)

    def rz_start(g, j, direct=False):
        pr = pr_of(g)
        total = g_part[g][j, rows(piece, pr, pr)].astype(f32)
        if direct:
            for off in plane_offs:
                rp(g, off, j).wait_recv()
                total = total + g_rb[g][off - 1, j].astype(f32)
        else:
            for h, m in rh_all(g, bits - 1):
                rh(g, h, bits - 1, m, j).wait_recv()
            total = total + g_rb[g][NP - 2, j].astype(f32)
        g_qb[g][j] = total.astype(bf16)

        @pl.when(j != z)
        def _():
            rz(g, j, z_apart(j)).start()

    def ap_start(g):
        pr = pr_of(g)
        total = g_qb[g][z].astype(f32)
        for dz in z_offs:
            rz(g, z, dz).wait_recv()
            total = total + g_rc[g][dz - 1].astype(f32)
        g_out[g][rows(piece, pr, pr)] = total.astype(bf16)
        for off in plane_offs:
            ap(g, off, plane).start()

    def ac_start(g):
        for off in plane_offs:
            ap(g, off, plane_from(off)).wait_recv()
        ac(g, core).start()
        if unpadded(g):
            result(g).start()

    def unpadded(g):
        return g_res[g].shape[0] == g_out[g].shape[0]

    def result(g):
        n, half = group.index(g), pr_of(g) * NP
        if unpadded(g):
            mine = rows(core, half, half)
            return pltpu.make_async_copy(g_out[g].at[mine], g_res[g].at[mine], r.ls.at[7 + n])
        got = g_out[g].at[pl.ds(0, g_res[g].shape[0])]
        return pltpu.make_async_copy(got, g_res[g], r.ls.at[7 + n])

    def ac_wait(g):
        ac(g, 1 - core).wait_recv()
        if not unpadded(g):
            result(g).start()

    def r_sent(g):
        def one(j, c):
            rc(g, j).wait_send()
            for s in range(bits):
                for h, m in rh_all(g, s):
                    rh(g, h, s, m, j).wait_send()
            return c

        def direct(j, c):
            rc(g, j).wait_send()
            for off in plane_offs:
                rp(g, off, j).wait_send()
            return c

        if g == "qkv":
            lax.fori_loop(0, M - 1, lambda t, c: one(step_of(t), c), 0)
            direct(step_of(M - 1), 0)
        else:
            lax.fori_loop(0, M, one, 0)
        for dz in z_offs:
            rz(g, z_from(dz), dz).wait_send()

    def left(g):
        for off in plane_offs:
            ap(g, off, plane).wait_send()
        ac(g, core).wait_send()
        result(g).wait()

    def sc(k):
        return rcopy(r.S.at[k], r.Sc.at[k], r.scs.at[k], r.scr.at[k], partner)

    def sa(k, n, there):
        if there:
            at = lax.rem(plane + NP - n // M, NP) * M + lax.rem(z + M - n % M, M)
        else:
            at = plane * M + z
        return rcopy(r.Sa.at[k, at], r.Sa.at[k, at], r.sas.at[k, n - 1], r.sar.at[k, n - 1], chip_to(n))

    def sum_core(k):
        sc(k).start()

    def sum_chips(k):
        sc(k).wait_recv()
        r.Sa[k, plane * M + z] = r.S[k] + r.Sc[k]
        for n in reversed(range(1, NP * M)):
            sa(k, n, False).start()

    def sum_done(k):
        for n in range(1, NP * M):
            sa(k, n, True).wait_recv()
        total = r.Sa[k, 0]
        for n in range(1, NP * M):
            total = total + r.Sa[k, n]
        return total

    def sum_sent(k):
        sc(k).wait_send()
        for n in range(1, NP * M):
            sa(k, n, False).wait_send()

    def vc():
        return rcopy(r.V, r.Vc, r.vs.at[0], r.vr.at[0], partner)

    def vp(off, at):
        return rcopy(r.Vp.at[at], r.Vp.at[at], r.vs.at[off], r.vr.at[off], plane_to(off))

    def vz(dz, at):
        return rcopy(r.Vz.at[at], r.Vz.at[at], r.vs.at[NP - 1 + dz], r.vr.at[NP - 1 + dz], z_to(dz))

    def vec_plane():
        vc().wait_recv()
        r.Vp[plane] = r.V[...] + r.Vc[...]
        for off in plane_offs:
            vp(off, plane).start()

    def vec_z():
        for off in plane_offs:
            vp(off, plane_from(off)).wait_recv()
        total = r.Vp[0]
        for s in plane_offs:
            total = total + r.Vp[s]
        r.Vz[z] = total
        for dz in z_offs:
            vz(dz, z).start()

    def vec_done():
        for dz in z_offs:
            vz(dz, z_from(dz)).wait_recv()
        total = r.Vz[0]
        for s in z_offs:
            total = total + r.Vz[s]
        return total

    def vec_sent():
        vc().wait_send()
        for off in plane_offs:
            vp(off, plane).wait_send()
        for dz in z_offs:
            vz(dz, z).wait_send()

    def halo(j):
        return rcopy(r.HS.at[j], r.HR.at[j], r.hss.at[j], r.hsr.at[j], (dp, lax.rem(z + M - 1, M)))

    sharing = max(ROW // R, 1)
    first_shard = lax.rem((lax.div(z, sharing) + 1) * sharing, M)

    def step_of(t):
        return lax.rem(first_shard + t, M)

    joined = lax.rem(z * R, ROW) > 0

    def chunks(body, init=0):
        return lax.fori_loop(0, R // CHUNK, lambda c, s: body(rows(c, CHUNK, CHUNK), s), init, unroll=8)

    def wide(cols):
        return jnp.concatenate([cols] * (D // TILE), axis=1)

    gz_start("qkv")
    little["bias_up"].wait()
    little["bias_qv"].wait()
    r.SB[...] = jnp.zeros((8, sz.W), f32)
    r.SB[0:1, 0:F] = r.bias_up[...]
    r.SB[1:3, 0:HC] = r.bias_qv[...]
    r.RBI[z] = r.SB[...]
    for dz in z_offs:
        bias_copy(dz, z).start()
    gz_start("out")
    for dz in z_offs:
        gz("up", dz, z).start()
        gz("down", dz, z).start()

    for name in sz.little[2:]:
        little[name].wait()
    unit = M * R // TILE
    marks = []
    for b in range(KR // TILE):
        at = lax.rem(z * NQ + (b - HALO // TILE) + unit, unit)
        packed, col = lax.div(at, ROW // TILE), lax.rem(at, ROW // TILE)
        spot = rows(col, TILE, TILE)
        sent, present = r.segment_ids[0:1, spot], r.key_mask[0:1, spot]
        for p in range(1, r.segment_ids.shape[0]):
            sent = jnp.where(packed == p, r.segment_ids[p : p + 1, spot] + p * ROW, sent)
            present = jnp.where(packed == p, r.key_mask[p : p + 1, spot], present)
        sent, present = sent.astype(f32), present.astype(f32)
        keyed = jnp.where(present > 0.5, sent, -1.0)
        if b < HALO // TILE:
            keyed = jnp.where(z > 0, keyed, -1.0)
        else:
            own = b - HALO // TILE
            r.VAL[own * TILE : (own + 1) * TILE, :] = jnp.broadcast_to(present, (TILE, TILE)).T
        marks.append((sent, jnp.broadcast_to(keyed, (TILE, TILE)).T))
    key_pos = lax.broadcasted_iota(jnp.int32, (TILE, TILE), 0)
    query_pos = lax.broadcasted_iota(jnp.int32, (TILE, TILE), 1)
    for i in range(NQ):
        asker = marks[i + HALO // TILE][0]
        for b in range(WIN // TILE):
            allowed = marks[i + b][1] == asker
            if b == WIN // TILE - 1:
                allowed = allowed & (key_pos <= query_pos)
            r.MB[i, b * TILE : (b + 1) * TILE, :] = jnp.where(allowed, 0.0, shut)

    head_of = lax.broadcasted_iota(jnp.int32, (1, HC), 1) // HD
    in_head = [(head_of == h).astype(f32) for h in range(NH)]
    scale = HD ** (-0.5)

    def diagonal(both):
        return jnp.concatenate(
            [both[h * HD : (h + 1) * HD, h * TILE : (h + 1) * TILE] for h in range(NH)], axis=0
        )

    def split_heads(dst, j, whole, factor):
        for h in range(NH):
            one = (whole * (in_head[h] * factor)).astype(bf16)
            for i in range(NQ):
                dst[j, i, h * TILE : (h + 1) * TILE, :] = one[i * TILE : (i + 1) * TILE, :]

    def side_by_side(j):
        return jnp.concatenate([r.WQ[j, n * D : (n + 1) * D, :] for n in range(3)], axis=1)

    def project(j):
        bias = r.RBI[j]
        whole = dot(r.XB[...], side_by_side(j))
        split_heads(r.QM, j, whole[HALO:KR, 0:HC] + bias[1:2, 0:HC], scale)
        key = whole[:, HC : 2 * HC]
        r.KN[j] = key.astype(bf16)
        r.KT[j] = (key * scale).astype(bf16).T
        value = (whole[:, 2 * HC : 3 * HC] + bias[2:3, 0:HC]).astype(bf16)
        r.VN[j] = value
        r.VT[j] = value.T

    def attend(j):
        span = [slice(i * TILE, i * TILE + WIN) for i in range(NQ)]
        for some in (range(NQ),):
            scores = {i: dot_nt(r.KN[j, span[i], :], r.QM[j, i]) for i in some}
            for i in some:
                masked = scores[i] + jnp.concatenate([r.MB[i]] * NH, axis=1)
                top = jnp.maximum(jnp.max(masked, axis=0, keepdims=True), masked_fill)
                expo = jnp.exp(masked - top)
                total = jnp.maximum(jnp.sum(expo, axis=0, keepdims=True), 1.0)
                r.PS[j, i] = (expo * (1.0 / total)).astype(bf16)
            for i in some:
                context = diagonal(dot(r.VT[j, :, span[i]], r.PS[j, i])).astype(bf16)
                r.CXT[j, :, i * TILE : (i + 1) * TILE] = context
                r.CX[j, i * TILE : (i + 1) * TILE, :] = context.T

    load[0].wait()
    load[1].wait()
    load_w["qkv"].wait()
    project(z)
    attend(z)
    r.XT[...] = r.XB[HALO:KR, :].T
    r.S[0] = jnp.broadcast_to(
        jnp.sum(r.VAL[...].reshape(R // 8, 8, TILE), axis=0).sum(axis=0, keepdims=True), (8, TILE)
    )
    sum_core(0)
    gather(0, 1, "qkv")
    gather(0, 2, "qkv")
    gather(0, 3, "qkv")
    gather(2, 1, "qkv")
    gather(2, 2, "qkv")
    for which in (1, 2, 3):
        gather(0, which, "out")
    gather(0, 1, "up", "down")
    for dz in z_offs:
        bias_copy(dz, z_from(dz)).wait_recv()
    sum_chips(0)

    def forward_step(t, c):
        j = z_from(t)
        gc_wait("qkv", t)
        project(j)
        attend(j)

        @pl.when(t == 1)
        def _():
            gather(2, 3, "qkv")

        @pl.when(t == 2)
        def _():
            for which in (1, 2, 3):
                gather(2, which, "out")
            gather(1, 1, "up", "down")

        @pl.when(t == 3)
        def _():
            gather(0, 2, "up", "down")

        return c

    lax.fori_loop(1, M, forward_step, 0)
    for g in ("out", "up", "down"):
        load_w[g].wait()
    for dz in z_offs:
        gc_wait("out", dz)

    attn = r.bias_out[...]
    for j in range(M):
        attn = attn + dot(r.CX[j], r.WO[j])
    r.ACC[...] = attn

    def moments(k):
        def body(at, s):
            v, valid = r.ACC[at, :], wide(r.VAL[at, :])
            vv = v * valid
            return s[0] + jnp.sum(vv, axis=0, keepdims=True), s[1] + jnp.sum(vv * v, axis=0, keepdims=True)

        zero = jnp.zeros((1, D), f32)
        s = chunks(body, (zero, zero))
        for n in range(2):
            for b in range(D // TILE):
                at = n * (D // TILE) + b
                r.S[k, at : at + 1, :] = s[n][:, b * TILE : (b + 1) * TILE]

    def unfold(total, n):
        return jnp.concatenate([total[n * (D // TILE) + b :][:1] for b in range(D // TILE)], axis=1)

    def variance(total, count):
        col_mean = unfold(total, 0) / count
        return unfold(total, 1) / count - col_mean * col_mean

    moments(1)
    sum_core(1)
    gather(2, 1, "up", "down")
    gather(1, 2, "up", "down")
    sum_chips(1)
    gather(0, 3, "up", "down")
    count = sum_done(0)[0:1, 0:1]
    var_attn = variance(sum_done(1), count)
    omega_attn = jnp.sqrt(1.0 + var_attn)
    gather(1, 3, "up", "down")
    gain_one, shift_one = r.gain_one[...], r.shift_one[...]
    gain_two, shift_two = r.gain_two[...], r.shift_two[...]

    def normed(pre):
        centred = pre - jnp.mean(pre, axis=-1, keepdims=True)
        var = jnp.mean(centred * centred, axis=-1, keepdims=True)
        rstd = lax.rsqrt(var + norm_eps)
        return centred * rstd, rstd

    def norm_back(dy, n, rstd, gain):
        dn = dy * gain
        return rstd * (
            dn - jnp.mean(dn, axis=-1, keepdims=True) - n * jnp.mean(dn * n, axis=-1, keepdims=True)
        )

    def norm_one(c, s):
        at, xat = rows(c, CHUNK, CHUNK), rows(c + HALO // CHUNK, CHUNK, CHUNK)
        n, rstd = normed(r.XB[xat, :].astype(f32) * omega_attn + r.ACC[at, :])
        r.N1[at, :] = n
        r.RS[at, :] = jnp.broadcast_to(rstd, (CHUNK, TILE))
        r.HL[at, :] = (n * gain_one + shift_one).astype(bf16)
        return s

    lax.fori_loop(0, R // CHUNK, norm_one, 0, unroll=8)
    gather(2, 2, "up", "down")

    r.ACC[...] = jnp.broadcast_to(r.bias_down[...], (R, D))
    c0 = (2.0 / jnp.pi) ** 0.5

    parts = [slice(n * R // PARTS, (n + 1) * R // PARTS) for n in range(PARTS)]

    def ffn_step(t, c):
        j = z_from(t)

        @pl.when(t > 0)
        def _():
            gc_wait("up", t)
            gc_wait("down", t)

        for at in parts:
            u = dot(r.HL[at, :], r.WU[j]) + r.RBI[j, 0:1, 0:F]
            uu = u * u
            th = jnp.tanh(u * (c0 + (c0 * 0.044715) * uu))
            half = 0.5 + 0.5 * th
            r.AC[j, at, :] = (u * half).astype(bf16)
            r.GP[j, at, :] = half + (0.5 * u) * (1.0 - th * th) * (c0 + (3.0 * 0.044715 * c0) * uu)
        r.ACC[...] += dot(r.AC[j], r.WD[j])

        @pl.when(t == 2)
        def _():
            gather(2, 3, "up", "down")

        return c

    lax.fori_loop(0, M, ffn_step, 0)

    moments(2)
    sum_core(2)
    r.HLT[...] = r.HL[...].T
    sum_chips(2)
    for g in group:
        g_sent(g)
    for dz in z_offs:
        bias_copy(dz, z).wait_send()
    for k in range(2):
        sum_sent(k)
    omega_ffn = jnp.sqrt(1.0 + var_attn + variance(sum_done(2), count))
    r.OM[...] = jnp.concatenate([omega_attn, omega_ffn, jnp.zeros((6, D), f32)], axis=0)
    put_omega = pltpu.make_async_copy(r.OM, r.omega, r.ls.at[13])
    put_omega.start()
    load[2].wait()

    def norm_two(at, s):
        hidden = r.N1[at, :] * gain_one + shift_one
        n, rstd = normed(hidden * omega_ffn + r.ACC[at, :])
        r.GI[at, :] = n * gain_two + shift_two
        dy = r.CT[at, :].astype(f32)
        d_pre = norm_back(dy, n, rstd, gain_two)
        low = d_pre.astype(bf16)
        r.ACC[at, :] = omega_ffn * d_pre
        r.DF[at, :] = low
        return (
            s[0] + jnp.sum(low.astype(f32), axis=0, keepdims=True),
            s[1] + jnp.sum(dy * n, axis=0, keepdims=True),
            s[2] + jnp.sum(dy, axis=0, keepdims=True),
        )

    zero = jnp.zeros((1, D), f32)
    s = chunks(norm_two, (zero, zero, zero))
    r.V[...] = jnp.zeros(r.V.shape, f32)
    r.VB[...] = jnp.zeros(r.VB.shape, f32)
    for n in range(3):
        r.V[3 + n : 4 + n, :] = s[n]
    put_out = pltpu.make_async_copy(r.GI, r.layer_out, r.ls.at[11])
    put_out.start()


    shard = [z_from(t) for t in range(M)]

    def ffn_back(t, c):
        j = z_from(t)
        r.GD[j, 0:F, :] = dot(r.AC[j].T, r.DF[...]).astype(bf16)
        rc_start("down", j)
        total = jnp.zeros((1, F), f32)
        for at in parts:
            low = (dot_nt(r.DF[at, :], r.WD[j]) * r.GP[j, at, :]).astype(bf16)
            r.DI[at, :] = low
            total = total + jnp.sum(low.astype(f32), axis=0, keepdims=True)
        r.VB[j, 0:1, 0:F] = total
        r.GU[j, 0:D, :] = dot(r.HLT[...], r.DI[...]).astype(bf16)
        rc_start("up", j)
        r.ACC[...] += dot_nt(r.DI[...], r.WU[j])

        rp_start("down", j)

        @pl.when(t > 0)
        def _():
            rp_start("up", z_from(t - 1))

        @pl.when(t == 2)
        def _():
            mids("down", shard[0])

        return c

    lax.fori_loop(0, M, ffn_back, 0)

    put_out.wait()

    def back_one(at, s):
        dy = r.ACC[at, :]
        n = r.N1[at, :]
        d_pre = norm_back(dy, n, r.RS[at, 0:1], gain_one)
        low = d_pre.astype(bf16)
        r.DA[at, :] = low
        r.GI[at, :] = omega_attn * d_pre
        return (
            s[0] + jnp.sum(low.astype(f32), axis=0, keepdims=True),
            s[1] + jnp.sum(dy * n, axis=0, keepdims=True),
            s[2] + jnp.sum(dy, axis=0, keepdims=True),
        )

    s = chunks(back_one, (zero, zero, zero))
    for n in range(3):
        r.V[n : n + 1, :] = s[n]
    for j in range(M):
        r.V[6 + j : 7 + j, :] = r.VB[j, 0:1, :]
    vc().start()
    rp_start("up", shard[M - 1])
    mids("down", shard[1])
    mids("up", shard[0])

    def both(step, *a):
        step("down", *a)
        step("up", *a)

    def out_back(j, c):
        r.GO[j, 0:HC, :] = dot(r.CXT[j], r.DA[...]).astype(bf16)
        rc_start("out", j)
        split_heads(r.DCM, j, dot_nt(r.DA[...], r.WO[j]), 1.0)
        return c

    lax.fori_loop(0, M, out_back, 0, unroll=2)
    rz_start("down", shard[0])

    def attend_back(j, which):
        span = {i: slice(i * TILE, i * TILE + WIN) for i in which}
        d_probs = {i: dot_nt(r.VN[j, span[i], :], r.DCM[j, i]) for i in which}
        d_scores = {}
        for i in which:
            probs = r.PS[j, i].astype(f32)
            delta = jnp.sum(probs * d_probs[i], axis=0, keepdims=True)
            d_scores[i] = (probs * (d_probs[i] - delta)).astype(bf16)
        for i in which:
            d_query = diagonal(dot(r.KT[j, :, span[i]], d_scores[i])).astype(bf16)
            r.DL[j, 0, i * TILE : (i + 1) * TILE, :] = d_query.T
            r.DV[j, span[i], :] += dot(r.PS[j, i], r.DCM[j, i])
            r.DK[j, span[i], :] += dot(d_scores[i], r.QM[j, i])

    early = range(min(HALO // TILE, NQ))

    def attend_early(t, c):
        j = step_of(t)
        r.DK[j] = jnp.zeros((KR, HC), f32)
        r.DV[j] = jnp.zeros((KR, HC), f32)
        attend_back(j, early)
        r.HS[j, 0:HALO, :] = r.DK[j, 0:HALO, :].astype(bf16)
        r.HS[j, HALO : 2 * HALO, :] = r.DV[j, 0:HALO, :].astype(bf16)

        @pl.when(joined)
        def _():
            halo(j).start()

        @pl.when(t == 0)
        def _():
            vec_plane()

        @pl.when(t == 1)
        def _():
            mids("up", shard[1])
            mids("down", shard[2])

        @pl.when(t == 2)
        def _():
            rz_start("up", shard[0])

        @pl.when(t == 3)
        def _():
            vec_z()
            rz_start("down", shard[1])
            for_all("out", rp_start)

        return c

    def qkv_back(j):
        @pl.when(lax.rem((z + 1) * R, ROW) > 0)
        def _():
            halo(j).wait_recv()
            r.DK[j, R:KR, :] += r.HR[j, 0:HALO, :].astype(f32)
            r.DV[j, R:KR, :] += r.HR[j, HALO : 2 * HALO, :].astype(f32)

        r.DL[j, 1] = r.DK[j, HALO:KR, :].astype(bf16)
        r.DL[j, 2] = r.DV[j, HALO:KR, :].astype(bf16)
        two = [jnp.sum(r.DL[j, n].astype(f32), axis=0, keepdims=True) for n in (0, 2)]
        two = jnp.concatenate(two, axis=1)
        for n in range(2 * HC // TILE):
            r.VB[j, 1 + n : 2 + n, 0:TILE] = two[:, n * TILE : (n + 1) * TILE]
        whole = dot(r.XT[...], jnp.concatenate([r.DL[j, n] for n in range(3)], axis=1)).astype(bf16)
        for n in range(3):
            r.GQ[j, n * D : (n + 1) * D, :] = whole[:, n * HC : (n + 1) * HC]
        rc_start("qkv", j)

    def back_in(j, c):
        r.GI[...] += dot_nt(jnp.concatenate([r.DL[j, n] for n in range(3)], axis=1), side_by_side(j))
        return c

    def for_all(g, step):
        lax.fori_loop(0, M, lambda j, c: (step(g, j), c)[1], 0)

    lax.fori_loop(0, M, attend_early, 0)

    def attend_late(t, c):
        j = step_of(t)
        attend_back(j, range(len(early), NQ))
        qkv_back(j)

        @pl.when(t == 0)
        def _():
            mids("up", shard[2])
            for n in range(3, M):
                mids("down", shard[n])
            rz_start("up", shard[1])

        @pl.when(t == 1)
        def _():
            for n in range(3, M):
                mids("up", shard[n])
            rz_start("down", shard[2])
            for_all("out", mids)

        @pl.when(t == 2)
        def _():
            rz_start("up", shard[2])
            for n in range(3, M):
                rz_start("down", shard[n])

        @pl.when(t == 3)
        def _():
            for n in range(3, M):
                rz_start("up", shard[n])
            for_all("out", rz_start)

        @pl.when(t > 0)
        def _():
            rp_start("qkv", step_of(t - 1))

        @pl.when(t > 1)
        def _():
            mids("qkv", step_of(t - 2))

        @pl.when(t > 3)
        def _():
            rz_start("qkv", step_of(t - 4))

        return c

    lax.fori_loop(0, M, attend_late, 0)
    for j in range(M):
        for n in range(2 * HC // TILE):
            at = j * (2 * HC // TILE) + n
            r.S[3, at : at + 1, :] = r.VB[j, 1 + n : 2 + n, 0:TILE]
    sum_core(3)
    lax.fori_loop(0, 1, back_in, 0)
    rp_start("qkv", step_of(M - 1), True)
    rz_start("qkv", step_of(M - 4))
    sum_chips(3)
    mids("qkv", step_of(M - 2))
    lax.fori_loop(1, M, back_in, 0)
    put_in = pltpu.make_async_copy(r.GI, r.grad_layer_in, r.ls.at[12])
    put_in.start()
    rz_start("qkv", step_of(M - 3))
    ap_start("down")
    ap_start("up")
    rz_start("qkv", step_of(M - 2))
    rz_start("qkv", step_of(M - 1), True)
    ap_start("out")
    ac_start("down")
    ac_start("up")
    ac_start("out")
    total = vec_done()
    r.VEC[0:6, :] = total[0:6]
    for j in range(M):
        r.VB[j, 0:1, :] = total[6 + j : 7 + j]
    total = sum_done(3)
    for j in range(M):
        for n in range(2 * HC // TILE):
            at = j * (2 * HC // TILE) + n
            r.VB[j, 1 + n : 2 + n, 0:TILE] = total[at : at + 1]
    r.VEC[6:7, :] = r.VB[z, 0:1, :]
    r.VEC[7:8, :] = jnp.zeros((1, D), f32)
    for n in range(2 * HC // TILE):
        r.VEC[7:8, n * TILE : (n + 1) * TILE] = r.VB[z, 1 + n : 2 + n, 0:TILE]
    put_vectors = pltpu.make_async_copy(r.VEC, r.vectors, r.ls.at[14])
    put_vectors.start()
    for g in ("down", "up", "out"):
        ac_wait(g)
    ap_start("qkv")
    for g in ("down", "up", "out"):
        r_sent(g)
        left(g)
    r_sent("qkv")
    for k in range(2, 4):
        sum_sent(k)
    vec_sent()

    @pl.when(joined)
    def _():
        lax.fori_loop(0, M, lambda j, c: (halo(j).wait_send(), c)[1], 0)

    ac_start("qkv")
    ac_wait("qkv")

    left("qkv")
    put_in.wait()
    put_omega.wait()
    put_vectors.wait()


def shards(
    layer_in,
    cotangent,
    w_qkv,
    bias_qv,
    w_out,
    bias_out,
    gain_one,
    shift_one,
    w_up,
    bias_up,
    w_down,
    bias_down,
    gain_two,
    shift_two,
    segment_ids,
    key_mask,
):
    M, NDP = lax.axis_size("mp"), lax.axis_size("dp")
    D = layer_in.shape[1]
    HC, F, ROW = w_qkv.shape[2], w_up.shape[1], segment_ids.shape[1]
    R = layer_in.shape[0] // M
    NP, NH, NQ, KR, WIN = NDP // CORES, HC // HD, R // TILE, R + HALO, HALO + TILE
    little = ("bias_qv", "bias_up", "segment_ids", "key_mask", "bias_out")
    little += ("gain_one", "shift_one", "bias_down", "gain_two", "shift_two")
    sz = types.SimpleNamespace(little=little, M=M, NP=NP, R=R, ROW=ROW, HC=HC, F=F, D=D, W=max(F, HC))

    hbm, vmem = pl.BlockSpec(memory_space=pl.ANY), pl.BlockSpec(memory_space=pltpu.VMEM)
    ins = dict(
        layer_in=(layer_in, hbm),
        cotangent=(cotangent, hbm),
        w_qkv=(w_qkv.reshape(3 * D, HC), hbm),
        w_out=(w_out, hbm),
        w_up=(w_up, hbm),
        w_down=(w_down, hbm),
        bias_qv_in=(bias_qv, hbm),
        bias_up_in=(bias_up[None], hbm),
        bias_out_in=(bias_out[None], hbm),
        gain_one_in=(gain_one[None], hbm),
        shift_one_in=(shift_one[None], hbm),
        bias_down_in=(bias_down[None], hbm),
        gain_two_in=(gain_two[None], hbm),
        shift_two_in=(shift_two[None], hbm),
        segment_ids_in=(segment_ids, hbm),
        key_mask_in=(key_mask, hbm),
    )
    outs = dict(
        omega=((8, D), f32, hbm),
        layer_out=((R, D), f32, hbm),
        grad_layer_in=((R, D), f32, hbm),
        grad_w_qkv=((3 * D, HC), bf16, hbm),
        grad_w_out=((HC, D), bf16, hbm),
        grad_w_up=((D, F), bf16, hbm),
        grad_w_down=((F, D), bf16, hbm),
        vectors=((8, D), f32, hbm),
    )
    scratch = {
        name[:-3]: (value.shape, value.dtype) for name, (value, _) in ins.items() if name.endswith("_in")
    }
    scratch |= dict(
        XB=((KR, D), bf16),
        XT=((D, R), bf16),
        CT=((R, D), bf16),
        WQ=((M, 3 * D, HC), bf16),
        WO=((M, HC, D), bf16),
        WU=((M, D, F), bf16),
        WD=((M, F, D), bf16),
        SB=((8, sz.W), f32),
        RBI=((M, 8, sz.W), f32),
        QM=((M, NQ, NH * TILE, HC), bf16),
        KN=((M, KR, HC), bf16),
        KT=((M, HC, KR), bf16),
        VN=((M, KR, HC), bf16),
        VT=((M, HC, KR), bf16),
        PS=((M, NQ, WIN, NH * TILE), bf16),
        CX=((M, R, HC), bf16),
        CXT=((M, HC, R), bf16),
        DCM=((M, NQ, NH * TILE, HC), bf16),
        MB=((NQ, WIN, TILE), f32),
        VAL=((R, TILE), f32),
        ACC=((R, D), f32),
        N1=((R, D), f32),
        RS=((R, TILE), f32),
        HL=((R, D), bf16),
        HLT=((D, R), bf16),
        AC=((M, R, F), bf16),
        GP=((M, R, F), f32),
        DF=((R, D), bf16),
        DI=((R, F), bf16),
        DA=((R, D), bf16),
        GI=((R, D), f32),
        DK=((M, KR, HC), f32),
        DV=((M, KR, HC), f32),
        DL=((M, 3, R, HC), bf16),
        HS=((M, 2 * HALO, HC), bf16),
        HR=((M, 2 * HALO, HC), bf16),
        VB=((M, 8, D), f32),
        OM=((8, D), f32),
        VEC=((8, D), f32),
    )
    for tag, shape in (("Q", (3 * D, HC)), ("O", (HC, D)), ("U", (D, F)), ("D", (F, D))):
        pr = -(-shape[0] // (NDP * PACK)) * PACK
        scratch["G" + tag] = ((M, pr * NDP, shape[1]), bf16)
        scratch["RA" + tag] = ((M, pr * NP, shape[1]), bf16)
        scratch["RB" + tag] = ((NP - 1, M, pr, shape[1]), bf16)
        scratch["QB" + tag] = ((M, pr, shape[1]), bf16)
        scratch["RC" + tag] = ((M - 1, pr, shape[1]), bf16)
        scratch["O" + tag] = ((pr * NDP, shape[1]), bf16)
    vec_rows = -(-(6 + M) // 8) * 8
    scratch["V"] = scratch["Vc"] = ((vec_rows, D), f32)
    scratch["Vp"] = ((NP, vec_rows, D), f32)
    scratch["Vz"] = ((M, vec_rows, D), f32)
    scratch["S"] = scratch["Sc"] = ((4, 8, TILE), f32)
    scratch["Sa"] = ((4, NP * M, 8, TILE), f32)
    halves = 2 if any(-(-n // (NDP * PACK)) % 2 == 0 for n in (3 * D, D, F)) else 1
    sems = dict(
        ls=(15,),
        bs=(10,),
        gzs=(4, M - 1),
        gzr=(4, M - 1),
        gps=(4, halves, NP - 1, M - 1),
        gpr=(4, halves, NP - 1, M - 1),
        gcs=(4, M - 1),
        gcr=(4, M - 1),
        bzs=(M - 1,),
        bzr=(M - 1,),
        rcs=(4, M),
        rcr=(4, M),
        rps=(4, halves, NP - 1, M),
        rpr=(4, halves, NP - 1, M),
        rzs=(4, M - 1),
        rzr=(4, M - 1),
        aps=(4, NP - 1),
        apr=(4, NP - 1),
        acs=(4,),
        acr=(4,),
        scs=(4,),
        scr=(4,),
        sas=(4, NP * M - 1),
        sar=(4, NP * M - 1),
        vs=(NP - 1 + M,),
        vr=(NP - 1 + M,),
        hss=(M,),
        hsr=(M,),
    )
    names = list(ins) + list(outs) + list(scratch) + list(sems)
    got = pl.pallas_call(
        functools.partial(layer_kernel, sz, names),
        out_shape=[jax.ShapeDtypeStruct(s, t) for s, t, _ in outs.values()],
        in_specs=[spec for _, spec in ins.values()],
        out_specs=[spec for _, _, spec in outs.values()],
        scratch_shapes=[pltpu.VMEM(s, t) for s, t in scratch.values()]
        + [pltpu.SemaphoreType.DMA(s) for s in sems.values()],
        compiler_params=pltpu.CompilerParams(
            collective_id=0, has_side_effects=True, vmem_limit_bytes=62 << 20
        ),
    )(*[value for value, _ in ins.values()])
    shapes = [(2, D), (R, D), (R, D), (3 * D, HC), (2, HC), (HC, D)] + [(1, D)] * 3
    shapes += [(D, F), (1, F), (F, D)] + [(1, D)] * 3
    big = (1, 2, 3, 5, 9, 11)
    done = list(pl.pallas_call(
        functools.partial(result_kernel, HC, F),
        out_shape=[jax.ShapeDtypeStruct(s, f32) for s in shapes],
        in_specs=[hbm] * len(outs),
        out_specs=[hbm] * len(shapes),
        scratch_shapes=[
            pltpu.VMEM(shape, t)
            for n in (1, 2, 3, 9, 11, 5)
            for shape, t in ((shapes[n], f32 if n < 3 else bf16), ((8, TILE) if n < 3 else shapes[n], f32))
        ]
        + [pltpu.VMEM((8, D), f32)] * 2
        + [pltpu.VMEM(shape, f32) for n, shape in enumerate(shapes) if n not in big]
        + [pltpu.SemaphoreType.DMA((23,))],
    )(*got))
    done[3] = done[3].reshape(3, D, HC)
    return tuple(v[0] if v.shape[0] == 1 else v for v in done)


def result_kernel(HC, F, *refs):
    omega_in, layer_out, grad_in, g_qkv, g_out, g_up, g_down, vectors_in = refs[:8]
    out, held, (omega, vectors), little, sem = refs[8:23], refs[23:35], refs[35:37], refs[37:46], refs[46]
    pairs = ((layer_out, 1), (grad_in, 2), (g_qkv, 3), (g_up, 9), (g_down, 11), (g_out, 5))
    few = [pltpu.make_async_copy(omega_in, omega, sem.at[12]), pltpu.make_async_copy(vectors_in, vectors, sem.at[13])]
    reads, writes = [], []
    for n, (src, at) in enumerate(pairs):
        low, high = held[2 * n], held[2 * n + 1]
        reads.append(pltpu.make_async_copy(src, low, sem.at[n]))
        writes.append(pltpu.make_async_copy(low if n < 2 else high, out[at], sem.at[len(pairs) + n]))
        reads[n].start()
    for copy in few:
        copy.start()
    for copy in few:
        copy.wait()
    values = [omega[0:2, :], jnp.concatenate([vectors[7:8, 0:HC], vectors[7:8, HC : 2 * HC]], axis=0)]
    values += [vectors[n : n + 1, :] for n in range(3)] + [vectors[6:7, 0:F]]
    values += [vectors[n : n + 1, :] for n in range(3, 6)]
    for n, at in enumerate((0, 4, 6, 7, 8, 10, 12, 13, 14)):
        little[n][...] = values[n]
        writes.append(pltpu.make_async_copy(little[n], out[at], sem.at[14 + n]))
        writes[-1].start()
    for n in range(len(pairs)):
        reads[n].wait()
        if n >= 2:
            held[2 * n + 1][...] = held[2 * n][...].astype(f32)
        writes[n].start()
    for copy in writes:
        copy.wait()


def solution(mesh):
    in_specs = (
        P("dp", None),
        P("dp", None),
        P(None, None, "mp"),
        P(None, "mp"),
        P("mp", None),
        P(),
        P(),
        P(),
        P(None, "mp"),
        P("mp"),
        P("mp", None),
        P(),
        P(),
        P(),
        P("dp", None),
        P("dp", None),
    )
    out_specs = (
        P(),
        P(("dp", "mp"), None),
        P(("dp", "mp"), None),
        P(None, None, "mp"),
        P(None, "mp"),
        P("mp", None),
        P(),
        P(),
        P(),
        P(None, "mp"),
        P("mp"),
        P("mp", None),
        P(),
        P(),
        P(),
    )
    return jax.shard_map(shards, mesh=mesh, in_specs=in_specs, out_specs=out_specs, check_vma=False)
```

```python
import functools
import types

import jax
import jax.numpy as jnp
from jax import lax
from jax.experimental import pallas as pl
from jax.experimental.pallas import tpu as pltpu
from jax.sharding import PartitionSpec as P

HD = 64
LONGEST = 250
TILE = 128
HALO = -(-LONGEST // TILE) * TILE
CHUNK = 64
PARTS = 2
PACK = 16
CORES = 2

norm_eps = 1e-05
masked_fill = -1000000000.0
shut = -1e30
MESH = pl.DeviceIdType.MESH
f32 = jnp.float32
bf16 = jnp.bfloat16


def dot(a, b):
    return lax.dot_general(a, b, (((1,), (0,)), ((), ())), preferred_element_type=f32)


def dot_nt(a, b):
    return lax.dot_general(a, b, (((1,), (1,)), ((), ())), preferred_element_type=f32)


def layer_kernel(sz, names, *refs):
    r = types.SimpleNamespace(**dict(zip(names, refs)))
    M, NP, R, ROW, HC, F, D = sz.M, sz.NP, sz.R, sz.ROW, sz.HC, sz.F, sz.D
    NDP = NP * CORES
    NH, NQ, KR, WIN = HC // HD, R // TILE, R + HALO, HALO + TILE
    dp, z = lax.axis_index("dp"), lax.axis_index("mp")
    core, plane = lax.rem(dp, CORES), lax.div(dp, CORES)
    piece = core * NP + plane
    partner = (plane * CORES + 1 - core, z)

    def plane_to(off):
        return (lax.rem(plane + off, NP) * CORES + core, z)

    def plane_from(off):
        return lax.rem(plane + NP - off, NP)

    def flipped(at, mask, count):
        for b in range(count.bit_length() - 1):
            if mask >> b & 1:
                at = at + (1 - 2 * lax.rem(lax.div(at, 1 << b), 2)) * (1 << b)
        return at

    def z_from(dz):
        if isinstance(dz, int):
            return flipped(z, dz, M)
        return sum(
            (lax.rem(lax.div(z, 1 << b) + lax.div(dz, 1 << b), 2)) * (1 << b) for b in range(M.bit_length() - 1)
        )

    def z_apart(j):
        return z_from(j)

    def z_to(dz):
        return (dp, z_from(dz))

    def chip_to(n):
        return (lax.rem(plane + n // M, NP) * CORES + core, lax.rem(z + n % M, M))

    plane_offs, z_offs = range(1, NP), range(1, M)
    bits = NP.bit_length() - 1

    def flip(mask):
        return flipped(plane, mask, NP)

    def flip_to(mask):
        return (flip(mask) * CORES + core, z)

    orders = (tuple(range(bits)), tuple(reversed(range(bits))))

    def subsets(some):
        masks = [0]
        for b in some:
            masks = masks + [m | 1 << b for m in masks]
        return masks

    def rcopy(src, dst, send, recv, dev):
        return pltpu.make_async_remote_copy(
            src_ref=src, dst_ref=dst, send_sem=send, recv_sem=recv, device_id=dev, device_id_type=MESH
        )

    def rows(at, count, unit):
        return pl.ds(pl.multiple_of(at * unit, unit), count)

    bar = pltpu.get_barrier_semaphore()
    peers = [partner] + [chip_to(n) for n in range(1, NP * M)]
    for peer in peers:
        pl.semaphore_signal(bar, inc=1, device_id=peer, device_id_type=MESH)

    w_in = dict(qkv=r.w_qkv, out=r.w_out, up=r.w_up, down=r.w_down)
    w_all = dict(qkv=r.WQ, out=r.WO, up=r.WU, down=r.WD)
    group = ("qkv", "out", "up", "down")
    load = [
        pltpu.make_async_copy(r.layer_in.at[rows(z, R, R)], r.XB.at[pl.ds(HALO, R)], r.ls.at[0]),
        pltpu.make_async_copy(
            r.layer_in.at[rows(lax.rem(z * (R // TILE) + (M * R - HALO) // TILE, M * R // TILE), HALO, TILE)],
            r.XB.at[pl.ds(0, HALO)],
            r.ls.at[1],
        ),
        pltpu.make_async_copy(r.cotangent.at[rows(z, R, R)], r.CT, r.ls.at[2]),
    ]
    load_w = {
        g: pltpu.make_async_copy(w_in[g], w_all[g].at[z], r.ls.at[3 + n]) for n, g in enumerate(group)
    }
    little = {
        name: pltpu.make_async_copy(getattr(r, name + "_in"), getattr(r, name), r.bs.at[n])
        for n, name in enumerate(sz.little)
    }
    for name in sz.little:
        little[name].start()
    load[0].start()
    load[1].start()
    for g in group:
        load_w[g].start()
    load[2].start()

    pl.semaphore_wait(bar, len(peers))

    def g_split(g):
        return w_in[g].shape[0] % (NDP * PACK) == 0

    def gz(g, dz, zs):
        n = group.index(g)
        if not g_split(g):
            src, dst = w_in[g], w_all[g].at[zs]
        else:
            pr = w_in[g].shape[0] // NDP
            src, dst = w_in[g].at[rows(piece, pr, pr)], w_all[g].at[zs, rows(piece, pr, pr)]
        return rcopy(src, dst, r.gzs.at[n, dz - 1], r.gzr.at[n, dz - 1], z_to(dz))

    def g_halves(g):
        return 2 if w_in[g].shape[0] // NDP % (2 * PACK) == 0 else 1

    def gp(g, h, s, m, dz, there):
        n, hp = group.index(g), w_in[g].shape[0] // NDP // g_halves(g)
        order = orders[h]
        have = subsets(order[:s])[m] ^ (there << order[s])
        part = w_all[g].at[z_from(dz), rows((core * NP + flip(have)) * g_halves(g) + h, hp, hp)]
        at = (n, h, (1 << s) - 1 + m, dz - 1)
        return rcopy(part, part, r.gps.at[at], r.gpr.at[at], flip_to(1 << order[s]))

    straight = ("qkv", "out")

    def gd(g, off, dz, at_plane):
        n, pr = group.index(g), w_in[g].shape[0] // NDP
        part = w_all[g].at[z_from(dz), rows(core * NP + at_plane, pr, pr)]
        at = (n, 0, off - 1, dz - 1)
        return rcopy(part, part, r.gps.at[at], r.gpr.at[at], plane_to(off))

    def gc(g, dz, at_core):
        n, half = group.index(g), w_in[g].shape[0] // CORES
        part = w_all[g].at[z_from(dz), rows(at_core, half, half)]
        return rcopy(part, part, r.gcs.at[n, dz - 1], r.gcr.at[n, dz - 1], partner)

    def gz_start(g):
        for dz in z_offs:
            gz(g, dz, z).start()

    def gp_all(g, s):
        return [(h, m) for h in range(g_halves(g)) for m in range(1 << s)]

    def gp_start(g, s, dzs):
        for dz in dzs:
            if s == 0:
                gz(g, dz, z_from(dz)).wait_recv()
            if not g_split(g):
                continue
            if g in straight:
                if s == 0:
                    for off in plane_offs:
                        gd(g, off, dz, plane).start()
                if s == bits:
                    for off in plane_offs:
                        gd(g, off, dz, plane_from(off)).wait_recv()
                    gc(g, dz, core).start()
                continue
            if s > 0:
                for h, m in gp_all(g, s - 1):
                    gp(g, h, s - 1, m, dz, 1).wait_recv()
            if s < bits:
                for h, m in gp_all(g, s):
                    gp(g, h, s, m, dz, 0).start()
            else:
                gc(g, dz, core).start()

    near = [tuple(z_offs[0:1]), tuple(z_offs[1:2]), tuple(z_offs[2:])]

    def gather(phase, which, *groups):
        for dz in near[which - 1]:
            for s in ((0,), range(1, bits), (bits,))[phase]:
                for g in groups:
                    gp_start(g, s, (dz,))

    def gc_wait(g, dz):
        if g_split(g):
            gc(g, dz, 1 - core).wait_recv()

    def g_sent(g):
        for dz in z_offs:
            gz(g, dz, z).wait_send()
            if g_split(g):
                if g in straight:
                    for off in plane_offs:
                        gd(g, off, dz, plane).wait_send()
                else:
                    for s in range(bits):
                        for h, m in gp_all(g, s):
                            gp(g, h, s, m, dz, 0).wait_send()
                gc(g, dz, core).wait_send()

    def bias_copy(dz, zs):
        return rcopy(r.SB, r.RBI.at[zs], r.bzs.at[dz - 1], r.bzr.at[dz - 1], z_to(dz))

    g_part = dict(qkv=r.GQ, out=r.GO, up=r.GU, down=r.GD)
    g_ra = dict(qkv=r.RAQ, out=r.RAO, up=r.RAU, down=r.RAD)
    g_rb = dict(qkv=r.RBQ, out=r.RBO, up=r.RBU, down=r.RBD)
    g_qb = dict(qkv=r.QBQ, out=r.QBO, up=r.QBU, down=r.QBD)
    g_rc = dict(qkv=r.RCQ, out=r.RCO, up=r.RCU, down=r.RCD)
    g_out = dict(qkv=r.OQ, out=r.OO, up=r.OU, down=r.OD)
    g_res = dict(qkv=r.grad_w_qkv, out=r.grad_w_out, up=r.grad_w_up, down=r.grad_w_down)

    def pr_of(g):
        return g_part[g].shape[1] // NDP

    def rc(g, j):
        n, half = group.index(g), pr_of(g) * NP
        return rcopy(
            g_part[g].at[j, rows(1 - core, half, half)], g_ra[g].at[j], r.rcs.at[n, j], r.rcr.at[n, j], partner
        )

    def r_halves(g):
        return 2 if pr_of(g) % (2 * PACK) == 0 else 1

    def rp(g, off, j):
        n, pr = group.index(g), pr_of(g)
        at = core * NP + lax.rem(plane + off, NP)
        return rcopy(
            g_part[g].at[j, rows(at, pr, pr)],
            g_rb[g].at[off - 1, j],
            r.rps.at[n, 0, off - 1, j],
            r.rpr.at[n, 0, off - 1, j],
            plane_to(off),
        )

    def r_rows(g, h, mask):
        hp = pr_of(g) // r_halves(g)
        return rows((core * NP + flip(mask)) * r_halves(g) + h, hp, hp)

    def r_slot(g, h, s, m):
        hp = pr_of(g) // r_halves(g)
        return NP - (1 << (bits - s)) + m, pl.ds(h * hp, hp)

    def rh(g, h, s, m, j):
        n, order = group.index(g), orders[h]
        slot, half = r_slot(g, h, s, m)
        away = subsets(order[s + 1 :])[m] | 1 << order[s]
        return rcopy(
            g_part[g].at[j, r_rows(g, h, away)],
            g_rb[g].at[slot, j, half],
            r.rps.at[n, h, slot, j],
            r.rpr.at[n, h, slot, j],
            flip_to(1 << order[s]),
        )

    def rh_all(g, s):
        return [(h, m) for h in range(r_halves(g)) for m in range(1 << (bits - 1 - s))]

    def rz(g, j, dz):
        n = group.index(g)
        return rcopy(g_qb[g].at[j], g_rc[g].at[dz - 1], r.rzs.at[n, dz - 1], r.rzr.at[n, dz - 1], (dp, j))

    def ap(g, off, at_plane):
        n, pr = group.index(g), pr_of(g)
        part = g_out[g].at[rows(core * NP + at_plane, pr, pr)]
        return rcopy(part, part, r.aps.at[n, off - 1], r.apr.at[n, off - 1], plane_to(off))

    def ac(g, at_core):
        n, half = group.index(g), pr_of(g) * NP
        part = g_out[g].at[rows(at_core, half, half)]
        into = g_res[g].at[rows(at_core, half, half)] if unpadded(g) else part
        return rcopy(part, into, r.acs.at[n], r.acr.at[n], partner)

    def rc_start(g, j):
        rc(g, j).start()

    def rp_start(g, j, direct=False):
        rc(g, j).wait_recv()
        half = pr_of(g) * NP
        mine = rows(core, half, half)
        g_part[g][j, mine] = (g_part[g][j, mine].astype(f32) + g_ra[g][j].astype(f32)).astype(bf16)
        if direct:
            for off in plane_offs:
                rp(g, off, j).start()
        else:
            for h, m in rh_all(g, 0):
                rh(g, h, 0, m, j).start()

    def rp_step(g, j, s):
        for h, m in rh_all(g, s - 1):
            rh(g, h, s - 1, m, j).wait_recv()
            slot, half = r_slot(g, h, s - 1, m)
            at = r_rows(g, h, subsets(orders[h][s:])[m])
            g_part[g][j, at] = (g_part[g][j, at].astype(f32) + g_rb[g][slot, j, half].astype(f32)).astype(bf16)
        for h, m in rh_all(g, s):
            rh(g, h, s, m, j).start()

    def mids(g, j):
        for s in range(1, bits):
            rp_step(g, j, s)

    def rz_start(g, j, direct=False):
        pr = pr_of(g)
        total = g_part[g][j, rows(piece, pr, pr)].astype(f32)
        if direct:
            for off in plane_offs:
                rp(g, off, j).wait_recv()
                total = total + g_rb[g][off - 1, j].astype(f32)
        else:
            for h, m in rh_all(g, bits - 1):
                rh(g, h, bits - 1, m, j).wait_recv()
            total = total + g_rb[g][NP - 2, j].astype(f32)
        g_qb[g][j] = total.astype(bf16)

        @pl.when(j != z)
        def _():
            rz(g, j, z_apart(j)).start()

    def ap_start(g):
        pr = pr_of(g)
        total = g_qb[g][z].astype(f32)
        for dz in z_offs:
            rz(g, z, dz).wait_recv()
            total = total + g_rc[g][dz - 1].astype(f32)
        g_out[g][rows(piece, pr, pr)] = total.astype(bf16)
        for off in plane_offs:
            ap(g, off, plane).start()

    def ac_start(g):
        for off in plane_offs:
            ap(g, off, plane_from(off)).wait_recv()
        ac(g, core).start()
        if unpadded(g):
            result(g).start()

    def unpadded(g):
        return g_res[g].shape[0] == g_out[g].shape[0]

    def result(g):
        n, half = group.index(g), pr_of(g) * NP
        if unpadded(g):
            mine = rows(core, half, half)
            return pltpu.make_async_copy(g_out[g].at[mine], g_res[g].at[mine], r.ls.at[7 + n])
        got = g_out[g].at[pl.ds(0, g_res[g].shape[0])]
        return pltpu.make_async_copy(got, g_res[g], r.ls.at[7 + n])

    def ac_wait(g):
        ac(g, 1 - core).wait_recv()
        if not unpadded(g):
            result(g).start()

    def r_sent(g):
        def one(j, c):
            rc(g, j).wait_send()
            for s in range(bits):
                for h, m in rh_all(g, s):
                    rh(g, h, s, m, j).wait_send()
            return c

        def direct(j, c):
            rc(g, j).wait_send()
            for off in plane_offs:
                rp(g, off, j).wait_send()
            return c

        if g == "qkv":
            lax.fori_loop(0, M - 1, lambda t, c: one(step_of(t), c), 0)
            direct(step_of(M - 1), 0)
        else:
            lax.fori_loop(0, M, one, 0)
        for dz in z_offs:
            rz(g, z_from(dz), dz).wait_send()

    def left(g):
        for off in plane_offs:
            ap(g, off, plane).wait_send()
        ac(g, core).wait_send()
        result(g).wait()

    def sc(k):
        return rcopy(r.S.at[k], r.Sc.at[k], r.scs.at[k], r.scr.at[k], partner)

    def sa(k, n, there):
        if there:
            at = lax.rem(plane + NP - n // M, NP) * M + lax.rem(z + M - n % M, M)
        else:
            at = plane * M + z
        return rcopy(r.Sa.at[k, at], r.Sa.at[k, at], r.sas.at[k, n - 1], r.sar.at[k, n - 1], chip_to(n))

    def sum_core(k):
        sc(k).start()

    def sum_chips(k):
        sc(k).wait_recv()
        r.Sa[k, plane * M + z] = r.S[k] + r.Sc[k]
        for n in reversed(range(1, NP * M)):
            sa(k, n, False).start()

    def sum_done(k):
        for n in range(1, NP * M):
            sa(k, n, True).wait_recv()
        total = r.Sa[k, 0]
        for n in range(1, NP * M):
            total = total + r.Sa[k, n]
        return total

    def sum_sent(k):
        sc(k).wait_send()
        for n in range(1, NP * M):
            sa(k, n, False).wait_send()

    def vc():
        return rcopy(r.V, r.Vc, r.vs.at[0], r.vr.at[0], partner)

    def vp(off, at):
        return rcopy(r.Vp.at[at], r.Vp.at[at], r.vs.at[off], r.vr.at[off], plane_to(off))

    def vz(dz, at):
        return rcopy(r.Vz.at[at], r.Vz.at[at], r.vs.at[NP - 1 + dz], r.vr.at[NP - 1 + dz], z_to(dz))

    def vec_plane():
        vc().wait_recv()
        r.Vp[plane] = r.V[...] + r.Vc[...]
        for off in plane_offs:
            vp(off, plane).start()

    def vec_z():
        for off in plane_offs:
            vp(off, plane_from(off)).wait_recv()
        total = r.Vp[0]
        for s in plane_offs:
            total = total + r.Vp[s]
        r.Vz[z] = total
        for dz in z_offs:
            vz(dz, z).start()

    def vec_done():
        for dz in z_offs:
            vz(dz, z_from(dz)).wait_recv()
        total = r.Vz[0]
        for s in z_offs:
            total = total + r.Vz[s]
        return total

    def vec_sent():
        vc().wait_send()
        for off in plane_offs:
            vp(off, plane).wait_send()
        for dz in z_offs:
            vz(dz, z).wait_send()

    def halo(j):
        return rcopy(r.HS.at[j], r.HR.at[j], r.hss.at[j], r.hsr.at[j], (dp, lax.rem(z + M - 1, M)))

    sharing = max(ROW // R, 1)
    first_shard = lax.rem((lax.div(z, sharing) + 1) * sharing, M)

    def step_of(t):
        return lax.rem(first_shard + t, M)

    joined = lax.rem(z * R, ROW) > 0

    def chunks(body, init=0):
        return lax.fori_loop(0, R // CHUNK, lambda c, s: body(rows(c, CHUNK, CHUNK), s), init, unroll=8)

    def wide(cols):
        return jnp.concatenate([cols] * (D // TILE), axis=1)

    gz_start("qkv")
    little["bias_up"].wait()
    little["bias_qv"].wait()
    r.SB[...] = jnp.zeros((8, sz.W), f32)
    r.SB[0:1, 0:F] = r.bias_up[...]
    r.SB[1:3, 0:HC] = r.bias_qv[...]
    r.RBI[z] = r.SB[...]
    for dz in z_offs:
        bias_copy(dz, z).start()
    gz_start("out")
    for dz in z_offs:
        gz("up", dz, z).start()
        gz("down", dz, z).start()

    for name in sz.little[2:]:
        little[name].wait()
    unit = M * R // TILE
    marks = []
    for b in range(KR // TILE):
        at = lax.rem(z * NQ + (b - HALO // TILE) + unit, unit)
        packed, col = lax.div(at, ROW // TILE), lax.rem(at, ROW // TILE)
        spot = rows(col, TILE, TILE)
        sent, present = r.segment_ids[0:1, spot], r.key_mask[0:1, spot]
        for p in range(1, r.segment_ids.shape[0]):
            sent = jnp.where(packed == p, r.segment_ids[p : p + 1, spot] + p * ROW, sent)
            present = jnp.where(packed == p, r.key_mask[p : p + 1, spot], present)
        sent, present = sent.astype(f32), present.astype(f32)
        keyed = jnp.where(present > 0.5, sent, -1.0)
        if b < HALO // TILE:
            keyed = jnp.where(z > 0, keyed, -1.0)
        else:
            own = b - HALO // TILE
            r.VAL[own * TILE : (own + 1) * TILE, :] = jnp.broadcast_to(present, (TILE, TILE)).T
        marks.append((sent, jnp.broadcast_to(keyed, (TILE, TILE)).T))
    key_pos = lax.broadcasted_iota(jnp.int32, (TILE, TILE), 0)
    query_pos = lax.broadcasted_iota(jnp.int32, (TILE, TILE), 1)
    for i in range(NQ):
        asker = marks[i + HALO // TILE][0]
        for b in range(WIN // TILE):
            allowed = marks[i + b][1] == asker
            if b == WIN // TILE - 1:
                allowed = allowed & (key_pos <= query_pos)
            r.MB[i, b * TILE : (b + 1) * TILE, :] = jnp.where(allowed, 0.0, shut)

    head_of = lax.broadcasted_iota(jnp.int32, (1, HC), 1) // HD
    in_head = [(head_of == h).astype(f32) for h in range(NH)]
    scale = HD ** (-0.5)

    def diagonal(both):
        return jnp.concatenate(
            [both[h * HD : (h + 1) * HD, h * TILE : (h + 1) * TILE] for h in range(NH)], axis=0
        )

    def split_heads(dst, j, whole, factor):
        for h in range(NH):
            one = (whole * (in_head[h] * factor)).astype(bf16)
            for i in range(NQ):
                dst[j, i, h * TILE : (h + 1) * TILE, :] = one[i * TILE : (i + 1) * TILE, :]

    def side_by_side(j):
        return jnp.concatenate([r.WQ[j, n * D : (n + 1) * D, :] for n in range(3)], axis=1)

    def project(j):
        bias = r.RBI[j]
        whole = dot(r.XB[...], side_by_side(j))
        split_heads(r.QM, j, whole[HALO:KR, 0:HC] + bias[1:2, 0:HC], scale)
        key = whole[:, HC : 2 * HC]
        r.KN[j] = key.astype(bf16)
        r.KT[j] = (key * scale).astype(bf16).T
        value = (whole[:, 2 * HC : 3 * HC] + bias[2:3, 0:HC]).astype(bf16)
        r.VN[j] = value
        r.VT[j] = value.T

    def attend(j):
        span = [slice(i * TILE, i * TILE + WIN) for i in range(NQ)]
        for some in (range(NQ),):
            scores = {i: dot_nt(r.KN[j, span[i], :], r.QM[j, i]) for i in some}
            for i in some:
                masked = scores[i] + jnp.concatenate([r.MB[i]] * NH, axis=1)
                top = jnp.maximum(jnp.max(masked, axis=0, keepdims=True), masked_fill)
                expo = jnp.exp(masked - top)
                total = jnp.maximum(jnp.sum(expo, axis=0, keepdims=True), 1.0)
                r.PS[j, i] = (expo * (1.0 / total)).astype(bf16)
            for i in some:
                context = diagonal(dot(r.VT[j, :, span[i]], r.PS[j, i])).astype(bf16)
                r.CXT[j, :, i * TILE : (i + 1) * TILE] = context
                r.CX[j, i * TILE : (i + 1) * TILE, :] = context.T

    load[0].wait()
    load[1].wait()
    load_w["qkv"].wait()
    project(z)
    attend(z)
    r.XT[...] = r.XB[HALO:KR, :].T
    r.S[0] = jnp.broadcast_to(
        jnp.sum(r.VAL[...].reshape(R // 8, 8, TILE), axis=0).sum(axis=0, keepdims=True), (8, TILE)
    )
    sum_core(0)
    gather(0, 1, "qkv")
    gather(0, 2, "qkv")
    gather(0, 3, "qkv")
    gather(2, 1, "qkv")
    gather(2, 2, "qkv")
    for which in (1, 2, 3):
        gather(0, which, "out")
    gather(0, 1, "up", "down")
    for dz in z_offs:
        bias_copy(dz, z_from(dz)).wait_recv()
    sum_chips(0)

    def forward_step(t, c):
        j = z_from(t)
        gc_wait("qkv", t)
        project(j)
        attend(j)

        @pl.when(t == 1)
        def _():
            gather(2, 3, "qkv")

        @pl.when(t == 2)
        def _():
            for which in (1, 2, 3):
                gather(2, which, "out")
            gather(1, 1, "up", "down")

        @pl.when(t == 3)
        def _():
            gather(0, 2, "up", "down")

        return c

    lax.fori_loop(1, M, forward_step, 0)
    for g in ("out", "up", "down"):
        load_w[g].wait()
    for dz in z_offs:
        gc_wait("out", dz)

    attn = r.bias_out[...]
    for j in range(M):
        attn = attn + dot(r.CX[j], r.WO[j])
    r.ACC[...] = attn

    def moments(k):
        def body(at, s):
            v, valid = r.ACC[at, :], wide(r.VAL[at, :])
            vv = v * valid
            return s[0] + jnp.sum(vv, axis=0, keepdims=True), s[1] + jnp.sum(vv * v, axis=0, keepdims=True)

        zero = jnp.zeros((1, D), f32)
        s = chunks(body, (zero, zero))
        for n in range(2):
            for b in range(D // TILE):
                at = n * (D // TILE) + b
                r.S[k, at : at + 1, :] = s[n][:, b * TILE : (b + 1) * TILE]

    def unfold(total, n):
        return jnp.concatenate([total[n * (D // TILE) + b :][:1] for b in range(D // TILE)], axis=1)

    def variance(total, count):
        col_mean = unfold(total, 0) / count
        return unfold(total, 1) / count - col_mean * col_mean

    moments(1)
    sum_core(1)
    gather(2, 1, "up", "down")
    gather(1, 2, "up", "down")
    sum_chips(1)
    gather(0, 3, "up", "down")
    count = sum_done(0)[0:1, 0:1]
    var_attn = variance(sum_done(1), count)
    omega_attn = jnp.sqrt(1.0 + var_attn)
    gather(1, 3, "up", "down")
    gain_one, shift_one = r.gain_one[...], r.shift_one[...]
    gain_two, shift_two = r.gain_two[...], r.shift_two[...]

    def normed(pre):
        centred = pre - jnp.mean(pre, axis=-1, keepdims=True)
        var = jnp.mean(centred * centred, axis=-1, keepdims=True)
        rstd = lax.rsqrt(var + norm_eps)
        return centred * rstd, rstd

    def norm_back(dy, n, rstd, gain):
        dn = dy * gain
        return rstd * (
            dn - jnp.mean(dn, axis=-1, keepdims=True) - n * jnp.mean(dn * n, axis=-1, keepdims=True)
        )

    def norm_one(c, s):
        at, xat = rows(c, CHUNK, CHUNK), rows(c + HALO // CHUNK, CHUNK, CHUNK)
        n, rstd = normed(r.XB[xat, :].astype(f32) * omega_attn + r.ACC[at, :])
        r.N1[at, :] = n
        r.RS[at, :] = jnp.broadcast_to(rstd, (CHUNK, TILE))
        r.HL[at, :] = (n * gain_one + shift_one).astype(bf16)
        return s

    lax.fori_loop(0, R // CHUNK, norm_one, 0, unroll=8)
    gather(2, 2, "up", "down")

    r.ACC[...] = jnp.broadcast_to(r.bias_down[...], (R, D))
    c0 = (2.0 / jnp.pi) ** 0.5

    parts = [slice(n * R // PARTS, (n + 1) * R // PARTS) for n in range(PARTS)]

    def ffn_step(t, c):
        j = z_from(t)

        @pl.when(t > 0)
        def _():
            gc_wait("up", t)
            gc_wait("down", t)

        for at in parts:
            u = dot(r.HL[at, :], r.WU[j]) + r.RBI[j, 0:1, 0:F]
            uu = u * u
            th = jnp.tanh(u * (c0 + (c0 * 0.044715) * uu))
            half = 0.5 + 0.5 * th
            r.AC[j, at, :] = (u * half).astype(bf16)
            r.GP[j, at, :] = half + (0.5 * u) * (1.0 - th * th) * (c0 + (3.0 * 0.044715 * c0) * uu)
        r.ACC[...] += dot(r.AC[j], r.WD[j])

        @pl.when(t == 2)
        def _():
            gather(2, 3, "up", "down")

        return c

    lax.fori_loop(0, M, ffn_step, 0)

    moments(2)
    sum_core(2)
    r.HLT[...] = r.HL[...].T
    sum_chips(2)
    for g in group:
        g_sent(g)
    for dz in z_offs:
        bias_copy(dz, z).wait_send()
    for k in range(2):
        sum_sent(k)
    omega_ffn = jnp.sqrt(1.0 + var_attn + variance(sum_done(2), count))
    r.OM[...] = jnp.concatenate([omega_attn, omega_ffn, jnp.zeros((6, D), f32)], axis=0)
    put_omega = pltpu.make_async_copy(r.OM, r.omega, r.ls.at[13])
    put_omega.start()
    load[2].wait()

    def norm_two(at, s):
        hidden = r.N1[at, :] * gain_one + shift_one
        n, rstd = normed(hidden * omega_ffn + r.ACC[at, :])
        r.GI[at, :] = n * gain_two + shift_two
        dy = r.CT[at, :].astype(f32)
        d_pre = norm_back(dy, n, rstd, gain_two)
        low = d_pre.astype(bf16)
        r.ACC[at, :] = omega_ffn * d_pre
        r.DF[at, :] = low
        return (
            s[0] + jnp.sum(low.astype(f32), axis=0, keepdims=True),
            s[1] + jnp.sum(dy * n, axis=0, keepdims=True),
            s[2] + jnp.sum(dy, axis=0, keepdims=True),
        )

    zero = jnp.zeros((1, D), f32)
    s = chunks(norm_two, (zero, zero, zero))
    r.V[...] = jnp.zeros(r.V.shape, f32)
    r.VB[...] = jnp.zeros(r.VB.shape, f32)
    for n in range(3):
        r.V[3 + n : 4 + n, :] = s[n]
    put_out = pltpu.make_async_copy(r.GI, r.layer_out, r.ls.at[11])
    put_out.start()


    shard = [z_from(t) for t in range(M)]

    def ffn_back(t, c):
        j = z_from(t)
        r.GD[j, 0:F, :] = dot(r.AC[j].T, r.DF[...]).astype(bf16)
        rc_start("down", j)
        total = jnp.zeros((1, F), f32)
        for at in parts:
            low = (dot_nt(r.DF[at, :], r.WD[j]) * r.GP[j, at, :]).astype(bf16)
            r.DI[at, :] = low
            total = total + jnp.sum(low.astype(f32), axis=0, keepdims=True)
        r.VB[j, 0:1, 0:F] = total
        r.GU[j, 0:D, :] = dot(r.HLT[...], r.DI[...]).astype(bf16)
        rc_start("up", j)
        r.ACC[...] += dot_nt(r.DI[...], r.WU[j])

        rp_start("down", j)

        @pl.when(t > 0)
        def _():
            rp_start("up", z_from(t - 1))

        @pl.when(t == 2)
        def _():
            mids("down", shard[0])

        return c

    lax.fori_loop(0, M, ffn_back, 0)

    put_out.wait()

    def back_one(at, s):
        dy = r.ACC[at, :]
        n = r.N1[at, :]
        d_pre = norm_back(dy, n, r.RS[at, 0:1], gain_one)
        low = d_pre.astype(bf16)
        r.DA[at, :] = low
        r.GI[at, :] = omega_attn * d_pre
        return (
            s[0] + jnp.sum(low.astype(f32), axis=0, keepdims=True),
            s[1] + jnp.sum(dy * n, axis=0, keepdims=True),
            s[2] + jnp.sum(dy, axis=0, keepdims=True),
        )

    s = chunks(back_one, (zero, zero, zero))
    for n in range(3):
        r.V[n : n + 1, :] = s[n]
    for j in range(M):
        r.V[6 + j : 7 + j, :] = r.VB[j, 0:1, :]
    vc().start()
    rp_start("up", shard[M - 1])
    mids("down", shard[1])
    mids("up", shard[0])

    def both(step, *a):
        step("down", *a)
        step("up", *a)

    def out_back(j, c):
        r.GO[j, 0:HC, :] = dot(r.CXT[j], r.DA[...]).astype(bf16)
        rc_start("out", j)
        split_heads(r.DCM, j, dot_nt(r.DA[...], r.WO[j]), 1.0)
        return c

    lax.fori_loop(0, M, out_back, 0, unroll=True)
    rz_start("down", shard[0])

    def attend_back(j, which):
        span = {i: slice(i * TILE, i * TILE + WIN) for i in which}
        d_probs = {i: dot_nt(r.VN[j, span[i], :], r.DCM[j, i]) for i in which}
        d_scores = {}
        for i in which:
            probs = r.PS[j, i].astype(f32)
            delta = jnp.sum(probs * d_probs[i], axis=0, keepdims=True)
            d_scores[i] = (probs * (d_probs[i] - delta)).astype(bf16)
        for i in which:
            d_query = diagonal(dot(r.KT[j, :, span[i]], d_scores[i])).astype(bf16)
            r.DL[j, 0, i * TILE : (i + 1) * TILE, :] = d_query.T
            r.DV[j, span[i], :] += dot(r.PS[j, i], r.DCM[j, i])
            r.DK[j, span[i], :] += dot(d_scores[i], r.QM[j, i])

    early = range(min(HALO // TILE, NQ))

    def attend_early(t, c):
        j = step_of(t)
        r.DK[j] = jnp.zeros((KR, HC), f32)
        r.DV[j] = jnp.zeros((KR, HC), f32)
        attend_back(j, early)
        r.HS[j, 0:HALO, :] = r.DK[j, 0:HALO, :].astype(bf16)
        r.HS[j, HALO : 2 * HALO, :] = r.DV[j, 0:HALO, :].astype(bf16)

        @pl.when(joined)
        def _():
            halo(j).start()

        @pl.when(t == 0)
        def _():
            vec_plane()

        @pl.when(t == 1)
        def _():
            mids("up", shard[1])
            mids("down", shard[2])

        @pl.when(t == 2)
        def _():
            rz_start("up", shard[0])

        @pl.when(t == 3)
        def _():
            vec_z()
            rz_start("down", shard[1])
            for_all("out", rp_start)

        return c

    def qkv_back(j):
        @pl.when(lax.rem((z + 1) * R, ROW) > 0)
        def _():
            halo(j).wait_recv()
            r.DK[j, R:KR, :] += r.HR[j, 0:HALO, :].astype(f32)
            r.DV[j, R:KR, :] += r.HR[j, HALO : 2 * HALO, :].astype(f32)

        r.DL[j, 1] = r.DK[j, HALO:KR, :].astype(bf16)
        r.DL[j, 2] = r.DV[j, HALO:KR, :].astype(bf16)
        two = [jnp.sum(r.DL[j, n].astype(f32), axis=0, keepdims=True) for n in (0, 2)]
        two = jnp.concatenate(two, axis=1)
        for n in range(2 * HC // TILE):
            r.VB[j, 1 + n : 2 + n, 0:TILE] = two[:, n * TILE : (n + 1) * TILE]
        whole = dot(r.XT[...], jnp.concatenate([r.DL[j, n] for n in range(3)], axis=1)).astype(bf16)
        for n in range(3):
            r.GQ[j, n * D : (n + 1) * D, :] = whole[:, n * HC : (n + 1) * HC]
        rc_start("qkv", j)

    def back_in(j, c):
        r.GI[...] += dot_nt(jnp.concatenate([r.DL[j, n] for n in range(3)], axis=1), side_by_side(j))
        return c

    def for_all(g, step):
        lax.fori_loop(0, M, lambda j, c: (step(g, j), c)[1], 0)

    lax.fori_loop(0, M, attend_early, 0)

    def attend_late(t, c):
        j = step_of(t)
        attend_back(j, range(len(early), NQ))
        qkv_back(j)

        @pl.when(t == 0)
        def _():
            mids("up", shard[2])
            for n in range(3, M):
                mids("down", shard[n])
            rz_start("up", shard[1])

        @pl.when(t == 1)
        def _():
            for n in range(3, M):
                mids("up", shard[n])
            rz_start("down", shard[2])
            for_all("out", mids)

        @pl.when(t == 2)
        def _():
            rz_start("up", shard[2])
            for n in range(3, M):
                rz_start("down", shard[n])

        @pl.when(t == 3)
        def _():
            for n in range(3, M):
                rz_start("up", shard[n])
            for_all("out", rz_start)

        @pl.when(t > 0)
        def _():
            rp_start("qkv", step_of(t - 1))

        @pl.when(t > 1)
        def _():
            mids("qkv", step_of(t - 2))

        @pl.when(t > 3)
        def _():
            rz_start("qkv", step_of(t - 4))

        return c

    lax.fori_loop(0, M, attend_late, 0)
    for j in range(M):
        for n in range(2 * HC // TILE):
            at = j * (2 * HC // TILE) + n
            r.S[3, at : at + 1, :] = r.VB[j, 1 + n : 2 + n, 0:TILE]
    sum_core(3)
    lax.fori_loop(0, 1, back_in, 0)
    rp_start("qkv", step_of(M - 1), True)
    rz_start("qkv", step_of(M - 4))
    sum_chips(3)
    mids("qkv", step_of(M - 2))
    lax.fori_loop(1, M, back_in, 0, unroll=True)
    put_in = pltpu.make_async_copy(r.GI, r.grad_layer_in, r.ls.at[12])
    put_in.start()
    rz_start("qkv", step_of(M - 3))
    ap_start("down")
    ap_start("up")
    rz_start("qkv", step_of(M - 2))
    rz_start("qkv", step_of(M - 1), True)
    ap_start("out")
    ac_start("down")
    ac_start("up")
    ac_start("out")
    total = vec_done()
    r.VEC[0:6, :] = total[0:6]
    for j in range(M):
        r.VB[j, 0:1, :] = total[6 + j : 7 + j]
    total = sum_done(3)
    for j in range(M):
        for n in range(2 * HC // TILE):
            at = j * (2 * HC // TILE) + n
            r.VB[j, 1 + n : 2 + n, 0:TILE] = total[at : at + 1]
    r.VEC[6:7, :] = r.VB[z, 0:1, :]
    r.VEC[7:8, :] = jnp.zeros((1, D), f32)
    for n in range(2 * HC // TILE):
        r.VEC[7:8, n * TILE : (n + 1) * TILE] = r.VB[z, 1 + n : 2 + n, 0:TILE]
    put_vectors = pltpu.make_async_copy(r.VEC, r.vectors, r.ls.at[14])
    put_vectors.start()
    for g in ("down", "up", "out"):
        ac_wait(g)
    ap_start("qkv")
    for g in ("down", "up", "out"):
        r_sent(g)
        left(g)
    r_sent("qkv")
    for k in range(2, 4):
        sum_sent(k)
    vec_sent()

    @pl.when(joined)
    def _():
        lax.fori_loop(0, M, lambda j, c: (halo(j).wait_send(), c)[1], 0)

    ac_start("qkv")
    ac_wait("qkv")

    left("qkv")
    put_in.wait()
    put_omega.wait()
    put_vectors.wait()


def shards(
    layer_in,
    cotangent,
    w_qkv,
    bias_qv,
    w_out,
    bias_out,
    gain_one,
    shift_one,
    w_up,
    bias_up,
    w_down,
    bias_down,
    gain_two,
    shift_two,
    segment_ids,
    key_mask,
):
    M, NDP = lax.axis_size("mp"), lax.axis_size("dp")
    D = layer_in.shape[1]
    HC, F, ROW = w_qkv.shape[2], w_up.shape[1], segment_ids.shape[1]
    R = layer_in.shape[0] // M
    NP, NH, NQ, KR, WIN = NDP // CORES, HC // HD, R // TILE, R + HALO, HALO + TILE
    little = ("bias_qv", "bias_up", "segment_ids", "key_mask", "bias_out")
    little += ("gain_one", "shift_one", "bias_down", "gain_two", "shift_two")
    sz = types.SimpleNamespace(little=little, M=M, NP=NP, R=R, ROW=ROW, HC=HC, F=F, D=D, W=max(F, HC))

    hbm, vmem = pl.BlockSpec(memory_space=pl.ANY), pl.BlockSpec(memory_space=pltpu.VMEM)
    ins = dict(
        layer_in=(layer_in, hbm),
        cotangent=(cotangent, hbm),
        w_qkv=(w_qkv.reshape(3 * D, HC), hbm),
        w_out=(w_out, hbm),
        w_up=(w_up, hbm),
        w_down=(w_down, hbm),
        bias_qv_in=(bias_qv, hbm),
        bias_up_in=(bias_up[None], hbm),
        bias_out_in=(bias_out[None], hbm),
        gain_one_in=(gain_one[None], hbm),
        shift_one_in=(shift_one[None], hbm),
        bias_down_in=(bias_down[None], hbm),
        gain_two_in=(gain_two[None], hbm),
        shift_two_in=(shift_two[None], hbm),
        segment_ids_in=(segment_ids, hbm),
        key_mask_in=(key_mask, hbm),
    )
    outs = dict(
        omega=((8, D), f32, hbm),
        layer_out=((R, D), f32, hbm),
        grad_layer_in=((R, D), f32, hbm),
        grad_w_qkv=((3 * D, HC), bf16, hbm),
        grad_w_out=((HC, D), bf16, hbm),
        grad_w_up=((D, F), bf16, hbm),
        grad_w_down=((F, D), bf16, hbm),
        vectors=((8, D), f32, hbm),
    )
    scratch = {
        name[:-3]: (value.shape, value.dtype) for name, (value, _) in ins.items() if name.endswith("_in")
    }
    scratch |= dict(
        XB=((KR, D), bf16),
        XT=((D, R), bf16),
        CT=((R, D), bf16),
        WQ=((M, 3 * D, HC), bf16),
        WO=((M, HC, D), bf16),
        WU=((M, D, F), bf16),
        WD=((M, F, D), bf16),
        SB=((8, sz.W), f32),
        RBI=((M, 8, sz.W), f32),
        QM=((M, NQ, NH * TILE, HC), bf16),
        KN=((M, KR, HC), bf16),
        KT=((M, HC, KR), bf16),
        VN=((M, KR, HC), bf16),
        VT=((M, HC, KR), bf16),
        PS=((M, NQ, WIN, NH * TILE), bf16),
        CX=((M, R, HC), bf16),
        CXT=((M, HC, R), bf16),
        DCM=((M, NQ, NH * TILE, HC), bf16),
        MB=((NQ, WIN, TILE), f32),
        VAL=((R, TILE), f32),
        ACC=((R, D), f32),
        N1=((R, D), f32),
        RS=((R, TILE), f32),
        HL=((R, D), bf16),
        HLT=((D, R), bf16),
        AC=((M, R, F), bf16),
        GP=((M, R, F), f32),
        DF=((R, D), bf16),
        DI=((R, F), bf16),
        DA=((R, D), bf16),
        GI=((R, D), f32),
        DK=((M, KR, HC), f32),
        DV=((M, KR, HC), f32),
        DL=((M, 3, R, HC), bf16),
        HS=((M, 2 * HALO, HC), bf16),
        HR=((M, 2 * HALO, HC), bf16),
        VB=((M, 8, D), f32),
        OM=((8, D), f32),
        VEC=((8, D), f32),
    )
    for tag, shape in (("Q", (3 * D, HC)), ("O", (HC, D)), ("U", (D, F)), ("D", (F, D))):
        pr = -(-shape[0] // (NDP * PACK)) * PACK
        scratch["G" + tag] = ((M, pr * NDP, shape[1]), bf16)
        scratch["RA" + tag] = ((M, pr * NP, shape[1]), bf16)
        scratch["RB" + tag] = ((NP - 1, M, pr, shape[1]), bf16)
        scratch["QB" + tag] = ((M, pr, shape[1]), bf16)
        scratch["RC" + tag] = ((M - 1, pr, shape[1]), bf16)
        scratch["O" + tag] = ((pr * NDP, shape[1]), bf16)
    vec_rows = -(-(6 + M) // 8) * 8
    scratch["V"] = scratch["Vc"] = ((vec_rows, D), f32)
    scratch["Vp"] = ((NP, vec_rows, D), f32)
    scratch["Vz"] = ((M, vec_rows, D), f32)
    scratch["S"] = scratch["Sc"] = ((4, 8, TILE), f32)
    scratch["Sa"] = ((4, NP * M, 8, TILE), f32)
    halves = 2 if any(-(-n // (NDP * PACK)) % 2 == 0 for n in (3 * D, D, F)) else 1
    sems = dict(
        ls=(15,),
        bs=(10,),
        gzs=(4, M - 1),
        gzr=(4, M - 1),
        gps=(4, halves, NP - 1, M - 1),
        gpr=(4, halves, NP - 1, M - 1),
        gcs=(4, M - 1),
        gcr=(4, M - 1),
        bzs=(M - 1,),
        bzr=(M - 1,),
        rcs=(4, M),
        rcr=(4, M),
        rps=(4, halves, NP - 1, M),
        rpr=(4, halves, NP - 1, M),
        rzs=(4, M - 1),
        rzr=(4, M - 1),
        aps=(4, NP - 1),
        apr=(4, NP - 1),
        acs=(4,),
        acr=(4,),
        scs=(4,),
        scr=(4,),
        sas=(4, NP * M - 1),
        sar=(4, NP * M - 1),
        vs=(NP - 1 + M,),
        vr=(NP - 1 + M,),
        hss=(M,),
        hsr=(M,),
    )
    names = list(ins) + list(outs) + list(scratch) + list(sems)
    got = pl.pallas_call(
        functools.partial(layer_kernel, sz, names),
        out_shape=[jax.ShapeDtypeStruct(s, t) for s, t, _ in outs.values()],
        in_specs=[spec for _, spec in ins.values()],
        out_specs=[spec for _, _, spec in outs.values()],
        scratch_shapes=[pltpu.VMEM(s, t) for s, t in scratch.values()]
        + [pltpu.SemaphoreType.DMA(s) for s in sems.values()],
        compiler_params=pltpu.CompilerParams(
            collective_id=0, has_side_effects=True, vmem_limit_bytes=62 << 20
        ),
    )(*[value for value, _ in ins.values()])
    shapes = [(2, D), (R, D), (R, D), (3 * D, HC), (2, HC), (HC, D)] + [(1, D)] * 3
    shapes += [(D, F), (1, F), (F, D)] + [(1, D)] * 3
    big = (1, 2, 3, 5, 9, 11)
    done = list(pl.pallas_call(
        functools.partial(result_kernel, HC, F),
        out_shape=[jax.ShapeDtypeStruct(s, f32) for s in shapes],
        in_specs=[hbm] * len(outs),
        out_specs=[hbm] * len(shapes),
        scratch_shapes=[
            pltpu.VMEM(shape, t)
            for n in (1, 2, 3, 9, 11, 5)
            for shape, t in ((shapes[n], f32 if n < 3 else bf16), ((8, TILE) if n < 3 else shapes[n], f32))
        ]
        + [pltpu.VMEM((8, D), f32)] * 2
        + [pltpu.VMEM(shape, f32) for n, shape in enumerate(shapes) if n not in big]
        + [pltpu.SemaphoreType.DMA((23,))],
    )(*got))
    done[3] = done[3].reshape(3, D, HC)
    return tuple(v[0] if v.shape[0] == 1 else v for v in done)


def result_kernel(HC, F, *refs):
    omega_in, layer_out, grad_in, g_qkv, g_out, g_up, g_down, vectors_in = refs[:8]
    out, held, (omega, vectors), little, sem = refs[8:23], refs[23:35], refs[35:37], refs[37:46], refs[46]
    pairs = ((layer_out, 1), (grad_in, 2), (g_qkv, 3), (g_up, 9), (g_down, 11), (g_out, 5))
    few = [pltpu.make_async_copy(omega_in, omega, sem.at[12]), pltpu.make_async_copy(vectors_in, vectors, sem.at[13])]
    reads, writes = [], []
    for n, (src, at) in enumerate(pairs):
        low, high = held[2 * n], held[2 * n + 1]
        reads.append(pltpu.make_async_copy(src, low, sem.at[n]))
        writes.append(pltpu.make_async_copy(low if n < 2 else high, out[at], sem.at[len(pairs) + n]))
        reads[n].start()
    for copy in few:
        copy.start()
    for copy in few:
        copy.wait()
    values = [omega[0:2, :], jnp.concatenate([vectors[7:8, 0:HC], vectors[7:8, HC : 2 * HC]], axis=0)]
    values += [vectors[n : n + 1, :] for n in range(3)] + [vectors[6:7, 0:F]]
    values += [vectors[n : n + 1, :] for n in range(3, 6)]
    for n, at in enumerate((0, 4, 6, 7, 8, 10, 12, 13, 14)):
        little[n][...] = values[n]
        writes.append(pltpu.make_async_copy(little[n], out[at], sem.at[14 + n]))
        writes[-1].start()
    for n in range(len(pairs)):
        reads[n].wait()
        if n >= 2:
            held[2 * n + 1][...] = held[2 * n][...].astype(f32)
        writes[n].start()
    for copy in writes:
        copy.wait()


def solution(mesh):
    in_specs = (
        P("dp", None),
        P("dp", None),
        P(None, None, "mp"),
        P(None, "mp"),
        P("mp", None),
        P(),
        P(),
        P(),
        P(None, "mp"),
        P("mp"),
        P("mp", None),
        P(),
        P(),
        P(),
        P("dp", None),
        P("dp", None),
    )
    out_specs = (
        P(),
        P(("dp", "mp"), None),
        P(("dp", "mp"), None),
        P(None, None, "mp"),
        P(None, "mp"),
        P("mp", None),
        P(),
        P(),
        P(),
        P(None, "mp"),
        P("mp"),
        P("mp", None),
        P(),
        P(),
        P(),
    )
    return jax.shard_map(shards, mesh=mesh, in_specs=in_specs, out_specs=out_specs, check_vma=False)
```
